512 devices in a mesh: member: 16 (over x, y_lo, core), lon: 32 (over y_hi, z).
Axes of the slice: x: 4, y: 4 (y_hi: 2, y_lo: 2; y = y_hi * 2 + y_lo), z: 16, core: 2. Of those that a mesh axis runs over, the one named last changes fastest.
Arguments:
- ensemble: bfloat16 [32, 3, 512, 2048], P('member', None, 'lon'), may hold values from -6 to 6
- copy_list: int32 [32], replicated, may hold values from 0 to 31, as said below
- depth: float32 [512, 2048], P('lon'), may hold values from 0.25 to 4
- land_mask: int32 [512, 2048], P('lon'), may hold values 0 or 1
- friction: float32 [512, 2048], P('lon'), may hold values from 0.05 to 2
- coriolis: float32 [2048], replicated, may hold values from -1 to 1
- spread: float32 [2048, 2048], P('member'), may hold values from -0.125 to 0.125
- observed: float32 [512, 2048], P('lon'), may hold values from -6 to 6
Outputs:
- new_state: float32 [32, 3, 512, 2048], P('member', None, 'lon')
- misfit: float32 [32], P('member')
The draws below stay inside these ranges and needn't reach their ends.
Inputs may be any that keep to these rules, and one draw needn't show every extreme that they name: `copy_list`: each entry names a particle of the ensemble; the entries name exactly 8 different particles.
All inputs are finite; a program needn't handle non-finite values. No bound on the sum of `land_mask` on one device may be relied on, other than what follows from the above.
Results may differ from the reference program's by a relative error of at most 0.0013.
Values may be sent and summed in bfloat16 or wider, within the bound.
No kernel may reach another device: no remote copies, remote signals or barrier semaphores. Data moves between devices by JAX's collectives and lax.ppermute only.
A program may use at most 64 MiB of HBM per device.

```python
import math
import jax
import jax.numpy as jnp
from jax import lax

LAT = 2048
STEPS = 2
DISTINCT = 8
P_SIZE = 32
NLON = 512


def draw_copy_list(key, part):
    key = jax.random.fold_in(key, 7)
    first, second, third = jax.random.split(key, 3)
    middle = (jax.random.permutation(first, P_SIZE - 2)[:DISTINCT - 2] + 1).astype(jnp.int32)
    chosen = jnp.concatenate([jnp.array([0, P_SIZE - 1], dtype=jnp.int32), middle])
    assign = jax.random.randint(second, (P_SIZE,), 0, DISTINCT).astype(jnp.int32)
    places = jax.random.permutation(third, P_SIZE)[:DISTINCT]
    assign = assign.at[places].set(jnp.arange(DISTINCT, dtype=jnp.int32))
    return chosen[assign].astype(jnp.int32)


def place_ends(entries, rng, smallest, largest):
    shape = entries.shape
    index_at = [jax.random.randint(jax.random.fold_in(rng, axis), (), 0, shape[axis]) for axis in range(len(shape))]
    entries = entries.at[tuple(index_at)].set(smallest)
    longest = shape.index(max(shape))
    index_at[longest] = (index_at[longest] + 1) % shape[longest]
    return entries.at[tuple(index_at)].set(largest)


def shard_levels(own_key, extent, cuts, least, largest):
    level, own = 1.0, jax.random.fold_in(own_key, 6)
    for axis_at, blocks in cuts:
        steps = jnp.exp(jax.random.uniform(jax.random.fold_in(own, axis_at), (blocks,), jnp.float32, least / len(cuts), largest / len(cuts)))
        level = level * jnp.repeat(steps, extent[axis_at] // blocks).reshape([-1 if axis == axis_at else 1 for axis in range(len(extent))])
    return level


def scatter_about(key, extent, scale, bound, pieces=(), kind=jnp.bfloat16):
    values = jax.random.normal(key, extent, jnp.float32) * scale
    if len(pieces) > 0:
        values = shard_levels(key, extent, pieces, -0.22, 0.18) * values
    return jnp.clip(values, min=-bound, max=bound).astype(kind)


def setup_inputs(seed: int = 0) -> dict:
    keys = jax.random.split(jax.random.key(seed), 9)
    ensemble = scatter_about(keys[0], (P_SIZE, 3, NLON, LAT), 1.0, 6.0, ((0, 16), (2, 32)))
    copy_list = draw_copy_list(jax.random.fold_in(keys[8], 71), 0)
    depth = jnp.clip(jnp.exp(math.log(4.0) - 2.7725887 * jax.random.uniform(keys[2], (NLON, LAT), jnp.float32) ** shard_levels(keys[2], (NLON, LAT), ((0, 32),), -0.2, 0.2)), 0.25, 4.0)
    land_mask = place_ends((jax.random.randint(keys[3], (NLON, LAT), 0, 10) < 9).astype(jnp.int32), jax.random.fold_in(keys[3], 1), 0, 1)
    friction = jnp.clip(jnp.exp(math.log(2.0) - 3.6888794 * jax.random.uniform(keys[4], (NLON, LAT), jnp.float32) ** shard_levels(keys[4], (NLON, LAT), ((0, 32),), -0.2, 0.2)), 0.05, 2.0)
    coriolis = jnp.clip(jax.random.uniform(keys[5], (LAT,), jnp.float32, -1.0, 1.0), -1.0, 1.0)
    spread = scatter_about(keys[6], (LAT, LAT), LAT ** -0.5, 0.125, ((0, 16),), jnp.float32)
    observed = scatter_about(keys[7], (NLON, LAT), 1.0, 6.0, ((0, 32),), jnp.float32)
    return dict(ensemble=ensemble, copy_list=copy_list, depth=depth, land_mask=land_mask, friction=friction, coriolis=coriolis, spread=spread, observed=observed)


time_step = 0.2
gravity = 1.0
nudge_rate = 0.3


def east_diff(field):
    return 0.5 * (jnp.roll(field, -1, axis=-2) - jnp.roll(field, 1, axis=-2))


def north_diff(field):
    padded = jnp.pad(field, ((0, 0), (1, 1)))
    return 0.5 * (padded[:, 2:] - padded[:, :-2])


def reference(ensemble, copy_list, depth, land_mask, friction, coriolis, spread, observed):
    wet = jnp.where(land_mask == 1, 1.0, 0.0).astype(jnp.float32)
    damping = 1.0 / (1.0 + time_step * friction)
    turning = coriolis[None, :]
    column = jnp.arange(NLON).astype(jnp.float32)
    weight = 1.0 + 2.0 * column / NLON

    def advance(source):
        fields = ensemble[source].astype(jnp.float32)
        height, zonal, meridional = fields[0], fields[1], fields[2]
        for step in range(STEPS):
            divergence = east_diff(depth * zonal) + north_diff(depth * meridional)
            fresh = height - time_step * wet * divergence
            east_slope = east_diff(fresh)
            north_slope = north_diff(fresh)
            zonal_next = wet * (zonal + time_step * (turning * meridional - gravity * east_slope)) * damping
            meridional_next = wet * (meridional - time_step * (turning * zonal + gravity * north_slope)) * damping
            innovation = observed - fresh
            correction = innovation + jnp.dot(innovation, spread.T, precision=lax.Precision.HIGHEST)
            height = fresh + nudge_rate * wet * correction
            zonal, meridional = zonal_next, meridional_next
        misfit = jnp.sum(wet * weight[:, None] * (observed - height) ** 2) / (LAT * NLON)
        return jnp.stack([height, zonal, meridional]), misfit

    new_state, misfit = lax.map(advance, copy_list)
    return new_state, misfit
```

```python
import functools

import jax
import jax.numpy as jnp
from jax import lax
from jax.experimental import pallas as pl
from jax.experimental.pallas import tpu as pltpu
from jax.sharding import PartitionSpec as P

DISTINCT = 8
HALO = 3
LANES = 128
time_step = 0.2
nudge_rate = 0.3
f32 = jnp.float32
bf16 = jnp.bfloat16

VMEM = pl.BlockSpec(memory_space=pltpu.VMEM)
SMEM = pl.BlockSpec(memory_space=pltpu.SMEM)


def call(kernel, out_shape, in_specs, out_specs, scratch=(), flops=1e6, bytes_accessed=1e6):
    return pl.pallas_call(
        kernel,
        out_shape=out_shape,
        in_specs=in_specs,
        out_specs=out_specs,
        scratch_shapes=list(scratch),
        compiler_params=pltpu.CompilerParams(vmem_limit_bytes=24 * 1024 * 1024),
        cost_estimate=pl.CostEstimate(
            flops=int(flops), bytes_accessed=int(bytes_accessed), transcendentals=0
        ),
    )


def pieces(x):
    first = x.astype(bf16).astype(f32)
    rest = x - first
    second = rest.astype(bf16).astype(f32)
    return first, second, rest - second


def pack_kernel(copy_ref, ens_ref, depth_ref, mask_ref, fric_ref, head_ref, tail_ref, idx_ref, rows, seen):
    columns = depth_ref.shape[0]
    for p in range(32):
        seen[p] = 0
    for s in range(32):
        seen[copy_ref[s]] = 1
    for i in range(DISTINCT):
        idx_ref[i] = 0
    count = jnp.int32(0)
    for p in range(32):
        used = seen[p]
        place = jnp.minimum(count, DISTINCT - 1)
        idx_ref[place] = jnp.where(used == 1, p, idx_ref[place])
        seen[p] = place
        count = count + used
    for s in range(32):
        idx_ref[DISTINCT + s] = seen[copy_ref[s]]

    depth3 = pieces(depth_ref[...])
    fric3 = pieces(fric_ref[...])
    wet = jnp.where(mask_ref[...] == 1, 1.0, 0.0).astype(f32)
    for out, lo, near2, near1 in (
        (head_ref, 0, 0, 0),
        (tail_ref, columns - HALO, columns - 2, columns - 1),
    ):
        for p in range(2):
            for f in range(3):
                at = (p * 3 + f) * HALO
                rows[at : at + HALO, :] = ens_ref[p, f].astype(f32)[lo : lo + HALO, :]
        for k in range(3):
            rows[18 + 3 * k : 21 + 3 * k, :] = depth3[k][lo : lo + HALO, :]
            rows[29 + k : 30 + k, :] = fric3[k][near1 : near1 + 1, :]
        rows[27:29, :] = wet[near2 : near2 + 2, :]
        out[...] = rows[...].astype(bf16)


def east(x):
    return 0.5 * (pltpu.roll(x, x.shape[0] - 1, 0) - pltpu.roll(x, 1, 0))


def north(x):
    n = x.shape[1]
    lane = lax.broadcasted_iota(jnp.int32, x.shape, 1)
    up = jnp.where(lane == n - 1, 0.0, pltpu.roll(x, n - 1, 1))
    down = jnp.where(lane == 0, 0.0, pltpu.roll(x, 1, 1))
    return 0.5 * (up - down)


def source_kernel(
    ens_ref, left_ref, right_ref, depth_ref, mask_ref, fric_ref, cor_ref, obs_ref,
    innov_ref, rest_ref, ext, lrows, rrows, sdepth, swet, sfric,
):
    columns, lat = depth_ref.shape
    blocks = lat // LANES
    lo, hi = 8, 8 + columns
    lrows[...] = left_ref[...].astype(f32)
    rrows[...] = right_ref[...].astype(f32)

    def three(rows, at, n, step):
        a, b, c = (rows[at + step * k : at + step * k + n, :] for k in range(3))
        return (a + b) + c

    for ref in (sdepth, swet, sfric):
        ref[0:8, :] = jnp.zeros((8, lat), f32)
        ref[hi : hi + 8, :] = jnp.zeros((8, lat), f32)
    sdepth[lo:hi, :] = depth_ref[...]
    sdepth[lo - 3 : lo, :] = three(lrows, 18, 3, 3)
    sdepth[hi : hi + 3, :] = three(rrows, 18, 3, 3)
    swet[lo:hi, :] = jnp.where(mask_ref[...] == 1, 1.0, 0.0).astype(f32)
    swet[lo - 2 : lo, :] = lrows[27:29, :]
    swet[hi : hi + 2, :] = rrows[27:29, :]
    sfric[lo:hi, :] = fric_ref[...]
    sfric[lo - 1 : lo, :] = three(lrows, 29, 1, 1)
    sfric[hi : hi + 1, :] = three(rrows, 29, 1, 1)
    depth = sdepth[...]
    wet = swet[...]
    damped = wet * (1.0 / (1.0 + time_step * sfric[...]))
    turning = cor_ref[...]

    for p in range(2):
        fields = []
        for f in range(3):
            at = (p * 3 + f) * HALO
            ext[f, 0:8, :] = jnp.zeros((8, lat), f32)
            ext[f, hi : hi + 8, :] = jnp.zeros((8, lat), f32)
            ext[f, lo:hi, :] = ens_ref[p, f].astype(f32)
            ext[f, lo - HALO : lo, :] = lrows[at : at + HALO, :]
            ext[f, hi : hi + HALO, :] = rrows[at : at + HALO, :]
            fields.append(ext[f])
        height, zonal, meridional = fields
        fresh = height - time_step * wet * (east(depth * zonal) + north(depth * meridional))
        innov = obs_ref[...] - fresh[lo:hi, :]
        for b in range(blocks):
            innov_ref[b, p] = innov[:, b * LANES : (b + 1) * LANES]
        zonal1 = damped * (zonal + time_step * (turning * meridional - east(fresh)))
        meridional1 = damped * (meridional - time_step * (turning * zonal + north(fresh)))
        change = -time_step * wet * (east(depth * zonal1) + north(depth * meridional1))
        zonal_part = damped * (zonal1 + time_step * (turning * meridional1))
        meridional_part = damped * (meridional1 - time_step * (turning * zonal1))
        for k, value in enumerate((change, zonal_part, meridional_part)):
            for b in range(blocks):
                rest_ref[b, p, k] = value[lo:hi, b * LANES : (b + 1) * LANES]


def split_kernel(spread_ref, out_ref):
    s = spread_ref[...]
    high = s.astype(bf16)
    out_ref[0] = high
    out_ref[1] = (s - high.astype(f32)).astype(bf16)


def select_kernel(idx_ref, all_ref, mine_ref, copies_ref):
    columns = all_ref.shape[1]
    for i in range(DISTINCT):
        v = all_ref[idx_ref[i]]
        mine_ref[i] = v
        b = v.astype(bf16)
        for d in range(copies_ref.shape[0]):
            copies_ref[d, i * columns : (i + 1) * columns, :] = b


def spread_dot(gathered_ref, spread_ref):
    blocks = gathered_ref.shape[0]
    lhs = jnp.concatenate([gathered_ref[b] for b in range(blocks)], axis=1)
    dims = (((1,), (1,)), ((), ()))
    return lax.dot_general(
        lhs, spread_ref[0], dims, preferred_element_type=f32
    ) + lax.dot_general(lhs, spread_ref[1], dims, preferred_element_type=f32)


def block_of(ref, b):
    return ref[:, pl.ds(pl.multiple_of(b * LANES, LANES), LANES)]


def wet_block(mask_ref, b):
    return jnp.where(block_of(mask_ref, b) == 1, 1.0, 0.0).astype(f32)


def update_kernel(
    idx_ref, gathered_ref, spread_ref, mine_ref, rest_ref, mask_ref, obs_ref,
    innov_ref, copies_ref, edge_ref,
):
    columns = mask_ref.shape[0]
    me = lax.axis_index("member")
    wet = wet_block(mask_ref, me)
    obs = block_of(obs_ref, me)
    spreaded = spread_dot(gathered_ref, spread_ref)
    for i in range(DISTINCT):
        innov = mine_ref[i]
        sp = spreaded[i * columns : (i + 1) * columns, :]
        new = innov - nudge_rate * wet * (innov + sp) - rest_ref[idx_ref[i], 0]
        innov_ref[i] = new
        b = new.astype(bf16)
        for d in range(copies_ref.shape[0]):
            copies_ref[d, i * columns : (i + 1) * columns, :] = b
        fresh = obs - new
        edge_ref[0, i : i + 1, :] = fresh[0:1, :]
        edge_ref[1, i : i + 1, :] = fresh[columns - 1 : columns, :]


def height_kernel(
    idx_ref, gathered_ref, spread_ref, innov_ref, mask_ref, obs_ref, out_ref, height
):
    columns = mask_ref.shape[0]
    me = lax.axis_index("member")
    wet = wet_block(mask_ref, me)
    obs = block_of(obs_ref, me)
    spreaded = spread_dot(gathered_ref, spread_ref)
    for i in range(DISTINCT):
        innov = innov_ref[i]
        sp = spreaded[i * columns : (i + 1) * columns, :]
        height[i] = (obs - innov) + nudge_rate * wet * (innov + sp)
    for s in range(32):
        out_ref[s // 2, s % 2] = height[idx_ref[DISTINCT + s]]


def velocity_kernel(
    idx_ref, gathered_ref, innov_ref, left_ref, right_ref, rest_ref, mask_ref, fric_ref, obs_ref,
    out_ref, zonal, meridional,
):
    columns = mask_ref.shape[0]
    blocks = gathered_ref.shape[0]
    me = lax.axis_index("member")
    wet = wet_block(mask_ref, me)
    obs = block_of(obs_ref, me)
    damped = wet * (1.0 / (1.0 + time_step * block_of(fric_ref, me)))
    before = jnp.maximum(me - 1, 0)
    after = jnp.minimum(me + 1, blocks - 1)
    obs_before = block_of(obs_ref, before)
    obs_after = block_of(obs_ref, after)
    has_before = jnp.where(me > 0, 1.0, 0.0).astype(f32)
    has_after = jnp.where(me < blocks - 1, 1.0, 0.0).astype(f32)
    lane = lax.broadcasted_iota(jnp.int32, (columns, LANES), 1)
    row = lax.broadcasted_iota(jnp.int32, (columns, LANES), 0)
    for i in range(DISTINCT):
        fresh = obs - innov_ref[i]
        part = slice(i * columns, (i + 1) * columns)
        fresh_before = has_before * (obs_before - gathered_ref[before, part, :].astype(f32))
        fresh_after = has_after * (obs_after - gathered_ref[after, part, :].astype(f32))
        down = jnp.where(lane == 0, pltpu.roll(fresh_before, 1, 1), pltpu.roll(fresh, 1, 1))
        up = jnp.where(
            lane == LANES - 1,
            pltpu.roll(fresh_after, LANES - 1, 1),
            pltpu.roll(fresh, LANES - 1, 1),
        )
        west = jnp.where(row == 0, left_ref[i : i + 1, :], pltpu.roll(fresh, 1, 0))
        easterly = jnp.where(
            row == columns - 1, right_ref[i : i + 1, :], pltpu.roll(fresh, columns - 1, 0)
        )
        src = idx_ref[i]
        zonal[i] = rest_ref[src, 1] - damped * (time_step * 0.5 * (easterly - west))
        meridional[i] = rest_ref[src, 2] - damped * (time_step * 0.5 * (up - down))
    for s in range(32):
        place = idx_ref[DISTINCT + s]
        out_ref[s // 2, s % 2, 0] = zonal[place]
        out_ref[s // 2, s % 2, 1] = meridional[place]


def misfit_kernel(h_ref, mask_ref, obs_ref, out_ref, *, total):
    columns, lat = mask_ref.shape
    blocks = lat // LANES
    first = (lax.axis_index("lon") * columns).astype(f32)
    column = first + lax.broadcasted_iota(jnp.int32, (columns, LANES), 0).astype(f32)
    weight = 1.0 + 2.0 * column / total
    lane = lax.broadcasted_iota(jnp.int32, (1, LANES), 1)
    sums = jnp.zeros((1, LANES), f32)
    for p in range(2):
        acc = jnp.zeros((columns, LANES), f32)
        for b in range(blocks):
            part = slice(b * LANES, (b + 1) * LANES)
            wet = jnp.where(mask_ref[:, part] == 1, 1.0, 0.0).astype(f32)
            gap = obs_ref[:, part] - h_ref[b, p]
            acc = acc + wet * (gap * gap)
        sums = jnp.where(lane == p, jnp.sum(acc * weight), sums)
    for d in range(out_ref.shape[0]):
        out_ref[d] = sums


def output_kernel(h_ref, zm_ref, out_ref):
    blocks = h_ref.shape[0]
    for p in range(2):
        for b in range(blocks):
            part = slice(b * LANES, (b + 1) * LANES)
            out_ref[p, 0, :, part] = h_ref[b, p]
            out_ref[p, 1, :, part] = zm_ref[b, p, 0]
            out_ref[p, 2, :, part] = zm_ref[b, p, 1]


def per_device(ensemble, copy_list, depth, land_mask, friction, coriolis, spread, observed):
    columns, lat = depth.shape
    members = lax.axis_size("member")
    lons = lax.axis_size("lon")
    blocks = lat // LANES
    rows = DISTINCT * columns
    shape = jax.ShapeDtypeStruct
    eastward = [(i, (i + 1) % lons) for i in range(lons)]
    westward = [((i + 1) % lons, i) for i in range(lons)]

    def swap(x):
        return lax.all_to_all(x, "member", 0, 0, tiled=True)

    head, tail, idx = call(
        pack_kernel,
        (shape((32, lat), bf16), shape((32, lat), bf16), shape((64,), jnp.int32)),
        [SMEM, VMEM, VMEM, VMEM, VMEM],
        (VMEM, VMEM, SMEM),
        [pltpu.VMEM((32, lat), f32), pltpu.SMEM((32,), jnp.int32)],
    )(copy_list, ensemble, depth, land_mask, friction)
    left = lax.ppermute(tail, "lon", eastward)
    right = lax.ppermute(head, "lon", westward)
    parts = call(
        split_kernel, shape((2,) + spread.shape, bf16), [VMEM], VMEM
    )(spread)

    ext_rows = columns + 16
    innov1, rest = call(
        source_kernel,
        (
            shape((blocks, 2, columns, LANES), f32),
            shape((blocks, 2, 3, columns, LANES), f32),
        ),
        [VMEM] * 8,
        (VMEM, VMEM),
        [pltpu.VMEM((3, ext_rows, lat), f32)]
        + [pltpu.VMEM((32, lat), f32)] * 2
        + [pltpu.VMEM((ext_rows, lat), f32)] * 3,
    )(ensemble, left, right, depth, land_mask, friction, coriolis[None, :], observed)

    innov1 = swap(innov1).reshape(2 * members, columns, LANES)
    rest = swap(rest).reshape(2 * members, 3, columns, LANES)
    mine, copies = call(
        select_kernel,
        (shape((DISTINCT, columns, LANES), f32), shape((members, rows, LANES), bf16)),
        [SMEM, VMEM],
        (VMEM, VMEM),
    )(idx, innov1)
    gathered1 = swap(copies)
    innov2, copies, edges = call(
        update_kernel,
        (
            shape((DISTINCT, columns, LANES), f32),
            shape((members, rows, LANES), bf16),
            shape((2, DISTINCT, LANES), f32),
        ),
        [SMEM] + [VMEM] * 6,
        (VMEM, VMEM, VMEM),
        flops=2 * 2 * rows * LANES * lat,
    )(idx, gathered1, parts, mine, rest, land_mask, observed)
    gathered2 = swap(copies)
    left = lax.ppermute(edges[1], "lon", eastward)
    right = lax.ppermute(edges[0], "lon", westward)
    heights = call(
        height_kernel,
        shape((members, 2, columns, LANES), f32),
        [SMEM] + [VMEM] * 5,
        VMEM,
        [pltpu.VMEM((DISTINCT, columns, LANES), f32)],
        flops=2 * 2 * rows * LANES * lat,
    )(idx, gathered2, parts, innov2, land_mask, observed)
    heights = swap(heights)
    velocities = call(
        velocity_kernel,
        shape((members, 2, 2, columns, LANES), f32),
        [SMEM] + [VMEM] * 8,
        VMEM,
        [pltpu.VMEM((DISTINCT, columns, LANES), f32)] * 2,
    )(idx, gathered2, innov2, left, right, rest, land_mask, friction, observed)
    velocities = swap(velocities)
    sums = call(
        functools.partial(misfit_kernel, total=float(columns * lons)),
        shape((lons, 1, LANES), f32),
        [VMEM] * 3,
        VMEM,
    )(heights, land_mask, observed)
    sums = lax.all_to_all(sums, "lon", 0, 0, tiled=True)
    misfit = jnp.sum(sums, axis=(0, 1))[:2] / (lat * columns * lons)
    new_state = call(
        output_kernel,
        shape((2, 3, columns, lat), f32),
        [VMEM, VMEM],
        VMEM,
    )(heights, velocities)
    return new_state, misfit


def solution(mesh):
    placed = (
        P("member", None, "lon", None),
        P(),
        P("lon", None),
        P("lon", None),
        P("lon", None),
        P(),
        P("member", None),
        P("lon", None),
    )
    return jax.shard_map(
        per_device,
        mesh=mesh,
        in_specs=placed,
        out_specs=(P("member", None, "lon", None), P("member")),
        check_vma=False,
    )
```

```python
import functools

import jax
import jax.numpy as jnp
from jax import lax
from jax.experimental import pallas as pl
from jax.experimental.pallas import tpu as pltpu
from jax.sharding import PartitionSpec as P

DISTINCT = 8
HALO = 3
LANES = 128
time_step = 0.2
nudge_rate = 0.3
f32 = jnp.float32
bf16 = jnp.bfloat16

VMEM = pl.BlockSpec(memory_space=pltpu.VMEM)
SMEM = pl.BlockSpec(memory_space=pltpu.SMEM)
ANY = pl.BlockSpec(memory_space=pl.ANY)


def call(kernel, out_shape, in_specs, out_specs, scratch=(), flops=1e6, bytes_accessed=1e6, limit=24):
    return pl.pallas_call(
        kernel,
        out_shape=out_shape,
        in_specs=in_specs,
        out_specs=out_specs,
        scratch_shapes=list(scratch),
        compiler_params=pltpu.CompilerParams(vmem_limit_bytes=limit * 1024 * 1024),
        cost_estimate=pl.CostEstimate(
            flops=int(flops), bytes_accessed=int(bytes_accessed), transcendentals=0
        ),
    )


def pieces(x):
    first = x.astype(bf16).astype(f32)
    rest = x - first
    second = rest.astype(bf16).astype(f32)
    return first, second, rest - second


def pack_kernel(
    copy_ref, ens_hbm, depth_hbm, mask_hbm, fric_hbm, head_ref, tail_ref, idx_ref,
    ens_ref, depth_ref, mask_ref, fric_ref, rows, seen, sems,
):
    columns = depth_ref.shape[0]
    fetches = [
        pltpu.make_async_copy(src, dst, sems.at[k])
        for k, (src, dst) in enumerate(
            ((ens_hbm, ens_ref), (depth_hbm, depth_ref), (mask_hbm, mask_ref), (fric_hbm, fric_ref))
        )
    ]
    for fetch in fetches:
        fetch.start()
    for p in range(32):
        seen[p] = 0
    for s in range(32):
        seen[copy_ref[s]] = 1
    for i in range(DISTINCT):
        idx_ref[i] = 0
    count = jnp.int32(0)
    for p in range(32):
        used = seen[p]
        place = jnp.minimum(count, DISTINCT - 1)
        idx_ref[place] = jnp.where(used == 1, p, idx_ref[place])
        seen[p] = place
        count = count + used
    for s in range(32):
        idx_ref[DISTINCT + s] = seen[copy_ref[s]]

    for fetch in fetches:
        fetch.wait()
    depth3 = pieces(depth_ref[...])
    fric3 = pieces(fric_ref[...])
    wet = jnp.where(mask_ref[...] == 1, 1.0, 0.0).astype(f32)
    for out, lo, near2, near1 in (
        (head_ref, 0, 0, 0),
        (tail_ref, columns - HALO, columns - 2, columns - 1),
    ):
        for p in range(2):
            for f in range(3):
                at = (p * 3 + f) * HALO
                rows[at : at + HALO, :] = ens_ref[p, f].astype(f32)[lo : lo + HALO, :]
        for k in range(3):
            rows[18 + 3 * k : 21 + 3 * k, :] = depth3[k][lo : lo + HALO, :]
            rows[29 + k : 30 + k, :] = fric3[k][near1 : near1 + 1, :]
        rows[27:29, :] = wet[near2 : near2 + 2, :]
        out[...] = rows[...].astype(bf16)


def east(x):
    return 0.5 * (pltpu.roll(x, x.shape[0] - 1, 0) - pltpu.roll(x, 1, 0))


def north(x):
    n = x.shape[1]
    lane = lax.broadcasted_iota(jnp.int32, x.shape, 1)
    up = jnp.where(lane == n - 1, 0.0, pltpu.roll(x, n - 1, 1))
    down = jnp.where(lane == 0, 0.0, pltpu.roll(x, 1, 1))
    return 0.5 * (up - down)


def source_kernel(
    ens_ref, left_ref, right_ref, depth_ref, mask_ref, fric_ref, cor_ref, obs_ref,
    out_ref, ext, lrows, rrows, sdepth, swet, sfric,
):
    columns, lat = depth_ref.shape
    blocks = lat // LANES
    lo, hi = 8, 8 + columns
    lrows[...] = left_ref[...].astype(f32)
    rrows[...] = right_ref[...].astype(f32)

    def three(rows, at, n, step):
        a, b, c = (rows[at + step * k : at + step * k + n, :] for k in range(3))
        return (a + b) + c

    for ref in (sdepth, swet, sfric):
        ref[0:8, :] = jnp.zeros((8, lat), f32)
        ref[hi : hi + 8, :] = jnp.zeros((8, lat), f32)
    sdepth[lo:hi, :] = depth_ref[...]
    sdepth[lo - 3 : lo, :] = three(lrows, 18, 3, 3)
    sdepth[hi : hi + 3, :] = three(rrows, 18, 3, 3)
    swet[lo:hi, :] = jnp.where(mask_ref[...] == 1, 1.0, 0.0).astype(f32)
    swet[lo - 2 : lo, :] = lrows[27:29, :]
    swet[hi : hi + 2, :] = rrows[27:29, :]
    sfric[lo:hi, :] = fric_ref[...]
    sfric[lo - 1 : lo, :] = three(lrows, 29, 1, 1)
    sfric[hi : hi + 1, :] = three(rrows, 29, 1, 1)
    depth = sdepth[...]
    wet = swet[...]
    damped = wet * (1.0 / (1.0 + time_step * sfric[...]))
    turning = cor_ref[...]

    for p in range(2):
        fields = []
        for f in range(3):
            at = (p * 3 + f) * HALO
            ext[f, 0:8, :] = jnp.zeros((8, lat), f32)
            ext[f, hi : hi + 8, :] = jnp.zeros((8, lat), f32)
            ext[f, lo:hi, :] = ens_ref[p, f].astype(f32)
            ext[f, lo - HALO : lo, :] = lrows[at : at + HALO, :]
            ext[f, hi : hi + HALO, :] = rrows[at : at + HALO, :]
            fields.append(ext[f])
        height, zonal, meridional = fields
        fresh = height - time_step * wet * (east(depth * zonal) + north(depth * meridional))
        innov = obs_ref[...] - fresh[lo:hi, :]
        for b in range(blocks):
            out_ref[b, p, 0] = innov[:, b * LANES : (b + 1) * LANES]
        zonal1 = damped * (zonal + time_step * (turning * meridional - east(fresh)))
        meridional1 = damped * (meridional - time_step * (turning * zonal + north(fresh)))
        change = -time_step * wet * (east(depth * zonal1) + north(depth * meridional1))
        zonal_part = damped * (zonal1 + time_step * (turning * meridional1))
        meridional_part = damped * (meridional1 - time_step * (turning * zonal1))
        for k, value in enumerate((change, zonal_part, meridional_part)):
            for b in range(blocks):
                out_ref[b, p, k + 1] = value[lo:hi, b * LANES : (b + 1) * LANES]


def split_kernel(spread_ref, out_ref):
    s = spread_ref[...]
    high = s.astype(bf16)
    out_ref[0] = high
    out_ref[1] = (s - high.astype(f32)).astype(bf16)


def select_kernel(idx_ref, all_ref, copies_ref):
    columns = all_ref.shape[2]
    for i in range(DISTINCT):
        v = all_ref[idx_ref[i], 0]
        b = v.astype(bf16)
        for d in range(copies_ref.shape[0]):
            copies_ref[d, i * columns : (i + 1) * columns, :] = b


def spread_dot(gathered_ref, spread_ref):
    blocks = gathered_ref.shape[0]
    lhs = jnp.concatenate([gathered_ref[b] for b in range(blocks)], axis=1)
    dims = (((1,), (1,)), ((), ()))
    return lax.dot_general(
        lhs, spread_ref[0], dims, preferred_element_type=f32
    ) + lax.dot_general(lhs, spread_ref[1], dims, preferred_element_type=f32)


def block_of(ref, b):
    return ref[:, pl.ds(pl.multiple_of(b * LANES, LANES), LANES)]


def wet_block(mask_ref, b):
    return jnp.where(block_of(mask_ref, b) == 1, 1.0, 0.0).astype(f32)


def update_kernel(
    idx_ref, gathered_ref, spread_ref, all_ref, mask_ref, obs_ref,
    innov_ref, copies_ref, edge_ref,
):
    columns = mask_ref.shape[0]
    me = lax.axis_index("member")
    wet = wet_block(mask_ref, me)
    obs = block_of(obs_ref, me)
    spreaded = spread_dot(gathered_ref, spread_ref)
    for i in range(DISTINCT):
        innov = all_ref[idx_ref[i], 0]
        sp = spreaded[i * columns : (i + 1) * columns, :]
        new = innov - nudge_rate * wet * (innov + sp) - all_ref[idx_ref[i], 1]
        innov_ref[i] = new
        b = new.astype(bf16)
        for d in range(copies_ref.shape[0]):
            copies_ref[d, i * columns : (i + 1) * columns, :] = b
        fresh = obs - new
        edge_ref[0, i : i + 1, :] = fresh[0:1, :]
        edge_ref[1, i : i + 1, :] = fresh[columns - 1 : columns, :]


def final_kernel(
    idx_ref, gathered_ref, spread_ref, innov_ref, left_ref, right_ref, all_ref,
    mask_ref, fric_ref, obs_ref, out_ref, state,
):
    columns = mask_ref.shape[0]
    blocks = gathered_ref.shape[0]
    me = lax.axis_index("member")
    wet = wet_block(mask_ref, me)
    obs = block_of(obs_ref, me)
    damped = wet * (1.0 / (1.0 + time_step * block_of(fric_ref, me)))
    before = jnp.maximum(me - 1, 0)
    after = jnp.minimum(me + 1, blocks - 1)
    obs_before = block_of(obs_ref, before)
    obs_after = block_of(obs_ref, after)
    has_before = jnp.where(me > 0, 1.0, 0.0).astype(f32)
    has_after = jnp.where(me < blocks - 1, 1.0, 0.0).astype(f32)
    lane = lax.broadcasted_iota(jnp.int32, (columns, LANES), 1)
    row = lax.broadcasted_iota(jnp.int32, (columns, LANES), 0)
    spreaded = spread_dot(gathered_ref, spread_ref)
    for i in range(DISTINCT):
        innov = innov_ref[i]
        fresh = obs - innov
        part = slice(i * columns, (i + 1) * columns)
        state[i, 0] = fresh + nudge_rate * wet * (innov + spreaded[part, :])
        fresh_before = has_before * (obs_before - gathered_ref[before, part, :].astype(f32))
        fresh_after = has_after * (obs_after - gathered_ref[after, part, :].astype(f32))
        down = jnp.where(lane == 0, pltpu.roll(fresh_before, 1, 1), pltpu.roll(fresh, 1, 1))
        up = jnp.where(
            lane == LANES - 1,
            pltpu.roll(fresh_after, LANES - 1, 1),
            pltpu.roll(fresh, LANES - 1, 1),
        )
        west = jnp.where(row == 0, left_ref[i : i + 1, :], pltpu.roll(fresh, 1, 0))
        easterly = jnp.where(
            row == columns - 1, right_ref[i : i + 1, :], pltpu.roll(fresh, columns - 1, 0)
        )
        src = idx_ref[i]
        state[i, 1] = all_ref[src, 2] - damped * (time_step * 0.5 * (easterly - west))
        state[i, 2] = all_ref[src, 3] - damped * (time_step * 0.5 * (up - down))
    for s in range(32):
        out_ref[s // 2, s % 2] = state[idx_ref[DISTINCT + s]]


def misfit_kernel(h_ref, mask_ref, obs_ref, out_ref, *, total):
    columns, lat = mask_ref.shape
    blocks = lat // LANES
    first = (lax.axis_index("lon") * columns).astype(f32)
    column = first + lax.broadcasted_iota(jnp.int32, (columns, LANES), 0).astype(f32)
    weight = 1.0 + 2.0 * column / total
    lane = lax.broadcasted_iota(jnp.int32, (1, LANES), 1)
    sums = jnp.zeros((1, LANES), f32)
    for p in range(2):
        acc = jnp.zeros((columns, LANES), f32)
        for b in range(blocks):
            part = slice(b * LANES, (b + 1) * LANES)
            wet = jnp.where(mask_ref[:, part] == 1, 1.0, 0.0).astype(f32)
            gap = obs_ref[:, part] - h_ref[b, p, 0]
            acc = acc + wet * (gap * gap)
        sums = jnp.where(lane == p, jnp.sum(acc * weight), sums)
    for d in range(out_ref.shape[0]):
        out_ref[d] = sums


def output_kernel(state_ref, out_ref):
    for b in range(state_ref.shape[0]):
        out_ref[:, :, :, b * LANES : (b + 1) * LANES] = state_ref[b]


def per_device(ensemble, copy_list, depth, land_mask, friction, coriolis, spread, observed):
    columns, lat = depth.shape
    members = lax.axis_size("member")
    lons = lax.axis_size("lon")
    blocks = lat // LANES
    rows = DISTINCT * columns
    shape = jax.ShapeDtypeStruct
    eastward = [(i, (i + 1) % lons) for i in range(lons)]
    westward = [((i + 1) % lons, i) for i in range(lons)]

    def swap(x):
        return lax.all_to_all(x, "member", 0, 0, tiled=True)

    head, tail, idx = call(
        pack_kernel,
        (shape((32, lat), bf16), shape((32, lat), bf16), shape((64,), jnp.int32)),
        [SMEM, ANY, ANY, ANY, ANY],
        (VMEM, VMEM, SMEM),
        [
            pltpu.VMEM(ensemble.shape, bf16),
            pltpu.VMEM(depth.shape, f32),
            pltpu.VMEM(depth.shape, jnp.int32),
            pltpu.VMEM(depth.shape, f32),
            pltpu.VMEM((32, lat), f32),
            pltpu.SMEM((32,), jnp.int32),
            pltpu.SemaphoreType.DMA((4,)),
        ],
        limit=60,
    )(copy_list, ensemble, depth, land_mask, friction)
    left = lax.ppermute(tail, "lon", eastward)
    right = lax.ppermute(head, "lon", westward)
    parts = call(
        split_kernel, shape((2,) + spread.shape, bf16), [VMEM], VMEM
    )(spread)

    ext_rows = columns + 16
    step1 = call(
        source_kernel,
        shape((blocks, 2, 4, columns, LANES), f32),
        [VMEM] * 8,
        VMEM,
        [pltpu.VMEM((3, ext_rows, lat), f32)]
        + [pltpu.VMEM((32, lat), f32)] * 2
        + [pltpu.VMEM((ext_rows, lat), f32)] * 3,
    )(ensemble, left, right, depth, land_mask, friction, coriolis[None, :], observed)
    step1 = swap(step1).reshape(2 * members, 4, columns, LANES)
    copies = call(
        select_kernel, shape((members, rows, LANES), bf16), [SMEM, VMEM], VMEM
    )(idx, step1)
    gathered1 = swap(copies)
    innov2, copies, edges = call(
        update_kernel,
        (
            shape((DISTINCT, columns, LANES), f32),
            shape((members, rows, LANES), bf16),
            shape((2, DISTINCT, LANES), f32),
        ),
        [SMEM] + [VMEM] * 5,
        (VMEM, VMEM, VMEM),
        flops=2 * 2 * rows * LANES * lat,
    )(idx, gathered1, parts, step1, land_mask, observed)
    gathered2 = swap(copies)
    left = lax.ppermute(edges[1], "lon", eastward)
    right = lax.ppermute(edges[0], "lon", westward)
    state = call(
        final_kernel,
        shape((members, 2, 3, columns, LANES), f32),
        [SMEM] + [VMEM] * 9,
        VMEM,
        [pltpu.VMEM((DISTINCT, 3, columns, LANES), f32)],
        flops=2 * 2 * rows * LANES * lat,
    )(idx, gathered2, parts, innov2, left, right, step1, land_mask, friction, observed)
    state = swap(state)
    sums = call(
        functools.partial(misfit_kernel, total=float(columns * lons)),
        shape((lons, 1, LANES), f32),
        [VMEM] * 3,
        VMEM,
    )(state, land_mask, observed)
    sums = lax.all_to_all(sums, "lon", 0, 0, tiled=True)
    misfit = jnp.sum(sums, axis=(0, 1))[:2] / (lat * columns * lons)
    new_state = call(output_kernel, shape((2, 3, columns, lat), f32), [VMEM], VMEM)(state)
    return new_state, misfit


def solution(mesh):
    placed = (
        P("member", None, "lon", None),
        P(),
        P("lon", None),
        P("lon", None),
        P("lon", None),
        P(),
        P("member", None),
        P("lon", None),
    )
    return jax.shard_map(
        per_device,
        mesh=mesh,
        in_specs=placed,
        out_specs=(P("member", None, "lon", None), P("member")),
        check_vma=False,
    )
```

```python
import functools

import jax
import jax.numpy as jnp
from jax import lax
from jax.experimental import pallas as pl
from jax.experimental.pallas import tpu as pltpu
from jax.sharding import PartitionSpec as P

DISTINCT = 8
HALO = 3
LANES = 128
time_step = 0.2
nudge_rate = 0.3
f32 = jnp.float32
bf16 = jnp.bfloat16

VMEM = pl.BlockSpec(memory_space=pltpu.VMEM)
SMEM = pl.BlockSpec(memory_space=pltpu.SMEM)
ANY = pl.BlockSpec(memory_space=pl.ANY)


def call(kernel, out_shape, in_specs, out_specs, scratch=(), flops=1e6, bytes_accessed=1e6, limit=24):
    return pl.pallas_call(
        kernel,
        out_shape=out_shape,
        in_specs=in_specs,
        out_specs=out_specs,
        scratch_shapes=list(scratch),
        compiler_params=pltpu.CompilerParams(vmem_limit_bytes=limit * 1024 * 1024),
        cost_estimate=pl.CostEstimate(
            flops=int(flops), bytes_accessed=int(bytes_accessed), transcendentals=0
        ),
    )


def pack_kernel(copy_ref, ens_hbm, out_ref, idx_ref, ens_ref, seen, sem):
    lat = ens_ref.shape[-1]
    blocks = out_ref.shape[0]
    fetch = pltpu.make_async_copy(ens_hbm, ens_ref, sem)
    fetch.start()
    for p in range(32):
        seen[p] = 0
    for s in range(32):
        seen[copy_ref[s]] = 1
    for i in range(DISTINCT):
        idx_ref[i] = 0
    count = jnp.int32(0)
    for p in range(32):
        used = seen[p]
        place = jnp.minimum(count, DISTINCT - 1)
        idx_ref[place] = jnp.where(used == 1, p, idx_ref[place])
        seen[p] = place
        count = count + used
    for s in range(32):
        idx_ref[DISTINCT + s] = seen[copy_ref[s]]

    row = lax.broadcasted_iota(jnp.int32, (16 * blocks, lat), 0)
    lane = lax.broadcasted_iota(jnp.int32, (16 * blocks, lat), 1)
    beside = row % 16
    source = (row // 16) * LANES + jnp.where(beside < HALO, beside - HALO, beside - HALO + LANES)
    pick = jnp.where((source == lane) & (beside < 2 * HALO), 1.0, 0.0).astype(bf16)
    fetch.wait()
    x = jnp.concatenate([ens_ref[p, f] for p in range(2) for f in range(3)], axis=0)
    halos = lax.dot_general(pick, x, (((1,), (1,)), ((), ())), preferred_element_type=f32)
    n = x.shape[0]
    halos = jnp.concatenate([halos, jnp.zeros((16 * blocks, LANES - n), f32)], axis=1).astype(bf16)
    for b in range(blocks):
        out_ref[b, 0:n, :] = x[:, b * LANES : (b + 1) * LANES]
        out_ref[b, n : n + 16, :] = halos[16 * b : 16 * b + 16, :]


def static_kernel(depth_ref, mask_ref, fric_ref, head_ref, tail_ref):
    columns = depth_ref.shape[0]
    wet = jnp.where(mask_ref[...] == 1, 1.0, 0.0).astype(f32)
    for out, lo, near2, near1 in (
        (head_ref, 0, 0, 0),
        (tail_ref, columns - HALO, columns - 2, columns - 1),
    ):
        out[0:3, :] = depth_ref[lo : lo + HALO, :]
        out[3:5, :] = wet[near2 : near2 + 2, :]
        out[5:6, :] = fric_ref[near1 : near1 + 1, :]
        out[6:8, :] = jnp.zeros((2, wet.shape[1]), f32)


def select_kernel(idx_ref, all_ref, fields_ref, head_ref, tail_ref, rows):
    columns = fields_ref.shape[1] // 3
    part = 3 * columns
    h = lax.broadcasted_iota(jnp.int32, (16, LANES), 0)
    lane = lax.broadcasted_iota(jnp.int32, (16, LANES), 1)
    target = jnp.where(h < HALO, h + LANES - HALO, h - HALO)
    place = jnp.where((target == lane) & (h < 2 * HALO), 1.0, 0.0).astype(bf16)
    for i in range(DISTINCT):
        particle = idx_ref[i]
        src, p = particle // 2, particle % 2
        main = all_ref[src, pl.ds(pl.multiple_of(p * part, 16), part), :]
        halos = all_ref[src, 2 * part : 2 * part + 16, :]
        tile = lax.dot_general(halos, place, (((0,), (0,)), ((), ())), preferred_element_type=f32)
        fields_ref[i, :, :LANES] = main.astype(f32)
        fields_ref[i, :, LANES:] = jnp.where(p == 0, tile[:part], tile[part : 2 * part])
    for out, lo in ((head_ref, 0), (tail_ref, columns - HALO)):
        rows[...] = jnp.zeros(rows.shape, f32)
        for i in range(DISTINCT):
            for f in range(3):
                at = (i * 3 + f) * HALO
                rows[at : at + HALO, :] = fields_ref[i, f * columns + lo : f * columns + lo + HALO, :]
        out[...] = rows[...].astype(bf16)


def east(x):
    return 0.5 * (pltpu.roll(x, x.shape[0] - 1, 0) - pltpu.roll(x, 1, 0))


def north(x):
    return 0.5 * (pltpu.roll(x, x.shape[1] - 1, 1) - pltpu.roll(x, 1, 1))


def widened(ref, b, blocks):
    main = block_of(ref, b)
    after = block_of(ref, jnp.minimum(b + 1, blocks - 1))
    before = block_of(ref, jnp.maximum(b - 1, 0))
    lane = lax.broadcasted_iota(jnp.int32, main.shape, 1)
    zero = jnp.zeros_like(main)
    after = jnp.where(b < blocks - 1, after, zero)
    before = jnp.where(b > 0, before, zero)
    return jnp.concatenate([main, jnp.where(lane < LANES // 2, after, before)], axis=1)


def step_kernel(
    fields_ref, left_ref, right_ref, depth_ref, mask_ref, fric_ref, cor_ref, obs_ref,
    sleft_ref, sright_ref, out_ref, copies_ref, ext, lrows, rrows, statics,
):
    columns, lat = depth_ref.shape
    blocks = lat // LANES
    lo, hi = 8, 8 + columns
    me = lax.axis_index("member")
    lrows[...] = left_ref[...].astype(f32)
    rrows[...] = right_ref[...].astype(f32)
    ext[...] = jnp.zeros(ext.shape, f32)
    statics[...] = jnp.zeros(statics.shape, f32)
    sleft = widened(sleft_ref, me, blocks)
    sright = widened(sright_ref, me, blocks)
    statics[0, lo:hi, :] = widened(depth_ref, me, blocks)
    statics[0, lo - 3 : lo, :] = sleft[0:3, :]
    statics[0, hi : hi + 3, :] = sright[0:3, :]
    statics[1, lo:hi, :] = jnp.where(widened(mask_ref, me, blocks) == 1, 1.0, 0.0).astype(f32)
    statics[1, lo - 2 : lo, :] = sleft[3:5, :]
    statics[1, hi : hi + 2, :] = sright[3:5, :]
    statics[2, lo:hi, :] = widened(fric_ref, me, blocks)
    statics[2, lo - 1 : lo, :] = sleft[5:6, :]
    statics[2, hi : hi + 1, :] = sright[5:6, :]
    depth = statics[0]
    wet = statics[1]
    damped = wet * (1.0 / (1.0 + time_step * statics[2]))
    turning = widened(cor_ref, me, blocks)
    obs = block_of(obs_ref, me)

    for i in range(DISTINCT):
        fields = []
        for f in range(3):
            at = (i * 3 + f) * HALO
            ext[f, lo:hi, :] = fields_ref[i, f * columns : (f + 1) * columns, :]
            ext[f, lo - HALO : lo, :] = lrows[at : at + HALO, :]
            ext[f, hi : hi + HALO, :] = rrows[at : at + HALO, :]
            fields.append(ext[f])
        height, zonal, meridional = fields
        fresh = height - time_step * wet * (east(depth * zonal) + north(depth * meridional))
        innov = obs - fresh[lo:hi, :LANES]
        out_ref[i, 0] = innov
        b = innov.astype(bf16)
        for d in range(copies_ref.shape[0]):
            copies_ref[d, i * columns : (i + 1) * columns, :] = b
        zonal1 = damped * (zonal + time_step * (turning * meridional - east(fresh)))
        meridional1 = damped * (meridional - time_step * (turning * zonal + north(fresh)))
        change = -time_step * wet * (east(depth * zonal1) + north(depth * meridional1))
        zonal_part = damped * (zonal1 + time_step * (turning * meridional1))
        meridional_part = damped * (meridional1 - time_step * (turning * zonal1))
        for k, value in enumerate((change, zonal_part, meridional_part)):
            out_ref[i, k + 1] = value[lo:hi, :LANES]


def split_kernel(spread_ref, out_ref):
    s = spread_ref[...]
    high = s.astype(bf16)
    out_ref[0] = high
    out_ref[1] = (s - high.astype(f32)).astype(bf16)


def spread_dot(gathered_ref, spread_ref):
    blocks = gathered_ref.shape[0]
    lhs = jnp.concatenate([gathered_ref[b] for b in range(blocks)], axis=1)
    dims = (((1,), (1,)), ((), ()))
    return lax.dot_general(
        lhs, spread_ref[0], dims, preferred_element_type=f32
    ) + lax.dot_general(lhs, spread_ref[1], dims, preferred_element_type=f32)


def block_of(ref, b):
    return ref[:, pl.ds(pl.multiple_of(b * LANES, LANES), LANES)]


def wet_block(mask_ref, b):
    return jnp.where(block_of(mask_ref, b) == 1, 1.0, 0.0).astype(f32)


def update_kernel(
    gathered_ref, spread_ref, all_ref, mask_ref, obs_ref,
    innov_ref, copies_ref, edge_ref,
):
    columns = mask_ref.shape[0]
    me = lax.axis_index("member")
    wet = wet_block(mask_ref, me)
    obs = block_of(obs_ref, me)
    spreaded = spread_dot(gathered_ref, spread_ref)
    for i in range(DISTINCT):
        innov = all_ref[i, 0]
        sp = spreaded[i * columns : (i + 1) * columns, :]
        new = innov - nudge_rate * wet * (innov + sp) - all_ref[i, 1]
        innov_ref[i] = new
        b = new.astype(bf16)
        for d in range(copies_ref.shape[0]):
            copies_ref[d, i * columns : (i + 1) * columns, :] = b
        fresh = obs - new
        edge_ref[0, i : i + 1, :] = fresh[0:1, :]
        edge_ref[1, i : i + 1, :] = fresh[columns - 1 : columns, :]


def final_kernel(
    idx_ref, gathered_ref, spread_ref, innov_ref, left_ref, right_ref, all_ref,
    mask_ref, fric_ref, obs_ref, out_ref, state,
):
    columns = mask_ref.shape[0]
    blocks = gathered_ref.shape[0]
    me = lax.axis_index("member")
    wet = wet_block(mask_ref, me)
    obs = block_of(obs_ref, me)
    damped = wet * (1.0 / (1.0 + time_step * block_of(fric_ref, me)))
    before = jnp.maximum(me - 1, 0)
    after = jnp.minimum(me + 1, blocks - 1)
    obs_before = block_of(obs_ref, before)
    obs_after = block_of(obs_ref, after)
    has_before = jnp.where(me > 0, 1.0, 0.0).astype(f32)
    has_after = jnp.where(me < blocks - 1, 1.0, 0.0).astype(f32)
    lane = lax.broadcasted_iota(jnp.int32, (columns, LANES), 1)
    row = lax.broadcasted_iota(jnp.int32, (columns, LANES), 0)
    spreaded = spread_dot(gathered_ref, spread_ref)
    for i in range(DISTINCT):
        innov = innov_ref[i]
        fresh = obs - innov
        part = slice(i * columns, (i + 1) * columns)
        state[i, 0] = fresh + nudge_rate * wet * (innov + spreaded[part, :])
        fresh_before = has_before * (obs_before - gathered_ref[before, part, :].astype(f32))
        fresh_after = has_after * (obs_after - gathered_ref[after, part, :].astype(f32))
        down = jnp.where(lane == 0, pltpu.roll(fresh_before, 1, 1), pltpu.roll(fresh, 1, 1))
        up = jnp.where(
            lane == LANES - 1,
            pltpu.roll(fresh_after, LANES - 1, 1),
            pltpu.roll(fresh, LANES - 1, 1),
        )
        west = jnp.where(row == 0, left_ref[i : i + 1, :], pltpu.roll(fresh, 1, 0))
        easterly = jnp.where(
            row == columns - 1, right_ref[i : i + 1, :], pltpu.roll(fresh, columns - 1, 0)
        )
        state[i, 1] = all_ref[i, 2] - damped * (time_step * 0.5 * (easterly - west))
        state[i, 2] = all_ref[i, 3] - damped * (time_step * 0.5 * (up - down))
    for s in range(32):
        out_ref[s // 2, s % 2] = state[idx_ref[DISTINCT + s]]


def misfit_kernel(h_ref, mask_ref, obs_ref, out_ref, *, total):
    columns, lat = mask_ref.shape
    blocks = lat // LANES
    first = (lax.axis_index("lon") * columns).astype(f32)
    column = first + lax.broadcasted_iota(jnp.int32, (columns, LANES), 0).astype(f32)
    weight = 1.0 + 2.0 * column / total
    lane = lax.broadcasted_iota(jnp.int32, (1, LANES), 1)
    sums = jnp.zeros((1, LANES), f32)
    for p in range(2):
        acc = jnp.zeros((columns, LANES), f32)
        for b in range(blocks):
            part = slice(b * LANES, (b + 1) * LANES)
            wet = jnp.where(mask_ref[:, part] == 1, 1.0, 0.0).astype(f32)
            gap = obs_ref[:, part] - h_ref[b, p, 0]
            acc = acc + wet * (gap * gap)
        sums = jnp.where(lane == p, jnp.sum(acc * weight), sums)
    for d in range(out_ref.shape[0]):
        out_ref[d] = sums


def output_kernel(state_ref, out_ref):
    for b in range(state_ref.shape[0]):
        out_ref[:, :, :, b * LANES : (b + 1) * LANES] = state_ref[b]


def per_device(ensemble, copy_list, depth, land_mask, friction, coriolis, spread, observed):
    columns, lat = depth.shape
    members = lax.axis_size("member")
    lons = lax.axis_size("lon")
    blocks = lat // LANES
    rows = DISTINCT * columns
    shape = jax.ShapeDtypeStruct
    eastward = [(i, (i + 1) % lons) for i in range(lons)]
    westward = [((i + 1) % lons, i) for i in range(lons)]

    def swap(x):
        return lax.all_to_all(x, "member", 0, 0, tiled=True)

    packed, idx = call(
        pack_kernel,
        (shape((blocks, 6 * columns + 16, LANES), bf16), shape((64,), jnp.int32)),
        [SMEM, ANY],
        (VMEM, SMEM),
        [
            pltpu.VMEM(ensemble.shape, bf16),
            pltpu.SMEM((32,), jnp.int32),
            pltpu.SemaphoreType.DMA(()),
        ],
        limit=60,
    )(copy_list, ensemble)
    packed = swap(packed)
    shead, stail = call(
        static_kernel, (shape((8, lat), f32),) * 2, [VMEM] * 3, (VMEM, VMEM)
    )(depth, land_mask, friction)
    sleft = lax.ppermute(stail, "lon", eastward)
    sright = lax.ppermute(shead, "lon", westward)
    parts = call(
        split_kernel, shape((2,) + spread.shape, bf16), [VMEM], VMEM
    )(spread)
    halo_rows = -(-DISTINCT * 3 * HALO // 16) * 16
    fields, head, tail = call(
        select_kernel,
        (
            shape((DISTINCT, 3 * columns, 2 * LANES), f32),
            shape((halo_rows, 2 * LANES), bf16),
            shape((halo_rows, 2 * LANES), bf16),
        ),
        [SMEM, VMEM],
        (VMEM, VMEM, VMEM),
        [pltpu.VMEM((halo_rows, 2 * LANES), f32)],
    )(idx, packed)
    left = lax.ppermute(tail, "lon", eastward)
    right = lax.ppermute(head, "lon", westward)
    ext_rows = columns + 16
    step1, copies = call(
        step_kernel,
        (
            shape((DISTINCT, 4, columns, LANES), f32),
            shape((members, rows, LANES), bf16),
        ),
        [VMEM] * 10,
        (VMEM, VMEM),
        [
            pltpu.VMEM((3, ext_rows, 2 * LANES), f32),
            pltpu.VMEM((halo_rows, 2 * LANES), f32),
            pltpu.VMEM((halo_rows, 2 * LANES), f32),
            pltpu.VMEM((3, ext_rows, 2 * LANES), f32),
        ],
    )(
        fields, left, right, depth, land_mask, friction, coriolis[None, :], observed,
        sleft, sright,
    )
    gathered1 = swap(copies)
    innov2, copies, edges = call(
        update_kernel,
        (
            shape((DISTINCT, columns, LANES), f32),
            shape((members, rows, LANES), bf16),
            shape((2, DISTINCT, LANES), f32),
        ),
        [VMEM] * 5,
        (VMEM, VMEM, VMEM),
        flops=2 * 2 * rows * LANES * lat,
    )(gathered1, parts, step1, land_mask, observed)
    gathered2 = swap(copies)
    left = lax.ppermute(edges[1], "lon", eastward)
    right = lax.ppermute(edges[0], "lon", westward)
    state = call(
        final_kernel,
        shape((members, 2, 3, columns, LANES), f32),
        [SMEM] + [VMEM] * 9,
        VMEM,
        [pltpu.VMEM((DISTINCT, 3, columns, LANES), f32)],
        flops=2 * 2 * rows * LANES * lat,
    )(idx, gathered2, parts, innov2, left, right, step1, land_mask, friction, observed)
    state = swap(state)
    sums = call(
        functools.partial(misfit_kernel, total=float(columns * lons)),
        shape((lons, 1, LANES), f32),
        [VMEM] * 3,
        VMEM,
    )(state, land_mask, observed)
    sums = lax.all_to_all(sums, "lon", 0, 0, tiled=True)
    misfit = jnp.sum(sums, axis=(0, 1))[:2] / (lat * columns * lons)
    new_state = call(output_kernel, shape((2, 3, columns, lat), f32), [VMEM], VMEM)(state)
    return new_state, misfit


def solution(mesh):
    placed = (
        P("member", None, "lon", None),
        P(),
        P("lon", None),
        P("lon", None),
        P("lon", None),
        P(),
        P("member", None),
        P("lon", None),
    )
    return jax.shard_map(
        per_device,
        mesh=mesh,
        in_specs=placed,
        out_specs=(P("member", None, "lon", None), P("member")),
        check_vma=False,
    )
```

```python
import functools

import jax
import jax.numpy as jnp
from jax import lax
from jax.experimental import pallas as pl
from jax.experimental.pallas import tpu as pltpu
from jax.sharding import PartitionSpec as P

DISTINCT = 8
HALO = 3
EXTRA = 8
SHIFT = 4
LANES = 128
time_step = 0.2
nudge_rate = 0.3
f32 = jnp.float32
bf16 = jnp.bfloat16

VMEM = pl.BlockSpec(memory_space=pltpu.VMEM)
SMEM = pl.BlockSpec(memory_space=pltpu.SMEM)
ANY = pl.BlockSpec(memory_space=pl.ANY)


def call(kernel, out_shape, in_specs, out_specs, scratch=(), flops=1e6, bytes_accessed=1e6, limit=24):
    return pl.pallas_call(
        kernel,
        out_shape=out_shape,
        in_specs=in_specs,
        out_specs=out_specs,
        scratch_shapes=list(scratch),
        compiler_params=pltpu.CompilerParams(vmem_limit_bytes=limit * 1024 * 1024),
        cost_estimate=pl.CostEstimate(
            flops=int(flops), bytes_accessed=int(bytes_accessed), transcendentals=0
        ),
    )


def pack_kernel(ens_hbm, out_ref, ens_ref, sem):
    lat = ens_ref.shape[-1]
    blocks = out_ref.shape[0]
    fetch = pltpu.make_async_copy(ens_hbm, ens_ref, sem)
    fetch.start()
    row = lax.broadcasted_iota(jnp.int32, (16 * blocks, lat), 0)
    lane = lax.broadcasted_iota(jnp.int32, (16 * blocks, lat), 1)
    beside = row % 16
    source = (row // 16) * LANES + jnp.where(beside < HALO, beside - HALO, beside - HALO + LANES)
    pick = jnp.where((source == lane) & (beside < 2 * HALO), 1.0, 0.0).astype(bf16)
    fetch.wait()
    x = jnp.concatenate([ens_ref[p, f] for p in range(2) for f in range(3)], axis=0)
    halos = lax.dot_general(pick, x, (((1,), (1,)), ((), ())), preferred_element_type=f32)
    n = x.shape[0]
    halos = jnp.concatenate([halos, jnp.zeros((16 * blocks, LANES - n), f32)], axis=1).astype(bf16)
    for b in range(blocks):
        out_ref[b, 0:n, :] = x[:, b * LANES : (b + 1) * LANES]
        out_ref[b, n : n + 16, :] = halos[16 * b : 16 * b + 16, :]


def block_of(ref, b):
    return ref[:, pl.ds(pl.multiple_of(b * LANES, LANES), LANES)]


def widened(ref, b, blocks):
    main = block_of(ref, b)
    after = block_of(ref, jnp.minimum(b + 1, blocks - 1))
    before = block_of(ref, jnp.maximum(b - 1, 0))
    lane = lax.broadcasted_iota(jnp.int32, main.shape, 1)
    zero = jnp.zeros_like(main)
    after = jnp.where(b < blocks - 1, after, zero)
    before = jnp.where(b > 0, before, zero)
    return jnp.concatenate([main, jnp.where(lane < LANES // 2, after, before)], axis=1)


def static_kernel(
    copy_ref, depth_ref, mask_ref, fric_ref, obs_ref, cor_ref, spread_ref,
    own_ref, head_ref, turn_ref, split_ref, idx_ref, seen,
):
    for p in range(32):
        seen[p] = 0
    for s in range(32):
        seen[copy_ref[s]] = 1
    for i in range(DISTINCT):
        idx_ref[i] = 0
    count = jnp.int32(0)
    for p in range(32):
        used = seen[p]
        place = jnp.minimum(count, DISTINCT - 1)
        idx_ref[place] = jnp.where(used == 1, p, idx_ref[place])
        seen[p] = place
        count = count + used
    for s in range(32):
        idx_ref[DISTINCT + s] = seen[copy_ref[s]]

    blocks = depth_ref.shape[1] // LANES
    me = lax.axis_index("member")
    wet = jnp.where(widened(mask_ref, me, blocks) == 1, 1.0, 0.0).astype(f32)
    for k, value in enumerate(
        (
            widened(depth_ref, me, blocks),
            wet,
            widened(fric_ref, me, blocks),
            widened(obs_ref, me, blocks),
        )
    ):
        own_ref[k] = value
        head_ref[EXTRA * k : EXTRA * (k + 1), :] = value[:EXTRA, :]
    turn_ref[...] = widened(cor_ref, me, blocks)
    spread = spread_ref[...]
    high = spread.astype(bf16)
    split_ref[0] = high
    split_ref[1] = (spread - high.astype(f32)).astype(bf16)


def select_kernel(idx_ref, all_ref, fields_ref, head_ref, rows):
    columns = fields_ref.shape[1] // 3
    part = 3 * columns
    h = lax.broadcasted_iota(jnp.int32, (16, LANES), 0)
    lane = lax.broadcasted_iota(jnp.int32, (16, LANES), 1)
    target = jnp.where(h < HALO, h + LANES - HALO, h - HALO)
    place = jnp.where((target == lane) & (h < 2 * HALO), 1.0, 0.0).astype(bf16)
    for i in range(DISTINCT):
        particle = idx_ref[i]
        src, p = particle // 2, particle % 2
        main = all_ref[src, pl.ds(pl.multiple_of(p * part, 16), part), :]
        halos = all_ref[src, 2 * part : 2 * part + 16, :]
        tile = lax.dot_general(halos, place, (((0,), (0,)), ((), ())), preferred_element_type=f32)
        fields_ref[i, :, :LANES] = main.astype(f32)
        fields_ref[i, :, LANES:] = jnp.where(p == 0, tile[:part], tile[part : 2 * part])
        for f in range(3):
            at = (i * 3 + f) * EXTRA
            rows[at : at + EXTRA, :] = fields_ref[i, f * columns : f * columns + EXTRA, :]
    head_ref[...] = rows[...].astype(bf16)


def east(x):
    return 0.5 * (pltpu.roll(x, x.shape[0] - 1, 0) - pltpu.roll(x, 1, 0))


def north(x):
    return 0.5 * (pltpu.roll(x, x.shape[1] - 1, 1) - pltpu.roll(x, 1, 1))


def step_kernel(
    fields_ref, right_ref, own_ref, sright_ref, turn_ref,
    out_ref, work_ref, copies_ref, rrows, compact,
):
    columns = own_ref.shape[1]
    width = columns + 2
    keep = slice(SHIFT - 1, SHIFT - 1 + width)
    rrows[...] = right_ref[...].astype(f32)

    def static(k):
        return jnp.concatenate([own_ref[k], sright_ref[EXTRA * k : EXTRA * (k + 1), :]], axis=0)

    depth, wet, friction, obs = (static(k) for k in range(4))
    damped = wet * (1.0 / (1.0 + time_step * friction))
    turning = turn_ref[...]
    for k, value in enumerate((wet, damped, obs)):
        work_ref[k] = value[keep, :]
    for i in range(DISTINCT):
        fields = []
        for f in range(3):
            at = (i * 3 + f) * EXTRA
            fields.append(
                jnp.concatenate(
                    [fields_ref[i, f * columns : (f + 1) * columns, :], rrows[at : at + EXTRA, :]],
                    axis=0,
                )
            )
        height, zonal, meridional = fields
        fresh = height - time_step * wet * (east(depth * zonal) + north(depth * meridional))
        zonal1 = damped * (zonal + time_step * (turning * meridional - east(fresh)))
        meridional1 = damped * (meridional - time_step * (turning * zonal + north(fresh)))
        change = -time_step * wet * (east(depth * zonal1) + north(depth * meridional1))
        zonal_part = damped * (zonal1 + time_step * (turning * meridional1))
        meridional_part = damped * (meridional1 - time_step * (turning * zonal1))
        innov = obs - fresh
        compact[i * width : (i + 1) * width, :] = innov[keep, :LANES]
        for k, value in enumerate((innov, change, zonal_part, meridional_part)):
            out_ref[i, k] = value[keep, :LANES]
    sent = compact[...].astype(bf16)
    for d in range(copies_ref.shape[0]):
        copies_ref[d] = sent


def spread_dot(gathered_ref, spread_ref):
    blocks = gathered_ref.shape[0]
    lhs = jnp.concatenate([gathered_ref[b] for b in range(blocks)], axis=1)
    dims = (((1,), (1,)), ((), ()))
    return lax.dot_general(
        lhs, spread_ref[0], dims, preferred_element_type=f32
    ) + lax.dot_general(lhs, spread_ref[1], dims, preferred_element_type=f32)


def update_kernel(
    gathered_ref, spread_ref, all_ref, work_ref, innov_ref, copies_ref, spreaded, compact
):
    width = work_ref.shape[1]
    wet = work_ref[0, :, :LANES]
    spreaded[...] = spread_dot(gathered_ref, spread_ref)
    for i in range(DISTINCT):
        innov = all_ref[i, 0]
        sp = spreaded[i * width : (i + 1) * width, :]
        new = innov - nudge_rate * wet * (innov + sp) - all_ref[i, 1]
        innov_ref[i] = new
        compact[i * width : (i + 1) * width, :] = new
    sent = compact[...].astype(bf16)
    for d in range(copies_ref.shape[0]):
        copies_ref[d] = sent


def final_kernel(
    idx_ref, gathered_ref, spread_ref, innov_ref, all_ref, work_ref,
    out_ref, state, sums, spreaded, sides, *, total,
):
    width = work_ref.shape[1]
    columns = width - 2
    blocks = gathered_ref.shape[0]
    me = lax.axis_index("member")
    inner = slice(1, 1 + columns)
    wet = work_ref[0, inner, :LANES]
    damped = work_ref[1, inner, :LANES]
    obs_tile = work_ref[2, inner, LANES:]
    obs = work_ref[2, inner, :LANES]
    before = jnp.maximum(me - 1, 0)
    after = jnp.minimum(me + 1, blocks - 1)
    has_before = jnp.where(me > 0, 1.0, 0.0).astype(f32)
    has_after = jnp.where(me < blocks - 1, 1.0, 0.0).astype(f32)
    lane = lax.broadcasted_iota(jnp.int32, (columns, LANES), 1)
    first = lax.axis_index("lon") * columns + SHIFT
    column = first + lax.broadcasted_iota(jnp.int32, (columns, LANES), 0)
    column = jnp.where(column >= total, column - total, column).astype(f32)
    weight = wet * (1.0 + 2.0 * column / total)
    spreaded[...] = spread_dot(gathered_ref, spread_ref)
    sides[0] = gathered_ref[before].astype(f32)
    sides[1] = gathered_ref[after].astype(f32)
    for i in range(DISTINCT):
        part = slice(i * width + 1, i * width + 1 + columns)
        innov = innov_ref[i, inner, :]
        fresh = obs - innov
        height = fresh + nudge_rate * wet * (innov + spreaded[part, :])
        state[i, 0:columns, :] = height
        gap = obs - height
        sums[i : i + 1, :] = jnp.sum(weight * (gap * gap), axis=0, keepdims=True)
        fresh_before = has_before * (obs_tile - sides[0, part, :])
        fresh_after = has_after * (obs_tile - sides[1, part, :])
        down = jnp.where(lane == 0, pltpu.roll(fresh_before, 1, 1), pltpu.roll(fresh, 1, 1))
        up = jnp.where(
            lane == LANES - 1,
            pltpu.roll(fresh_after, LANES - 1, 1),
            pltpu.roll(fresh, LANES - 1, 1),
        )
        west = work_ref[2, 0:columns, :LANES] - innov_ref[i, 0:columns, :]
        easterly = work_ref[2, 2:width, :LANES] - innov_ref[i, 2:width, :]
        state[i, columns : 2 * columns, :] = all_ref[i, 2, inner, :] - damped * (
            time_step * 0.5 * (easterly - west)
        )
        state[i, 2 * columns : 3 * columns, :] = all_ref[i, 3, inner, :] - damped * (
            time_step * 0.5 * (up - down)
        )
    n = 3 * columns
    for d in range(out_ref.shape[0]):
        out_ref[d, 2 * n : 2 * n + 8, :] = jnp.zeros((8, LANES), f32)
        for p in range(2):
            place = idx_ref[DISTINCT + 2 * d + p]
            out_ref[d, p * n : (p + 1) * n, :] = state[place]
            out_ref[d, 2 * n + p : 2 * n + p + 1, :] = sums[pl.ds(place, 1), :]


def tail_kernel(state_ref, sums_ref, tail_ref, *, columns):
    blocks = state_ref.shape[0]
    n = 6 * columns
    acc = state_ref[0, n : n + 8, :]
    for b in range(1, blocks):
        acc = acc + state_ref[b, n : n + 8, :]
    acc = jnp.sum(acc, axis=1, keepdims=True)
    lane = lax.broadcasted_iota(jnp.int32, (1, LANES), 1)
    row = jnp.where(lane == 0, acc[0:1], jnp.where(lane == 1, acc[1:2], 0.0))
    for d in range(sums_ref.shape[0]):
        sums_ref[d] = row
    for b in range(blocks):
        for k in range(6):
            at = (k + 1) * columns - SHIFT
            tail_ref[k * SHIFT : (k + 1) * SHIFT, b * LANES : (b + 1) * LANES] = state_ref[
                b, at : at + SHIFT, :
            ]


def output_kernel(state_ref, tail_ref, out_ref):
    columns = out_ref.shape[2]
    for b in range(state_ref.shape[0]):
        part = slice(b * LANES, (b + 1) * LANES)
        for p in range(2):
            for f in range(3):
                k = p * 3 + f
                out_ref[p, f, 0:SHIFT, part] = tail_ref[k * SHIFT : (k + 1) * SHIFT, part]
                out_ref[p, f, SHIFT:columns, part] = state_ref[
                    b, k * columns : (k + 1) * columns - SHIFT, :
                ]


def per_device(ensemble, copy_list, depth, land_mask, friction, coriolis, spread, observed):
    columns, lat = depth.shape
    members = lax.axis_size("member")
    lons = lax.axis_size("lon")
    blocks = lat // LANES
    width = columns + 2
    rows = DISTINCT * width
    wide = 2 * LANES
    shape = jax.ShapeDtypeStruct
    eastward = [(i, (i + 1) % lons) for i in range(lons)]
    westward = [((i + 1) % lons, i) for i in range(lons)]

    def swap(x):
        return lax.all_to_all(x, "member", 0, 0, tiled=True)

    packed = call(
        pack_kernel,
        shape((blocks, 6 * columns + 16, LANES), bf16),
        [ANY],
        VMEM,
        [pltpu.VMEM(ensemble.shape, bf16), pltpu.SemaphoreType.DMA(())],
        limit=60,
    )(ensemble)
    packed = swap(packed)
    own, shead, turning, parts, idx = call(
        static_kernel,
        (
            shape((4, columns, wide), f32),
            shape((4 * EXTRA, wide), f32),
            shape((1, wide), f32),
            shape((2,) + spread.shape, bf16),
            shape((64,), jnp.int32),
        ),
        [SMEM] + [VMEM] * 6,
        (VMEM, VMEM, VMEM, VMEM, SMEM),
        [pltpu.SMEM((32,), jnp.int32)],
    )(copy_list, depth, land_mask, friction, observed, coriolis[None, :], spread)
    sright = lax.ppermute(shead, "lon", westward)
    fields, head = call(
        select_kernel,
        (
            shape((DISTINCT, 3 * columns, wide), f32),
            shape((DISTINCT * 3 * EXTRA, wide), bf16),
        ),
        [SMEM, VMEM],
        (VMEM, VMEM),
        [pltpu.VMEM((DISTINCT * 3 * EXTRA, wide), f32)],
    )(idx, packed)
    right = lax.ppermute(head, "lon", westward)
    step1, work, copies = call(
        step_kernel,
        (
            shape((DISTINCT, 4, width, LANES), f32),
            shape((3, width, wide), f32),
            shape((members, rows, LANES), bf16),
        ),
        [VMEM] * 5,
        (VMEM, VMEM, VMEM),
        [
            pltpu.VMEM((DISTINCT * 3 * EXTRA, wide), f32),
            pltpu.VMEM((rows, LANES), f32),
        ],
    )(fields, right, own, sright, turning)
    gathered1 = swap(copies)
    innov2, copies = call(
        update_kernel,
        (
            shape((DISTINCT, width, LANES), f32),
            shape((members, rows, LANES), bf16),
        ),
        [VMEM] * 4,
        (VMEM, VMEM),
        [pltpu.VMEM((rows, LANES), f32)] * 2,
        flops=2 * 2 * rows * LANES * lat,
    )(gathered1, parts, step1, work)
    gathered2 = swap(copies)
    state = call(
        functools.partial(final_kernel, total=columns * lons),
        shape((members, 6 * columns + 8, LANES), f32),
        [SMEM] + [VMEM] * 5,
        VMEM,
        [
            pltpu.VMEM((DISTINCT, 3 * columns, LANES), f32),
            pltpu.VMEM((DISTINCT, LANES), f32),
            pltpu.VMEM((rows, LANES), f32),
            pltpu.VMEM((2, rows, LANES), f32),
        ],
        flops=2 * 2 * rows * LANES * lat,
    )(idx, gathered2, parts, innov2, step1, work)
    state = swap(state)
    sums, tail = call(
        functools.partial(tail_kernel, columns=columns),
        (shape((lons, 1, LANES), f32), shape((6 * SHIFT, lat), f32)),
        [VMEM],
        (VMEM, VMEM),
    )(state)
    sums = lax.all_to_all(sums, "lon", 0, 0, tiled=True)
    tail = lax.ppermute(tail, "lon", eastward)
    misfit = jnp.sum(sums, axis=(0, 1))[:2] / (lat * columns * lons)
    new_state = call(output_kernel, shape((2, 3, columns, lat), f32), [VMEM, VMEM], VMEM)(
        state, tail
    )
    return new_state, misfit


def solution(mesh):
    placed = (
        P("member", None, "lon", None),
        P(),
        P("lon", None),
        P("lon", None),
        P("lon", None),
        P(),
        P("member", None),
        P("lon", None),
    )
    return jax.shard_map(
        per_device,
        mesh=mesh,
        in_specs=placed,
        out_specs=(P("member", None, "lon", None), P("member")),
        check_vma=False,
    )
```

```python
import functools

import jax
import jax.numpy as jnp
from jax import lax
from jax.experimental import pallas as pl
from jax.experimental.pallas import tpu as pltpu
from jax.sharding import PartitionSpec as P

DISTINCT = 8
HALO = 3
EXTRA = 8
SHIFT = 4
LANES = 128
time_step = 0.2
nudge_rate = 0.3
f32 = jnp.float32
bf16 = jnp.bfloat16

VMEM = pl.BlockSpec(memory_space=pltpu.VMEM)
SMEM = pl.BlockSpec(memory_space=pltpu.SMEM)
ANY = pl.BlockSpec(memory_space=pl.ANY)


def call(kernel, out_shape, in_specs, out_specs, scratch=(), flops=1e6, bytes_accessed=1e6, limit=24):
    return pl.pallas_call(
        kernel,
        out_shape=out_shape,
        in_specs=in_specs,
        out_specs=out_specs,
        scratch_shapes=list(scratch),
        compiler_params=pltpu.CompilerParams(vmem_limit_bytes=limit * 1024 * 1024),
        cost_estimate=pl.CostEstimate(
            flops=int(flops), bytes_accessed=int(bytes_accessed), transcendentals=0
        ),
    )


def halo_lanes(shape):
    lane = lax.broadcasted_iota(jnp.int32, shape, 1)
    return (lane < HALO) | (lane >= LANES - HALO)


def fold(acc, tile, group):
    lane = lax.broadcasted_iota(jnp.int32, tile.shape, 1)
    at = 2 * HALO * group
    moved = pltpu.roll(tile, at + HALO, 1)
    return jnp.where((lane >= at) & (lane < at + 2 * HALO), moved, acc)


def unfold(acc, group):
    moved = pltpu.roll(acc, LANES - (2 * HALO * group + HALO), 1)
    return jnp.where(halo_lanes(acc.shape), moved, 0.0)


def pack_kernel(ens_hbm, out_ref, ens_ref, sem):
    blocks = out_ref.shape[0]
    columns = ens_ref.shape[2]
    fetch = pltpu.make_async_copy(ens_hbm, ens_ref, sem)
    fetch.start()
    fetch.wait()
    low = lax.broadcasted_iota(jnp.int32, (columns, LANES), 1) < LANES // 2
    zero = jnp.zeros((columns, LANES), f32)
    halos = [zero] * blocks
    for p in range(2):
        for f in range(3):
            k = p * 3 + f
            tiles = [ens_ref[p, f, :, b * LANES : (b + 1) * LANES] for b in range(blocks)]
            wide = [zero] + [t.astype(f32) for t in tiles] + [zero]
            for b in range(blocks):
                out_ref[b, k * columns : (k + 1) * columns, :] = tiles[b]
                halos[b] = fold(halos[b], jnp.where(low, wide[b + 2], wide[b]), k)
    for b in range(blocks):
        out_ref[b, 6 * columns : 7 * columns, :] = halos[b].astype(bf16)


def block_of(ref, b):
    return ref[:, pl.ds(pl.multiple_of(b * LANES, LANES), LANES)]


def widened(ref, b, blocks):
    main = block_of(ref, b)
    after = block_of(ref, jnp.minimum(b + 1, blocks - 1))
    before = block_of(ref, jnp.maximum(b - 1, 0))
    lane = lax.broadcasted_iota(jnp.int32, main.shape, 1)
    zero = jnp.zeros_like(main)
    after = jnp.where(b < blocks - 1, after, zero)
    before = jnp.where(b > 0, before, zero)
    return jnp.concatenate([main, jnp.where(lane < LANES // 2, after, before)], axis=1)


def pieces(x):
    first = x.astype(bf16).astype(f32)
    rest = x - first
    second = rest.astype(bf16).astype(f32)
    return first, second, rest - second


def static_kernel(depth_ref, mask_ref, fric_ref, obs_ref, cor_ref, own_ref, head_ref, turn_ref):
    blocks = depth_ref.shape[1] // LANES
    me = lax.axis_index("member")
    depth = widened(depth_ref, me, blocks)
    wet = jnp.where(widened(mask_ref, me, blocks) == 1, 1.0, 0.0).astype(f32)
    friction = widened(fric_ref, me, blocks)
    observed = widened(obs_ref, me, blocks)
    for k, value in enumerate((depth, wet, friction, observed)):
        own_ref[k] = value
    parts = [
        part for value in (depth, friction, observed) for part in pieces(value[:EXTRA, :])
    ]
    for k, part in enumerate(parts + [wet[:EXTRA, :]]):
        head_ref[EXTRA * k : EXTRA * (k + 1), :] = part
    turn_ref[...] = widened(cor_ref, me, blocks)


def index_kernel(copy_ref, spread_ref, split_ref, idx_ref, seen):
    for p in range(32):
        seen[p] = 0
    for s in range(32):
        seen[copy_ref[s]] = 1
    for i in range(DISTINCT):
        idx_ref[i] = 0
    count = jnp.int32(0)
    for p in range(32):
        used = seen[p]
        place = jnp.minimum(count, DISTINCT - 1)
        idx_ref[place] = jnp.where(used == 1, p, idx_ref[place])
        seen[p] = place
        count = count + used
    for s in range(32):
        idx_ref[DISTINCT + s] = seen[copy_ref[s]]
    spread = spread_ref[...]
    high = spread.astype(bf16)
    split_ref[0] = high
    split_ref[1] = (spread - high.astype(f32)).astype(bf16)


def select_kernel(idx_ref, all_ref, shead_ref, fields_ref, head_ref, rows):
    columns = fields_ref.shape[1] // 3
    part = 3 * columns
    for i in range(DISTINCT):
        particle = idx_ref[i]
        src, p = particle // 2, particle % 2
        main = all_ref[src, pl.ds(pl.multiple_of(p * part, 16), part), :]
        folded = all_ref[src, 2 * part : 2 * part + columns, :].astype(f32)
        fields_ref[i, :, :LANES] = main.astype(f32)
        for f in range(3):
            fields_ref[i, f * columns : (f + 1) * columns, LANES:] = jnp.where(
                p == 0, unfold(folded, f), unfold(folded, 3 + f)
            )
            at = (i * 3 + f) * EXTRA
            rows[at : at + EXTRA, :] = fields_ref[i, f * columns : f * columns + EXTRA, :]
    n = rows.shape[0]
    rows[DISTINCT * 3 * EXTRA : n, :] = shead_ref[...]
    head_ref[0:n, :] = rows[:, :LANES].astype(bf16)
    halos = jnp.zeros((16, LANES), f32)
    for g in range(n // 16):
        halos = fold(halos, rows[16 * g : 16 * g + 16, LANES:], g)
    head_ref[n : n + 16, :] = halos.astype(bf16)


def east(x):
    return 0.5 * (pltpu.roll(x, x.shape[0] - 1, 0) - pltpu.roll(x, 1, 0))


def north(x):
    return 0.5 * (pltpu.roll(x, x.shape[1] - 1, 1) - pltpu.roll(x, 1, 1))


def step_kernel(
    fields_ref, right_ref, own_ref, turn_ref, out_ref, work_ref, copies_ref, rrows,
):
    columns = own_ref.shape[1]
    keep = slice(SHIFT, SHIFT + columns)
    n = rrows.shape[0]
    rrows[:, :LANES] = right_ref[0:n, :].astype(f32)
    folded = right_ref[n : n + 16, :].astype(f32)
    for g in range(n // 16):
        rrows[16 * g : 16 * g + 16, LANES:] = unfold(folded, g)
    base = DISTINCT * 3 * EXTRA

    def beside(k):
        return rrows[base + EXTRA * k : base + EXTRA * (k + 1), :]

    def static(k, at):
        extra = (beside(at) + beside(at + 1)) + beside(at + 2)
        return jnp.concatenate([own_ref[k], extra], axis=0)

    depth = static(0, 0)
    friction = static(2, 3)
    obs = static(3, 6)
    wet = jnp.concatenate([own_ref[1], beside(9)], axis=0)
    damped = wet * (1.0 / (1.0 + time_step * friction))
    turning = turn_ref[...]
    for k, value in enumerate((wet, damped, obs)):
        work_ref[k] = value[keep, :]
    for i in range(DISTINCT):
        fields = []
        for f in range(3):
            at = (i * 3 + f) * EXTRA
            fields.append(
                jnp.concatenate(
                    [fields_ref[i, f * columns : (f + 1) * columns, :], rrows[at : at + EXTRA, :]],
                    axis=0,
                )
            )
        height, zonal, meridional = fields
        fresh = height - time_step * wet * (east(depth * zonal) + north(depth * meridional))
        zonal1 = damped * (zonal + time_step * (turning * meridional - east(fresh)))
        meridional1 = damped * (meridional - time_step * (turning * zonal + north(fresh)))
        change = -time_step * wet * (east(depth * zonal1) + north(depth * meridional1))
        zonal_part = damped * (zonal1 + time_step * (turning * meridional1))
        meridional_part = damped * (meridional1 - time_step * (turning * zonal1))
        innov = (obs - fresh)[keep, :LANES]
        sent = innov.astype(bf16)
        for d in range(copies_ref.shape[0]):
            copies_ref[d, i * columns : (i + 1) * columns, :] = sent
        out_ref[i, 0] = innov
        for k, value in enumerate((change, zonal_part, meridional_part)):
            out_ref[i, k + 1] = value[keep, :LANES]


def spread_dot(gathered_ref, spread_ref):
    blocks = gathered_ref.shape[0]
    lhs = jnp.concatenate([gathered_ref[b] for b in range(blocks)], axis=1)
    dims = (((1,), (1,)), ((), ()))
    return lax.dot_general(
        lhs, spread_ref[0], dims, preferred_element_type=f32
    ) + lax.dot_general(lhs, spread_ref[1], dims, preferred_element_type=f32)


def update_kernel(gathered_ref, spread_ref, all_ref, work_ref, innov_ref, copies_ref):
    columns = work_ref.shape[1]
    wet = work_ref[0, :, :LANES]
    spreaded = spread_dot(gathered_ref, spread_ref)
    for i in range(DISTINCT):
        innov = all_ref[i, 0]
        sp = spreaded[i * columns : (i + 1) * columns, :]
        new = innov - nudge_rate * wet * (innov + sp) - all_ref[i, 1]
        innov_ref[i] = new
        sent = new.astype(bf16)
        for d in range(copies_ref.shape[0]):
            copies_ref[d, i * columns : (i + 1) * columns, :] = sent


def final_kernel(
    gathered_ref, spread_ref, innov_ref, all_ref, work_ref,
    state_ref, tail_ref, edge_ref, sums_ref, *, total,
):
    columns = work_ref.shape[1]
    blocks = gathered_ref.shape[0]
    me = lax.axis_index("member")
    wet = work_ref[0, :, :LANES]
    damped = work_ref[1, :, :LANES]
    obs_tile = work_ref[2, :, LANES:]
    obs = work_ref[2, :, :LANES]
    before = jnp.maximum(me - 1, 0)
    after = jnp.minimum(me + 1, blocks - 1)
    has_before = jnp.where(me > 0, 1.0, 0.0).astype(f32)
    has_after = jnp.where(me < blocks - 1, 1.0, 0.0).astype(f32)
    lane = lax.broadcasted_iota(jnp.int32, (columns, LANES), 1)
    line = lax.broadcasted_iota(jnp.int32, (columns, LANES), 0)
    first = lax.axis_index("lon") * columns + SHIFT
    column = first + line
    column = jnp.where(column >= total, column - total, column).astype(f32)
    weight = wet * (1.0 + 2.0 * column / total)
    spreaded = spread_dot(gathered_ref, spread_ref)
    row = jnp.zeros((1, LANES), f32)
    for i in range(DISTINCT):
        part = slice(i * columns, (i + 1) * columns)
        innov = innov_ref[i]
        fresh = obs - innov
        height = fresh + nudge_rate * wet * (innov + spreaded[part, :])
        gap = obs - height
        row = jnp.where(lane[0:1] == i, jnp.sum(weight * (gap * gap)), row)
        near = gathered_ref[before, part, :].astype(f32)
        far = gathered_ref[after, part, :].astype(f32)
        fresh_before = has_before * (obs_tile - near)
        fresh_after = has_after * (obs_tile - far)
        down = jnp.where(lane == 0, pltpu.roll(fresh_before, 1, 1), pltpu.roll(fresh, 1, 1))
        up = jnp.where(
            lane == LANES - 1,
            pltpu.roll(fresh_after, LANES - 1, 1),
            pltpu.roll(fresh, LANES - 1, 1),
        )
        west = jnp.where(line == 0, 0.0, pltpu.roll(fresh, 1, 0))
        easterly = jnp.where(line == columns - 1, 0.0, pltpu.roll(fresh, columns - 1, 0))
        zonal = all_ref[i, 2] - damped * (time_step * 0.5 * (easterly - west))
        meridional = all_ref[i, 3] - damped * (time_step * 0.5 * (up - down))
        for f, value in enumerate((height, zonal, meridional)):
            state_ref[i, f * columns : (f + 1) * columns, :] = value
            at = (i * 3 + f) * SHIFT
            tail_ref[at : at + SHIFT, :] = value[columns - SHIFT :, :]
        at = DISTINCT * 3 * SHIFT + i
        tail_ref[at : at + 1, :] = fresh[columns - 1 :, :]
        edge_ref[i : i + 1, :] = fresh[0:1, :]
    for d in range(sums_ref.shape[0]):
        sums_ref[d] = row


def slots_kernel(idx_ref, state_ref, tail_ref, edge_ref, own_ref, sums_ref, out_ref, moved):
    columns = state_ref.shape[1] // 3
    at = slice(SHIFT - 1, SHIFT + 1)
    damped = own_ref[1, at, :LANES] * (1.0 / (1.0 + time_step * own_ref[2, at, :LANES]))
    side = damped * (time_step * 0.5)
    last = DISTINCT * 3 * SHIFT
    for i in range(DISTINCT):
        for f in range(3):
            k = i * 3 + f
            moved[i, f * columns : (f + 1) * columns, :] = jnp.concatenate(
                [
                    tail_ref[k * SHIFT : (k + 1) * SHIFT, :],
                    state_ref[i, f * columns : (f + 1) * columns - SHIFT, :],
                ],
                axis=0,
            )
        row = columns + SHIFT - 1
        moved[i, row : row + 1, :] = moved[i, row : row + 1, :] - side[0:1] * edge_ref[i : i + 1, :]
        moved[i, row + 1 : row + 2, :] = (
            moved[i, row + 1 : row + 2, :] + side[1:2] * tail_ref[last + i : last + i + 1, :]
        )
    row = jnp.broadcast_to(jnp.sum(sums_ref[...], axis=0), (8, LANES))
    n = 3 * columns
    for d in range(out_ref.shape[0]):
        for p in range(2):
            out_ref[d, p * n : (p + 1) * n, :] = moved[idx_ref[DISTINCT + 2 * d + p]]
        out_ref[d, 2 * n : 2 * n + 8, :] = row


def output_kernel(idx_ref, state_ref, out_ref, misfit_ref, *, cells):
    columns = out_ref.shape[2]
    blocks = state_ref.shape[0]
    n = 6 * columns
    me = lax.axis_index("member")
    row = jnp.zeros((1, LANES), f32)
    for b in range(blocks):
        row = row + state_ref[b, n : n + 1, :]
        for p in range(2):
            for f in range(3):
                k = p * 3 + f
                out_ref[p, f, :, b * LANES : (b + 1) * LANES] = state_ref[
                    b, k * columns : (k + 1) * columns, :
                ]
    lane = lax.broadcasted_iota(jnp.int32, (1, LANES), 1)
    for p in range(2):
        place = idx_ref[DISTINCT + 2 * me + p]
        misfit_ref[p] = jnp.sum(jnp.where(lane == place, row, 0.0)) / cells


def per_device(ensemble, copy_list, depth, land_mask, friction, coriolis, spread, observed):
    columns, lat = depth.shape
    members = lax.axis_size("member")
    lons = lax.axis_size("lon")
    blocks = lat // LANES
    rows = DISTINCT * columns
    wide = 2 * LANES
    statics = 10 * EXTRA
    halo_rows = DISTINCT * 3 * EXTRA + statics
    shape = jax.ShapeDtypeStruct
    eastward = [(i, (i + 1) % lons) for i in range(lons)]
    westward = [((i + 1) % lons, i) for i in range(lons)]

    def swap(x):
        return lax.all_to_all(x, "member", 0, 0, tiled=True)

    packed = call(
        pack_kernel,
        shape((blocks, 7 * columns, LANES), bf16),
        [ANY],
        VMEM,
        [pltpu.VMEM(ensemble.shape, bf16), pltpu.SemaphoreType.DMA(())],
        limit=60,
    )(ensemble)
    packed = swap(packed)
    own, shead, turning = call(
        static_kernel,
        (shape((4, columns, wide), f32), shape((statics, wide), f32), shape((1, wide), f32)),
        [VMEM] * 5,
        (VMEM, VMEM, VMEM),
    )(depth, land_mask, friction, observed, coriolis[None, :])
    parts, idx = call(
        index_kernel,
        (shape((2,) + spread.shape, bf16), shape((64,), jnp.int32)),
        [SMEM, VMEM],
        (VMEM, SMEM),
        [pltpu.SMEM((32,), jnp.int32)],
    )(copy_list, spread)
    packed, own, turning, parts = lax.optimization_barrier((packed, own, turning, parts))
    fields, head = call(
        select_kernel,
        (
            shape((DISTINCT, 3 * columns, wide), f32),
            shape((halo_rows + 16, LANES), bf16),
        ),
        [SMEM, VMEM, VMEM],
        (VMEM, VMEM),
        [pltpu.VMEM((halo_rows, wide), f32)],
    )(idx, packed, shead)
    right = lax.ppermute(head, "lon", westward)
    step1, work, copies = call(
        step_kernel,
        (
            shape((DISTINCT, 4, columns, LANES), f32),
            shape((3, columns, wide), f32),
            shape((members, rows, LANES), bf16),
        ),
        [VMEM] * 4,
        (VMEM, VMEM, VMEM),
        [pltpu.VMEM((halo_rows, wide), f32)],
    )(fields, right, own, turning)
    gathered1 = swap(copies)
    innov2, copies = call(
        update_kernel,
        (
            shape((DISTINCT, columns, LANES), f32),
            shape((members, rows, LANES), bf16),
        ),
        [VMEM] * 4,
        (VMEM, VMEM),
        flops=2 * 2 * rows * LANES * lat,
    )(gathered1, parts, step1, work)
    gathered2 = swap(copies)
    state, tail, edge, sums = call(
        functools.partial(final_kernel, total=columns * lons),
        (
            shape((DISTINCT, 3 * columns, LANES), f32),
            shape((DISTINCT * (3 * SHIFT + 1), LANES), f32),
            shape((DISTINCT, LANES), f32),
            shape((lons, 1, LANES), f32),
        ),
        [VMEM] * 5,
        (VMEM,) * 4,
        flops=2 * 2 * rows * LANES * lat,
    )(gathered2, parts, innov2, step1, work)
    sums = lax.all_to_all(sums, "lon", 0, 0, tiled=True)
    tail = lax.ppermute(tail, "lon", eastward)
    state = call(
        slots_kernel,
        shape((members, 6 * columns + 8, LANES), f32),
        [SMEM] + [VMEM] * 5,
        VMEM,
        [pltpu.VMEM((DISTINCT, 3 * columns, LANES), f32)],
    )(idx, state, tail, edge, own, sums)
    state = swap(state)
    return call(
        functools.partial(output_kernel, cells=float(lat * columns * lons)),
        (shape((2, 3, columns, lat), f32), shape((2,), f32)),
        [SMEM, VMEM],
        (VMEM, SMEM),
    )(idx, state)


def solution(mesh):
    placed = (
        P("member", None, "lon", None),
        P(),
        P("lon", None),
        P("lon", None),
        P("lon", None),
        P(),
        P("member", None),
        P("lon", None),
    )
    return jax.shard_map(
        per_device,
        mesh=mesh,
        in_specs=placed,
        out_specs=(P("member", None, "lon", None), P("member")),
        check_vma=False,
    )
```

```python
import functools

import jax
import jax.numpy as jnp
from jax import lax
from jax.experimental import pallas as pl
from jax.experimental.pallas import tpu as pltpu
from jax.sharding import PartitionSpec as P

DISTINCT = 8
HALO = 3
EXTRA = 8
SHIFT = 4
LANES = 128
time_step = 0.2
nudge_rate = 0.3
f32 = jnp.float32
bf16 = jnp.bfloat16

VMEM = pl.BlockSpec(memory_space=pltpu.VMEM)
SMEM = pl.BlockSpec(memory_space=pltpu.SMEM)
ANY = pl.BlockSpec(memory_space=pl.ANY)


def call(kernel, out_shape, in_specs, out_specs, scratch=(), flops=1e6, bytes_accessed=1e6, limit=24):
    return pl.pallas_call(
        kernel,
        out_shape=out_shape,
        in_specs=in_specs,
        out_specs=out_specs,
        scratch_shapes=list(scratch),
        compiler_params=pltpu.CompilerParams(vmem_limit_bytes=limit * 1024 * 1024),
        cost_estimate=pl.CostEstimate(
            flops=int(flops), bytes_accessed=int(bytes_accessed), transcendentals=0
        ),
    )


def halo_lanes(shape):
    lane = lax.broadcasted_iota(jnp.int32, shape, 1)
    return (lane < HALO) | (lane >= LANES - HALO)


def fold(acc, tile, group):
    lane = lax.broadcasted_iota(jnp.int32, tile.shape, 1)
    at = 2 * HALO * group
    moved = pltpu.roll(tile, at + HALO, 1)
    return jnp.where((lane >= at) & (lane < at + 2 * HALO), moved, acc)


def unfold(acc, group):
    moved = pltpu.roll(acc, LANES - (2 * HALO * group + HALO), 1)
    return jnp.where(halo_lanes(acc.shape), moved, 0.0)


def pack_kernel(ens_hbm, out_ref, ens_ref, sem):
    blocks = out_ref.shape[0]
    columns = ens_ref.shape[2]
    fetch = pltpu.make_async_copy(ens_hbm, ens_ref, sem)
    fetch.start()
    fetch.wait()
    low = lax.broadcasted_iota(jnp.int32, (columns, LANES), 1) < LANES // 2
    zero = jnp.zeros((columns, LANES), f32)
    halos = [zero] * blocks
    for p in range(2):
        for f in range(3):
            k = p * 3 + f
            tiles = [ens_ref[p, f, :, b * LANES : (b + 1) * LANES] for b in range(blocks)]
            wide = [zero] + [t.astype(f32) for t in tiles] + [zero]
            for b in range(blocks):
                out_ref[b, k * columns : (k + 1) * columns, :] = tiles[b]
                halos[b] = fold(halos[b], jnp.where(low, wide[b + 2], wide[b]), k)
    for b in range(blocks):
        out_ref[b, 6 * columns : 7 * columns, :] = halos[b].astype(bf16)


def block_of(ref, b):
    return ref[:, pl.ds(pl.multiple_of(b * LANES, LANES), LANES)]


def widened(ref, b, blocks):
    main = block_of(ref, b)
    after = block_of(ref, jnp.minimum(b + 1, blocks - 1))
    before = block_of(ref, jnp.maximum(b - 1, 0))
    lane = lax.broadcasted_iota(jnp.int32, main.shape, 1)
    zero = jnp.zeros_like(main)
    after = jnp.where(b < blocks - 1, after, zero)
    before = jnp.where(b > 0, before, zero)
    return jnp.concatenate([main, jnp.where(lane < LANES // 2, after, before)], axis=1)


def pieces(x):
    first = x.astype(bf16).astype(f32)
    rest = x - first
    second = rest.astype(bf16).astype(f32)
    return first, second, rest - second


def static_kernel(depth_ref, mask_ref, fric_ref, obs_ref, cor_ref, own_ref, head_ref, turn_ref):
    blocks = depth_ref.shape[1] // LANES
    me = lax.axis_index("member")
    depth = widened(depth_ref, me, blocks)
    wet = jnp.where(widened(mask_ref, me, blocks) == 1, 1.0, 0.0).astype(f32)
    friction = widened(fric_ref, me, blocks)
    observed = widened(obs_ref, me, blocks)
    for k, value in enumerate((depth, wet, friction, observed)):
        own_ref[k] = value
    parts = [
        part for value in (depth, friction, observed) for part in pieces(value[:EXTRA, :])
    ]
    for k, part in enumerate(parts + [wet[:EXTRA, :]]):
        head_ref[EXTRA * k : EXTRA * (k + 1), :] = part
    turn_ref[...] = widened(cor_ref, me, blocks)


def index_kernel(copy_ref, spread_ref, split_ref, idx_ref, seen):
    for p in range(32):
        seen[p] = 0
    for s in range(32):
        seen[copy_ref[s]] = 1
    for i in range(DISTINCT):
        idx_ref[i] = 0
    count = jnp.int32(0)
    for p in range(32):
        used = seen[p]
        place = jnp.minimum(count, DISTINCT - 1)
        idx_ref[place] = jnp.where(used == 1, p, idx_ref[place])
        seen[p] = place
        count = count + used
    for s in range(32):
        idx_ref[DISTINCT + s] = seen[copy_ref[s]]
    spread = spread_ref[...]
    high = spread.astype(bf16)
    split_ref[0] = high
    split_ref[1] = (spread - high.astype(f32)).astype(bf16)


def select_kernel(idx_ref, all_ref, shead_ref, fields_ref, head_ref, rows):
    columns = fields_ref.shape[1] // 3
    part = 3 * columns
    for i in range(DISTINCT):
        particle = idx_ref[i]
        src, p = particle // 2, particle % 2
        main = all_ref[src, pl.ds(pl.multiple_of(p * part, 16), part), :]
        folded = all_ref[src, 2 * part : 2 * part + columns, :].astype(f32)
        fields_ref[i, :, :LANES] = main.astype(f32)
        for f in range(3):
            fields_ref[i, f * columns : (f + 1) * columns, LANES:] = jnp.where(
                p == 0, unfold(folded, f), unfold(folded, 3 + f)
            )
            at = (i * 3 + f) * EXTRA
            rows[at : at + EXTRA, :] = fields_ref[i, f * columns : f * columns + EXTRA, :]
    n = rows.shape[0]
    rows[DISTINCT * 3 * EXTRA : n, :] = shead_ref[...]
    head_ref[0:n, :] = rows[:, :LANES].astype(bf16)
    halos = jnp.zeros((16, LANES), f32)
    for g in range(n // 16):
        halos = fold(halos, rows[16 * g : 16 * g + 16, LANES:], g)
    head_ref[n : n + 16, :] = halos.astype(bf16)


def east(x):
    return 0.5 * (pltpu.roll(x, x.shape[0] - 1, 0) - pltpu.roll(x, 1, 0))


def north(x):
    return 0.5 * (pltpu.roll(x, x.shape[1] - 1, 1) - pltpu.roll(x, 1, 1))


def step_kernel(
    fields_ref, right_ref, own_ref, turn_ref, out_ref, work_ref, copies_ref, rrows,
):
    columns = own_ref.shape[1]
    keep = slice(SHIFT, SHIFT + columns)
    n = rrows.shape[0]
    rrows[:, :LANES] = right_ref[0:n, :].astype(f32)
    folded = right_ref[n : n + 16, :].astype(f32)
    for g in range(n // 16):
        rrows[16 * g : 16 * g + 16, LANES:] = unfold(folded, g)
    base = DISTINCT * 3 * EXTRA

    def beside(k):
        return rrows[base + EXTRA * k : base + EXTRA * (k + 1), :]

    def static(k, at):
        extra = (beside(at) + beside(at + 1)) + beside(at + 2)
        return jnp.concatenate([own_ref[k], extra], axis=0)

    depth = static(0, 0)
    friction = static(2, 3)
    obs = static(3, 6)
    wet = jnp.concatenate([own_ref[1], beside(9)], axis=0)
    damped = wet * (1.0 / (1.0 + time_step * friction))
    turning = turn_ref[...]
    for k, value in enumerate((wet, damped, obs)):
        work_ref[k] = value[keep, :]
    for i in range(DISTINCT):
        fields = []
        for f in range(3):
            at = (i * 3 + f) * EXTRA
            fields.append(
                jnp.concatenate(
                    [fields_ref[i, f * columns : (f + 1) * columns, :], rrows[at : at + EXTRA, :]],
                    axis=0,
                )
            )
        height, zonal, meridional = fields
        fresh = height - time_step * wet * (east(depth * zonal) + north(depth * meridional))
        zonal1 = damped * (zonal + time_step * (turning * meridional - east(fresh)))
        meridional1 = damped * (meridional - time_step * (turning * zonal + north(fresh)))
        change = -time_step * wet * (east(depth * zonal1) + north(depth * meridional1))
        zonal_part = damped * (zonal1 + time_step * (turning * meridional1))
        meridional_part = damped * (meridional1 - time_step * (turning * zonal1))
        innov = (obs - fresh)[keep, :LANES]
        sent = innov.astype(bf16)
        for d in range(copies_ref.shape[0]):
            copies_ref[d, i * columns : (i + 1) * columns, :] = sent
        out_ref[i, 0] = innov
        for k, value in enumerate((change, zonal_part, meridional_part)):
            out_ref[i, k + 1] = value[keep, :LANES]


def spread_dot(gathered_ref, spread_ref):
    blocks = gathered_ref.shape[0]
    lhs = jnp.concatenate([gathered_ref[b] for b in range(blocks)], axis=1)
    dims = (((1,), (1,)), ((), ()))
    return lax.dot_general(
        lhs, spread_ref[0], dims, preferred_element_type=f32
    ) + lax.dot_general(lhs, spread_ref[1], dims, preferred_element_type=f32)


def update_kernel(gathered_ref, spread_ref, all_ref, work_ref, innov_ref, copies_ref):
    columns = work_ref.shape[1]
    wet = work_ref[0, :, :LANES]
    spreaded = spread_dot(gathered_ref, spread_ref)
    for i in range(DISTINCT):
        innov = all_ref[i, 0]
        sp = spreaded[i * columns : (i + 1) * columns, :]
        new = innov - nudge_rate * wet * (innov + sp) - all_ref[i, 1]
        innov_ref[i] = new
        sent = new.astype(bf16)
        for d in range(copies_ref.shape[0]):
            copies_ref[d, i * columns : (i + 1) * columns, :] = sent


def final_kernel(
    gathered_ref, spread_ref, innov_ref, all_ref, work_ref,
    state_ref, tail_ref, edge_ref, sums_ref, *, total,
):
    columns = work_ref.shape[1]
    blocks = gathered_ref.shape[0]
    me = lax.axis_index("member")
    wet = work_ref[0, :, :LANES]
    damped = work_ref[1, :, :LANES]
    obs_tile = work_ref[2, :, LANES:]
    obs = work_ref[2, :, :LANES]
    before = jnp.maximum(me - 1, 0)
    after = jnp.minimum(me + 1, blocks - 1)
    has_before = jnp.where(me > 0, 1.0, 0.0).astype(f32)
    has_after = jnp.where(me < blocks - 1, 1.0, 0.0).astype(f32)
    lane = lax.broadcasted_iota(jnp.int32, (columns, LANES), 1)
    line = lax.broadcasted_iota(jnp.int32, (columns, LANES), 0)
    first = lax.axis_index("lon") * columns + SHIFT
    column = first + line
    column = jnp.where(column >= total, column - total, column).astype(f32)
    weight = wet * (1.0 + 2.0 * column / total)
    spreaded = spread_dot(gathered_ref, spread_ref)
    row = jnp.zeros((1, LANES), f32)
    for i in range(DISTINCT):
        part = slice(i * columns, (i + 1) * columns)
        innov = innov_ref[i]
        fresh = obs - innov
        height = fresh + nudge_rate * wet * (innov + spreaded[part, :])
        gap = obs - height
        row = jnp.where(lane[0:1] == i, jnp.sum(weight * (gap * gap)), row)
        near = gathered_ref[before, part, :].astype(f32)
        far = gathered_ref[after, part, :].astype(f32)
        fresh_before = has_before * (obs_tile - near)
        fresh_after = has_after * (obs_tile - far)
        down = jnp.where(lane == 0, pltpu.roll(fresh_before, 1, 1), pltpu.roll(fresh, 1, 1))
        up = jnp.where(
            lane == LANES - 1,
            pltpu.roll(fresh_after, LANES - 1, 1),
            pltpu.roll(fresh, LANES - 1, 1),
        )
        west = jnp.where(line == 0, 0.0, pltpu.roll(fresh, 1, 0))
        easterly = jnp.where(line == columns - 1, 0.0, pltpu.roll(fresh, columns - 1, 0))
        zonal = all_ref[i, 2] - damped * (time_step * 0.5 * (easterly - west))
        meridional = all_ref[i, 3] - damped * (time_step * 0.5 * (up - down))
        for f, value in enumerate((height, zonal, meridional)):
            state_ref[i, f * columns : (f + 1) * columns, :] = value
            at = (i * 3 + f) * SHIFT
            tail_ref[at : at + SHIFT, :] = value[columns - SHIFT :, :]
        at = DISTINCT * 3 * SHIFT + i
        tail_ref[at : at + 1, :] = fresh[columns - 1 :, :]
        edge_ref[i : i + 1, :] = fresh[0:1, :]
    for d in range(sums_ref.shape[0]):
        sums_ref[d] = row


LEVELS = (9, 5, 5)


def residue_level(value, rounded, levels):
    size = jnp.maximum(jnp.abs(rounded), 1e-30)
    at = (value - rounded) * 256.0 / size + 1.0
    return jnp.clip(jnp.floor(at * (0.5 * levels)), 0.0, levels - 1.0)


def restored(rounded, level, levels):
    step = 2.0 / (256.0 * levels)
    return rounded + jnp.abs(rounded) * (level * step + (0.5 * step - 1.0 / 256.0))


def slots_kernel(idx_ref, state_ref, tail_ref, edge_ref, own_ref, sums_ref, out_ref, moved, coded):
    columns = state_ref.shape[1] // 3
    at = slice(SHIFT - 1, SHIFT + 1)
    damped = own_ref[1, at, :LANES] * (1.0 / (1.0 + time_step * own_ref[2, at, :LANES]))
    side = damped * (time_step * 0.5)
    last = DISTINCT * 3 * SHIFT
    for i in range(DISTINCT):
        for f in range(3):
            k = i * 3 + f
            moved[i, f * columns : (f + 1) * columns, :] = jnp.concatenate(
                [
                    tail_ref[k * SHIFT : (k + 1) * SHIFT, :],
                    state_ref[i, f * columns : (f + 1) * columns - SHIFT, :],
                ],
                axis=0,
            )
        row = columns + SHIFT - 1
        moved[i, row : row + 1, :] = moved[i, row : row + 1, :] - side[0:1] * edge_ref[i : i + 1, :]
        moved[i, row + 1 : row + 2, :] = (
            moved[i, row + 1 : row + 2, :] + side[1:2] * tail_ref[last + i : last + i + 1, :]
        )
        code = jnp.zeros((columns, LANES), f32)
        for f in (2, 1, 0):
            value = moved[i, f * columns : (f + 1) * columns, :]
            sent = value.astype(bf16)
            coded[i, f * columns : (f + 1) * columns, :] = sent
            code = code * LEVELS[f] + residue_level(value, sent.astype(f32), LEVELS[f])
        coded[i, 3 * columns : 4 * columns, :] = code.astype(bf16)
    parts = jnp.concatenate(
        pieces(jnp.sum(sums_ref[...], axis=0)) + (jnp.zeros((13, LANES), f32),), axis=0
    ).astype(bf16)
    n = 4 * columns
    for d in range(out_ref.shape[0]):
        for p in range(2):
            out_ref[d, p * n : (p + 1) * n, :] = coded[idx_ref[DISTINCT + 2 * d + p]]
        out_ref[d, 2 * n : 2 * n + 16, :] = parts


def output_kernel(idx_ref, state_ref, out_ref, misfit_ref, *, cells):
    columns = out_ref.shape[2]
    blocks = state_ref.shape[0]
    n = 4 * columns
    me = lax.axis_index("member")
    for p in range(2):
        for b in range(blocks):
            part = slice(b * LANES, (b + 1) * LANES)
            block = state_ref[b, p * n : (p + 1) * n, :].astype(f32)
            code = block[3 * columns :]
            for f in range(3):
                rounded = block[f * columns : (f + 1) * columns]
                level = code
                if f < 2:
                    code = jnp.floor(code * (1.0 / LEVELS[f]) + 0.5 / LEVELS[f])
                    level = level - code * LEVELS[f]
                out_ref[p, f, :, part] = restored(rounded, level, LEVELS[f])
    row = jnp.zeros((1, LANES), f32)
    for b in range(blocks):
        parts = state_ref[b, 2 * n : 2 * n + 16, :].astype(f32)
        row = row + ((parts[0:1] + parts[1:2]) + parts[2:3])
    lane = lax.broadcasted_iota(jnp.int32, (1, LANES), 1)
    for p in range(2):
        place = idx_ref[DISTINCT + 2 * me + p]
        misfit_ref[p] = jnp.sum(jnp.where(lane == place, row, 0.0)) / cells


def per_device(ensemble, copy_list, depth, land_mask, friction, coriolis, spread, observed):
    columns, lat = depth.shape
    members = lax.axis_size("member")
    lons = lax.axis_size("lon")
    blocks = lat // LANES
    rows = DISTINCT * columns
    wide = 2 * LANES
    statics = 10 * EXTRA
    halo_rows = DISTINCT * 3 * EXTRA + statics
    shape = jax.ShapeDtypeStruct
    eastward = [(i, (i + 1) % lons) for i in range(lons)]
    westward = [((i + 1) % lons, i) for i in range(lons)]

    def swap(x):
        return lax.all_to_all(x, "member", 0, 0, tiled=True)

    packed = call(
        pack_kernel,
        shape((blocks, 7 * columns, LANES), bf16),
        [ANY],
        VMEM,
        [pltpu.VMEM(ensemble.shape, bf16), pltpu.SemaphoreType.DMA(())],
        limit=60,
    )(ensemble)
    packed = swap(packed)
    own, shead, turning = call(
        static_kernel,
        (shape((4, columns, wide), f32), shape((statics, wide), f32), shape((1, wide), f32)),
        [VMEM] * 5,
        (VMEM, VMEM, VMEM),
    )(depth, land_mask, friction, observed, coriolis[None, :])
    parts, idx = call(
        index_kernel,
        (shape((2,) + spread.shape, bf16), shape((64,), jnp.int32)),
        [SMEM, VMEM],
        (VMEM, SMEM),
        [pltpu.SMEM((32,), jnp.int32)],
    )(copy_list, spread)
    packed, own, turning, parts = lax.optimization_barrier((packed, own, turning, parts))
    fields, head = call(
        select_kernel,
        (
            shape((DISTINCT, 3 * columns, wide), f32),
            shape((halo_rows + 16, LANES), bf16),
        ),
        [SMEM, VMEM, VMEM],
        (VMEM, VMEM),
        [pltpu.VMEM((halo_rows, wide), f32)],
    )(idx, packed, shead)
    right = lax.ppermute(head, "lon", westward)
    step1, work, copies = call(
        step_kernel,
        (
            shape((DISTINCT, 4, columns, LANES), f32),
            shape((3, columns, wide), f32),
            shape((members, rows, LANES), bf16),
        ),
        [VMEM] * 4,
        (VMEM, VMEM, VMEM),
        [pltpu.VMEM((halo_rows, wide), f32)],
    )(fields, right, own, turning)
    gathered1 = swap(copies)
    innov2, copies = call(
        update_kernel,
        (
            shape((DISTINCT, columns, LANES), f32),
            shape((members, rows, LANES), bf16),
        ),
        [VMEM] * 4,
        (VMEM, VMEM),
        flops=2 * 2 * rows * LANES * lat,
    )(gathered1, parts, step1, work)
    gathered2 = swap(copies)
    state, tail, edge, sums = call(
        functools.partial(final_kernel, total=columns * lons),
        (
            shape((DISTINCT, 3 * columns, LANES), f32),
            shape((DISTINCT * (3 * SHIFT + 1), LANES), f32),
            shape((DISTINCT, LANES), f32),
            shape((lons, 1, LANES), f32),
        ),
        [VMEM] * 5,
        (VMEM,) * 4,
        flops=2 * 2 * rows * LANES * lat,
    )(gathered2, parts, innov2, step1, work)
    sums = lax.all_to_all(sums, "lon", 0, 0, tiled=True)
    tail = lax.ppermute(tail, "lon", eastward)
    state = call(
        slots_kernel,
        shape((members, 8 * columns + 16, LANES), bf16),
        [SMEM] + [VMEM] * 5,
        VMEM,
        [
            pltpu.VMEM((DISTINCT, 3 * columns, LANES), f32),
            pltpu.VMEM((DISTINCT, 4 * columns, LANES), bf16),
        ],
    )(idx, state, tail, edge, own, sums)
    state = swap(state)
    return call(
        functools.partial(output_kernel, cells=float(lat * columns * lons)),
        (shape((2, 3, columns, lat), f32), shape((2,), f32)),
        [SMEM, VMEM],
        (VMEM, SMEM),
    )(idx, state)


def solution(mesh):
    placed = (
        P("member", None, "lon", None),
        P(),
        P("lon", None),
        P("lon", None),
        P("lon", None),
        P(),
        P("member", None),
        P("lon", None),
    )
    return jax.shard_map(
        per_device,
        mesh=mesh,
        in_specs=placed,
        out_specs=(P("member", None, "lon", None), P("member")),
        check_vma=False,
    )
```

```python
import functools

import jax
import jax.numpy as jnp
from jax import lax
from jax.experimental import pallas as pl
from jax.experimental.pallas import tpu as pltpu
from jax.sharding import PartitionSpec as P

DISTINCT = 8
HALO = 3
EXTRA = 8
SHIFT = 4
LANES = 128
time_step = 0.2
nudge_rate = 0.3
f32 = jnp.float32
bf16 = jnp.bfloat16

VMEM = pl.BlockSpec(memory_space=pltpu.VMEM)
SMEM = pl.BlockSpec(memory_space=pltpu.SMEM)
ANY = pl.BlockSpec(memory_space=pl.ANY)


def call(kernel, out_shape, in_specs, out_specs, scratch=(), flops=1e6, bytes_accessed=1e6, limit=24):
    return pl.pallas_call(
        kernel,
        out_shape=out_shape,
        in_specs=in_specs,
        out_specs=out_specs,
        scratch_shapes=list(scratch),
        compiler_params=pltpu.CompilerParams(vmem_limit_bytes=limit * 1024 * 1024),
        cost_estimate=pl.CostEstimate(
            flops=int(flops), bytes_accessed=int(bytes_accessed), transcendentals=0
        ),
    )


def halo_lanes(shape):
    lane = lax.broadcasted_iota(jnp.int32, shape, 1)
    return (lane < HALO) | (lane >= LANES - HALO)


def fold(acc, tile, group):
    lane = lax.broadcasted_iota(jnp.int32, tile.shape, 1)
    at = 2 * HALO * group
    moved = pltpu.roll(tile, at + HALO, 1)
    return jnp.where((lane >= at) & (lane < at + 2 * HALO), moved, acc)


def unfold(acc, group):
    moved = pltpu.roll(acc, LANES - (2 * HALO * group + HALO), 1)
    return jnp.where(halo_lanes(acc.shape), moved, 0.0)


def pack_kernel(ens_hbm, out_ref, ens_ref, sem):
    blocks = out_ref.shape[0]
    columns = ens_ref.shape[2]
    fetch = pltpu.make_async_copy(ens_hbm, ens_ref, sem)
    fetch.start()
    fetch.wait()
    low = lax.broadcasted_iota(jnp.int32, (columns, LANES), 1) < LANES // 2
    zero = jnp.zeros((columns, LANES), f32)
    halos = [zero] * blocks
    for p in range(2):
        for f in range(3):
            k = p * 3 + f
            tiles = [ens_ref[p, f, :, b * LANES : (b + 1) * LANES] for b in range(blocks)]
            wide = [zero] + [t.astype(f32) for t in tiles] + [zero]
            for b in range(blocks):
                out_ref[b, k * columns : (k + 1) * columns, :] = tiles[b]
                halos[b] = fold(halos[b], jnp.where(low, wide[b + 2], wide[b]), k)
    for b in range(blocks):
        out_ref[b, 6 * columns : 7 * columns, :] = halos[b].astype(bf16)


def block_of(ref, b):
    return ref[:, pl.ds(pl.multiple_of(b * LANES, LANES), LANES)]


def widened(ref, b, blocks):
    main = block_of(ref, b)
    after = block_of(ref, jnp.minimum(b + 1, blocks - 1))
    before = block_of(ref, jnp.maximum(b - 1, 0))
    lane = lax.broadcasted_iota(jnp.int32, main.shape, 1)
    zero = jnp.zeros_like(main)
    after = jnp.where(b < blocks - 1, after, zero)
    before = jnp.where(b > 0, before, zero)
    return jnp.concatenate([main, jnp.where(lane < LANES // 2, after, before)], axis=1)


def pieces(x):
    first = x.astype(bf16).astype(f32)
    rest = x - first
    second = rest.astype(bf16).astype(f32)
    return first, second, rest - second


def static_kernel(depth_ref, mask_ref, fric_ref, obs_ref, cor_ref, own_ref, head_ref, turn_ref):
    blocks = depth_ref.shape[1] // LANES
    me = lax.axis_index("member")
    depth = widened(depth_ref, me, blocks)
    wet = jnp.where(widened(mask_ref, me, blocks) == 1, 1.0, 0.0).astype(f32)
    friction = widened(fric_ref, me, blocks)
    observed = widened(obs_ref, me, blocks)
    for k, value in enumerate((depth, wet, friction, observed)):
        own_ref[k] = value
    parts = [
        part for value in (depth, friction, observed) for part in pieces(value[:EXTRA, :])
    ]
    for k, part in enumerate(parts + [wet[:EXTRA, :]]):
        head_ref[EXTRA * k : EXTRA * (k + 1), :] = part
    turn_ref[...] = widened(cor_ref, me, blocks)


def index_kernel(copy_ref, spread_ref, split_ref, out_ref, idx_ref, seen):
    for p in range(32):
        seen[p] = 0
    for s in range(32):
        seen[copy_ref[s]] = 1
    for i in range(DISTINCT):
        idx_ref[i] = 0
    count = jnp.int32(0)
    for p in range(32):
        used = seen[p]
        place = jnp.minimum(count, DISTINCT - 1)
        idx_ref[place] = jnp.where(used == 1, p, idx_ref[place])
        seen[p] = place
        count = count + used
    for s in range(32):
        idx_ref[DISTINCT + s] = seen[copy_ref[s]]
    lane = lax.broadcasted_iota(jnp.int32, out_ref.shape, 1)
    values = jnp.zeros(out_ref.shape, jnp.int32)
    for k in range(DISTINCT + 32):
        values = jnp.where(lane == k, idx_ref[k], values)
    out_ref[...] = values
    spread = spread_ref[...]
    high = spread.astype(bf16)
    split_ref[0] = high
    split_ref[1] = (spread - high.astype(f32)).astype(bf16)


def particle_of(idx, all_ref, i, columns):
    part = 3 * columns
    particle = idx[0, i]
    src, p = particle // 2, particle % 2
    main = all_ref[src, pl.ds(pl.multiple_of(p * part, 16), part), :].astype(f32)
    folded = all_ref[src, 2 * part : 2 * part + columns, :].astype(f32)
    halos = [jnp.where(p == 0, unfold(folded, f), unfold(folded, 3 + f)) for f in range(3)]
    return main, halos


def head_kernel(idx_ref, all_ref, shead_ref, head_ref, rows):
    columns = all_ref.shape[1] // 7
    idx = idx_ref[0:1, :]
    for i in range(DISTINCT):
        main, halos = particle_of(idx, all_ref, i, columns)
        for f in range(3):
            at = (i * 3 + f) * EXTRA
            rows[at : at + EXTRA, :LANES] = main[f * columns : f * columns + EXTRA, :]
            rows[at : at + EXTRA, LANES:] = halos[f][:EXTRA, :]
    n = rows.shape[0]
    rows[DISTINCT * 3 * EXTRA : n, :] = shead_ref[...]
    head_ref[0:n, :] = rows[:, :LANES].astype(bf16)
    halos = jnp.zeros((16, LANES), f32)
    for g in range(n // 16):
        halos = fold(halos, rows[16 * g : 16 * g + 16, LANES:], g)
    head_ref[n : n + 16, :] = halos.astype(bf16)


def fields_kernel(idx_ref, all_ref, fields_ref):
    columns = fields_ref.shape[1] // 3
    idx = idx_ref[0:1, :]
    for i in range(DISTINCT):
        main, halos = particle_of(idx, all_ref, i, columns)
        fields_ref[i, :, :LANES] = main
        for f in range(3):
            fields_ref[i, f * columns : (f + 1) * columns, LANES:] = halos[f]


def east(x):
    return 0.5 * (pltpu.roll(x, x.shape[0] - 1, 0) - pltpu.roll(x, 1, 0))


def north(x):
    return 0.5 * (pltpu.roll(x, x.shape[1] - 1, 1) - pltpu.roll(x, 1, 1))


def step_kernel(
    fields_ref, right_ref, own_ref, turn_ref, out_ref, work_ref, copies_ref, rrows,
):
    columns = own_ref.shape[1]
    keep = slice(SHIFT, SHIFT + columns)
    n = rrows.shape[0]
    rrows[:, :LANES] = right_ref[0:n, :].astype(f32)
    folded = right_ref[n : n + 16, :].astype(f32)
    for g in range(n // 16):
        rrows[16 * g : 16 * g + 16, LANES:] = unfold(folded, g)
    base = DISTINCT * 3 * EXTRA

    def beside(k):
        return rrows[base + EXTRA * k : base + EXTRA * (k + 1), :]

    def static(k, at):
        extra = (beside(at) + beside(at + 1)) + beside(at + 2)
        return jnp.concatenate([own_ref[k], extra], axis=0)

    depth = static(0, 0)
    friction = static(2, 3)
    obs = static(3, 6)
    wet = jnp.concatenate([own_ref[1], beside(9)], axis=0)
    damped = wet * (1.0 / (1.0 + time_step * friction))
    turning = turn_ref[...]
    for k, value in enumerate((wet, damped, obs)):
        work_ref[k] = value[keep, :]
    for i in range(DISTINCT):
        fields = []
        for f in range(3):
            at = (i * 3 + f) * EXTRA
            fields.append(
                jnp.concatenate(
                    [fields_ref[i, f * columns : (f + 1) * columns, :], rrows[at : at + EXTRA, :]],
                    axis=0,
                )
            )
        height, zonal, meridional = fields
        fresh = height - time_step * wet * (east(depth * zonal) + north(depth * meridional))
        zonal1 = damped * (zonal + time_step * (turning * meridional - east(fresh)))
        meridional1 = damped * (meridional - time_step * (turning * zonal + north(fresh)))
        change = -time_step * wet * (east(depth * zonal1) + north(depth * meridional1))
        zonal_part = damped * (zonal1 + time_step * (turning * meridional1))
        meridional_part = damped * (meridional1 - time_step * (turning * zonal1))
        innov = (obs - fresh)[keep, :LANES]
        sent = innov.astype(bf16)
        for d in range(copies_ref.shape[0]):
            copies_ref[d, i * columns : (i + 1) * columns, :] = sent
        out_ref[i, 0] = innov
        for k, value in enumerate((change, zonal_part, meridional_part)):
            out_ref[i, k + 1] = value[keep, :LANES]


def spread_dot(gathered_ref, spread_ref):
    blocks = gathered_ref.shape[0]
    lhs = jnp.concatenate([gathered_ref[b] for b in range(blocks)], axis=1)
    dims = (((1,), (1,)), ((), ()))
    return lax.dot_general(
        lhs, spread_ref[0], dims, preferred_element_type=f32
    ) + lax.dot_general(lhs, spread_ref[1], dims, preferred_element_type=f32)


def update_kernel(gathered_ref, spread_ref, all_ref, work_ref, innov_ref, copies_ref):
    columns = work_ref.shape[1]
    wet = work_ref[0, :, :LANES]
    spreaded = spread_dot(gathered_ref, spread_ref)
    for i in range(DISTINCT):
        innov = all_ref[i, 0]
        sp = spreaded[i * columns : (i + 1) * columns, :]
        new = innov - nudge_rate * wet * (innov + sp) - all_ref[i, 1]
        innov_ref[i] = new
        sent = new.astype(bf16)
        for d in range(copies_ref.shape[0]):
            copies_ref[d, i * columns : (i + 1) * columns, :] = sent


def height_kernel(
    gathered_ref, spread_ref, innov_ref, work_ref, height_ref, sums_ref, shares, *, total
):
    columns = work_ref.shape[1]
    wet = work_ref[0, :, :LANES]
    obs = work_ref[2, :, :LANES]
    column = lax.axis_index("lon") * columns + SHIFT + lax.broadcasted_iota(
        jnp.int32, (columns, LANES), 0
    )
    column = jnp.where(column >= total, column - total, column).astype(f32)
    weight = wet * (1.0 + 2.0 * column / total)
    spreaded = spread_dot(gathered_ref, spread_ref)
    for i in range(DISTINCT):
        innov = innov_ref[i]
        sp = spreaded[i * columns : (i + 1) * columns, :]
        height = (obs - innov) + nudge_rate * wet * (innov + sp)
        height_ref[i] = height
        gap = obs - height
        shares[i : i + 1, :] = jnp.sum(weight * (gap * gap), axis=0, keepdims=True)
    total_of = jnp.broadcast_to(jnp.sum(shares[...], axis=1, keepdims=True), shares.shape)
    lane = lax.broadcasted_iota(jnp.int32, shares.shape, 1)
    line = lax.broadcasted_iota(jnp.int32, shares.shape, 0)
    row = jnp.sum(jnp.where(lane == line, total_of, 0.0), axis=0, keepdims=True)
    for d in range(sums_ref.shape[0]):
        sums_ref[d] = row


def velocity_kernel(
    gathered_ref, innov_ref, all_ref, work_ref, height_ref, state_ref, tail_ref, edge_ref
):
    columns = work_ref.shape[1]
    blocks = gathered_ref.shape[0]
    me = lax.axis_index("member")
    damped = work_ref[1, :, :LANES]
    obs = work_ref[2, :, :LANES]
    obs_tile = work_ref[2, :, LANES:]
    before = jnp.maximum(me - 1, 0)
    after = jnp.minimum(me + 1, blocks - 1)
    has_before = jnp.where(me > 0, 1.0, 0.0).astype(f32)
    has_after = jnp.where(me < blocks - 1, 1.0, 0.0).astype(f32)
    lane = lax.broadcasted_iota(jnp.int32, (columns, LANES), 1)
    line = lax.broadcasted_iota(jnp.int32, (columns, LANES), 0)
    for i in range(DISTINCT):
        part = slice(i * columns, (i + 1) * columns)
        fresh = obs - innov_ref[i]
        near = gathered_ref[before, part, :].astype(f32)
        far = gathered_ref[after, part, :].astype(f32)
        fresh_before = has_before * (obs_tile - near)
        fresh_after = has_after * (obs_tile - far)
        down = jnp.where(lane == 0, pltpu.roll(fresh_before, 1, 1), pltpu.roll(fresh, 1, 1))
        up = jnp.where(
            lane == LANES - 1,
            pltpu.roll(fresh_after, LANES - 1, 1),
            pltpu.roll(fresh, LANES - 1, 1),
        )
        west = jnp.where(line == 0, 0.0, pltpu.roll(fresh, 1, 0))
        easterly = jnp.where(line == columns - 1, 0.0, pltpu.roll(fresh, columns - 1, 0))
        zonal = all_ref[i, 2] - damped * (time_step * 0.5 * (easterly - west))
        meridional = all_ref[i, 3] - damped * (time_step * 0.5 * (up - down))
        for f, value in enumerate((height_ref[i], zonal, meridional)):
            state_ref[i, f * columns : (f + 1) * columns, :] = value
            at = (i * 3 + f) * SHIFT
            tail_ref[at : at + SHIFT, :] = value[columns - SHIFT :, :]
        at = DISTINCT * 3 * SHIFT + i
        tail_ref[at : at + 1, :] = fresh[columns - 1 :, :]
        edge_ref[i : i + 1, :] = fresh[0:1, :]


LEVELS = (9, 5, 5)


def residue_level(value, rounded, levels):
    size = jnp.maximum(jnp.abs(rounded), 1e-30)
    at = (value - rounded) * 256.0 / size + 1.0
    return jnp.clip(jnp.floor(at * (0.5 * levels)), 0.0, levels - 1.0)


def restored(rounded, level, levels):
    step = 2.0 / (256.0 * levels)
    return rounded + jnp.abs(rounded) * (level * step + (0.5 * step - 1.0 / 256.0))


def coding_kernel(state_ref, tail_ref, edge_ref, own_ref, coded_ref, moved):
    columns = state_ref.shape[1] // 3
    at = slice(SHIFT - 1, SHIFT + 1)
    damped = own_ref[1, at, :LANES] * (1.0 / (1.0 + time_step * own_ref[2, at, :LANES]))
    side = damped * (time_step * 0.5)
    last = DISTINCT * 3 * SHIFT
    for i in range(DISTINCT):
        for f in range(3):
            k = i * 3 + f
            moved[i, f * columns : (f + 1) * columns, :] = jnp.concatenate(
                [
                    tail_ref[k * SHIFT : (k + 1) * SHIFT, :],
                    state_ref[i, f * columns : (f + 1) * columns - SHIFT, :],
                ],
                axis=0,
            )
        row = columns + SHIFT - 1
        moved[i, row : row + 1, :] = moved[i, row : row + 1, :] - side[0:1] * edge_ref[i : i + 1, :]
        moved[i, row + 1 : row + 2, :] = (
            moved[i, row + 1 : row + 2, :] + side[1:2] * tail_ref[last + i : last + i + 1, :]
        )
        code = jnp.zeros((columns, LANES), f32)
        for f in (2, 1, 0):
            value = moved[i, f * columns : (f + 1) * columns, :]
            sent = value.astype(bf16)
            coded_ref[i, f * columns : (f + 1) * columns, :] = sent
            code = code * LEVELS[f] + residue_level(value, sent.astype(f32), LEVELS[f])
        coded_ref[i, 3 * columns : 4 * columns, :] = code.astype(bf16)


def slots_kernel(idx_ref, coded_ref, sums_ref, out_ref):
    parts = jnp.concatenate(
        pieces(jnp.sum(sums_ref[...], axis=0)) + (jnp.zeros((13, LANES), f32),), axis=0
    ).astype(bf16)
    n = coded_ref.shape[1]
    idx = idx_ref[0:1, :]
    for d in range(out_ref.shape[0]):
        for p in range(2):
            out_ref[d, p * n : (p + 1) * n, :] = coded_ref[idx[0, DISTINCT + 2 * d + p]]
        out_ref[d, 2 * n : 2 * n + 16, :] = parts


def output_kernel(idx_ref, state_ref, out_ref, misfit_ref, *, cells):
    columns = out_ref.shape[2]
    blocks = state_ref.shape[0]
    n = 4 * columns
    me = lax.axis_index("member")
    row = jnp.zeros((1, LANES), f32)
    for b in range(blocks):
        parts = state_ref[b, 2 * n : 2 * n + 16, :].astype(f32)
        row = row + ((parts[0:1] + parts[1:2]) + parts[2:3])
    lane = lax.broadcasted_iota(jnp.int32, (1, LANES), 1)
    idx = idx_ref[0:1, :]
    for p in range(2):
        place = jnp.sum(jnp.where(lane == DISTINCT + 2 * me + p, idx, 0))
        misfit_ref[p] = jnp.sum(jnp.where(lane == place, row, 0.0)) / cells
    for p in range(2):
        for b in range(blocks):
            part = slice(b * LANES, (b + 1) * LANES)
            block = state_ref[b, p * n : (p + 1) * n, :].astype(f32)
            code = block[3 * columns :]
            for f in range(3):
                rounded = block[f * columns : (f + 1) * columns]
                level = code
                if f < 2:
                    code = jnp.floor(code * (1.0 / LEVELS[f]) + 0.5 / LEVELS[f])
                    level = level - code * LEVELS[f]
                out_ref[p, f, :, part] = restored(rounded, level, LEVELS[f])


def per_device(ensemble, copy_list, depth, land_mask, friction, coriolis, spread, observed):
    columns, lat = depth.shape
    members = lax.axis_size("member")
    lons = lax.axis_size("lon")
    blocks = lat // LANES
    rows = DISTINCT * columns
    wide = 2 * LANES
    statics = 10 * EXTRA
    halo_rows = DISTINCT * 3 * EXTRA + statics
    shape = jax.ShapeDtypeStruct
    eastward = [(i, (i + 1) % lons) for i in range(lons)]
    westward = [((i + 1) % lons, i) for i in range(lons)]

    def swap(x):
        return lax.all_to_all(x, "member", 0, 0, tiled=True)

    packed = call(
        pack_kernel,
        shape((blocks, 7 * columns, LANES), bf16),
        [ANY],
        VMEM,
        [pltpu.VMEM(ensemble.shape, bf16), pltpu.SemaphoreType.DMA(())],
        limit=60,
    )(ensemble)
    packed = swap(packed)
    own, shead, turning = call(
        static_kernel,
        (shape((4, columns, wide), f32), shape((statics, wide), f32), shape((1, wide), f32)),
        [VMEM] * 5,
        (VMEM, VMEM, VMEM),
    )(depth, land_mask, friction, observed, coriolis[None, :])
    parts, idx = call(
        index_kernel,
        (shape((2,) + spread.shape, bf16), shape((8, LANES), jnp.int32)),
        [SMEM, VMEM],
        (VMEM, VMEM),
        [pltpu.SMEM((DISTINCT + 32,), jnp.int32), pltpu.SMEM((32,), jnp.int32)],
    )(copy_list, spread)
    packed, own, turning, parts = lax.optimization_barrier((packed, own, turning, parts))
    head = call(
        head_kernel,
        shape((halo_rows + 16, LANES), bf16),
        [VMEM] * 3,
        VMEM,
        [pltpu.VMEM((halo_rows, wide), f32)],
    )(idx, packed, shead)
    right = lax.ppermute(head, "lon", westward)
    packed, head = lax.optimization_barrier((packed, head))
    fields = call(
        fields_kernel, shape((DISTINCT, 3 * columns, wide), f32), [VMEM, VMEM], VMEM
    )(idx, packed)
    step1, work, copies = call(
        step_kernel,
        (
            shape((DISTINCT, 4, columns, LANES), f32),
            shape((3, columns, wide), f32),
            shape((members, rows, LANES), bf16),
        ),
        [VMEM] * 4,
        (VMEM, VMEM, VMEM),
        [pltpu.VMEM((halo_rows, wide), f32)],
    )(fields, right, own, turning)
    gathered1 = swap(copies)
    innov2, copies = call(
        update_kernel,
        (
            shape((DISTINCT, columns, LANES), f32),
            shape((members, rows, LANES), bf16),
        ),
        [VMEM] * 4,
        (VMEM, VMEM),
        flops=2 * 2 * rows * LANES * lat,
    )(gathered1, parts, step1, work)
    gathered2 = swap(copies)
    height, sums = call(
        functools.partial(height_kernel, total=columns * lons),
        (shape((DISTINCT, columns, LANES), f32), shape((lons, 1, LANES), f32)),
        [VMEM] * 4,
        (VMEM, VMEM),
        [pltpu.VMEM((DISTINCT, LANES), f32)],
        flops=2 * 2 * rows * LANES * lat,
    )(gathered2, parts, innov2, work)
    shared = lax.all_to_all(sums, "lon", 0, 0, tiled=True)
    height, sums = lax.optimization_barrier((height, sums))
    state, tail, edge = call(
        velocity_kernel,
        (
            shape((DISTINCT, 3 * columns, LANES), f32),
            shape((DISTINCT * (3 * SHIFT + 1), LANES), f32),
            shape((DISTINCT, LANES), f32),
        ),
        [VMEM] * 5,
        (VMEM,) * 3,
    )(gathered2, innov2, step1, work, height)
    tail = lax.ppermute(tail, "lon", eastward)
    coded = call(
        coding_kernel,
        shape((DISTINCT, 4 * columns, LANES), bf16),
        [VMEM] * 4,
        VMEM,
        [pltpu.VMEM((DISTINCT, 3 * columns, LANES), f32)],
    )(state, tail, edge, own)
    coded, shared = lax.optimization_barrier((coded, shared))
    state = call(
        slots_kernel,
        shape((members, 8 * columns + 16, LANES), bf16),
        [VMEM] * 3,
        VMEM,
    )(idx, coded, shared)
    state = swap(state)
    return call(
        functools.partial(output_kernel, cells=float(lat * columns * lons)),
        (shape((2, 3, columns, lat), f32), shape((2,), f32)),
        [VMEM, VMEM],
        (VMEM, SMEM),
    )(idx, state)


def solution(mesh):
    placed = (
        P("member", None, "lon", None),
        P(),
        P("lon", None),
        P("lon", None),
        P("lon", None),
        P(),
        P("member", None),
        P("lon", None),
    )
    return jax.shard_map(
        per_device,
        mesh=mesh,
        in_specs=placed,
        out_specs=(P("member", None, "lon", None), P("member")),
        check_vma=False,
    )
```

```python
import functools

import jax
import jax.numpy as jnp
from jax import lax
from jax.experimental import pallas as pl
from jax.experimental.pallas import tpu as pltpu
from jax.sharding import PartitionSpec as P

DISTINCT = 8
HALO = 3
EXTRA = 8
SHIFT = 4
LANES = 128
time_step = 0.2
nudge_rate = 0.3
f32 = jnp.float32
bf16 = jnp.bfloat16

VMEM = pl.BlockSpec(memory_space=pltpu.VMEM)
SMEM = pl.BlockSpec(memory_space=pltpu.SMEM)
ANY = pl.BlockSpec(memory_space=pl.ANY)


def call(kernel, out_shape, in_specs, out_specs, scratch=(), flops=1e6, bytes_accessed=1e6, limit=24):
    return pl.pallas_call(
        kernel,
        out_shape=out_shape,
        in_specs=in_specs,
        out_specs=out_specs,
        scratch_shapes=list(scratch),
        compiler_params=pltpu.CompilerParams(vmem_limit_bytes=limit * 1024 * 1024),
        cost_estimate=pl.CostEstimate(
            flops=int(flops), bytes_accessed=int(bytes_accessed), transcendentals=0
        ),
    )


def halo_lanes(shape):
    lane = lax.broadcasted_iota(jnp.int32, shape, 1)
    return (lane < HALO) | (lane >= LANES - HALO)


def fold(acc, tile, group):
    lane = lax.broadcasted_iota(jnp.int32, tile.shape, 1)
    at = 2 * HALO * group
    moved = pltpu.roll(tile, at + HALO, 1)
    return jnp.where((lane >= at) & (lane < at + 2 * HALO), moved, acc)


def unfold(acc, group):
    moved = pltpu.roll(acc, LANES - (2 * HALO * group + HALO), 1)
    return jnp.where(halo_lanes(acc.shape), moved, 0.0)


def pack_kernel(ens_hbm, out_ref, ens_ref, sem):
    blocks = out_ref.shape[0]
    columns = ens_ref.shape[2]
    fetch = pltpu.make_async_copy(ens_hbm, ens_ref, sem)
    fetch.start()
    fetch.wait()
    low = lax.broadcasted_iota(jnp.int32, (columns, LANES), 1) < LANES // 2
    zero = jnp.zeros((columns, LANES), f32)
    halos = [zero] * blocks
    for p in range(2):
        for f in range(3):
            k = p * 3 + f
            tiles = [ens_ref[p, f, :, b * LANES : (b + 1) * LANES] for b in range(blocks)]
            wide = [zero] + [t.astype(f32) for t in tiles] + [zero]
            for b in range(blocks):
                out_ref[b, k * columns : (k + 1) * columns, :] = tiles[b]
                halos[b] = fold(halos[b], jnp.where(low, wide[b + 2], wide[b]), k)
    for b in range(blocks):
        out_ref[b, 6 * columns : 7 * columns, :] = halos[b].astype(bf16)


def block_of(ref, b):
    return ref[:, pl.ds(pl.multiple_of(b * LANES, LANES), LANES)]


def widened(ref, b, blocks):
    main = block_of(ref, b)
    after = block_of(ref, jnp.minimum(b + 1, blocks - 1))
    before = block_of(ref, jnp.maximum(b - 1, 0))
    lane = lax.broadcasted_iota(jnp.int32, main.shape, 1)
    zero = jnp.zeros_like(main)
    after = jnp.where(b < blocks - 1, after, zero)
    before = jnp.where(b > 0, before, zero)
    return jnp.concatenate([main, jnp.where(lane < LANES // 2, after, before)], axis=1)


def pieces(x):
    first = x.astype(bf16).astype(f32)
    rest = x - first
    second = rest.astype(bf16).astype(f32)
    return first, second, rest - second


def static_kernel(depth_ref, mask_ref, fric_ref, obs_ref, cor_ref, own_ref, head_ref, turn_ref):
    blocks = depth_ref.shape[1] // LANES
    me = lax.axis_index("member")
    depth = widened(depth_ref, me, blocks)
    wet = jnp.where(widened(mask_ref, me, blocks) == 1, 1.0, 0.0).astype(f32)
    friction = widened(fric_ref, me, blocks)
    observed = widened(obs_ref, me, blocks)
    for k, value in enumerate((depth, wet, friction, observed)):
        own_ref[k] = value
    parts = [
        part for value in (depth, friction, observed) for part in pieces(value[:EXTRA, :])
    ]
    for k, part in enumerate(parts + [wet[:EXTRA, :]]):
        head_ref[EXTRA * k : EXTRA * (k + 1), :] = part
    turn_ref[...] = widened(cor_ref, me, blocks)


def index_kernel(copy_ref, spread_ref, split_ref, out_ref, idx_ref, seen):
    for p in range(32):
        seen[p] = 0
    for s in range(32):
        seen[copy_ref[s]] = 1
    for i in range(DISTINCT):
        idx_ref[i] = 0
    count = jnp.int32(0)
    for p in range(32):
        used = seen[p]
        place = jnp.minimum(count, DISTINCT - 1)
        idx_ref[place] = jnp.where(used == 1, p, idx_ref[place])
        seen[p] = place
        count = count + used
    for s in range(32):
        idx_ref[DISTINCT + s] = seen[copy_ref[s]]
    lane = lax.broadcasted_iota(jnp.int32, out_ref.shape, 1)
    values = jnp.zeros(out_ref.shape, jnp.int32)
    for k in range(DISTINCT + 32):
        values = jnp.where(lane == k, idx_ref[k], values)
    out_ref[...] = values
    spread = spread_ref[...]
    high = spread.astype(bf16)
    split_ref[0] = high
    split_ref[1] = (spread - high.astype(f32)).astype(bf16)


def particle_of(idx, all_ref, i, columns):
    part = 3 * columns
    particle = idx[0, i]
    src, p = particle // 2, particle % 2
    main = all_ref[src, pl.ds(pl.multiple_of(p * part, 16), part), :].astype(f32)
    folded = all_ref[src, 2 * part : 2 * part + columns, :].astype(f32)
    halos = [jnp.where(p == 0, unfold(folded, f), unfold(folded, 3 + f)) for f in range(3)]
    return main, halos


def head_kernel(idx_ref, all_ref, shead_ref, head_ref, rows):
    columns = all_ref.shape[1] // 7
    idx = idx_ref[0:1, :]
    for i in range(DISTINCT):
        main, halos = particle_of(idx, all_ref, i, columns)
        for f in range(3):
            at = (i * 3 + f) * EXTRA
            rows[at : at + EXTRA, :LANES] = main[f * columns : f * columns + EXTRA, :]
            rows[at : at + EXTRA, LANES:] = halos[f][:EXTRA, :]
    n = rows.shape[0]
    rows[DISTINCT * 3 * EXTRA : n, :] = shead_ref[...]
    head_ref[0:n, :] = rows[:, :LANES].astype(bf16)
    halos = jnp.zeros((16, LANES), f32)
    for g in range(n // 16):
        halos = fold(halos, rows[16 * g : 16 * g + 16, LANES:], g)
    head_ref[n : n + 16, :] = halos.astype(bf16)


def fields_kernel(idx_ref, all_ref, fields_ref):
    columns = fields_ref.shape[1] // 3
    idx = idx_ref[0:1, :]
    for i in range(DISTINCT):
        main, halos = particle_of(idx, all_ref, i, columns)
        fields_ref[i, :, :LANES] = main
        for f in range(3):
            fields_ref[i, f * columns : (f + 1) * columns, LANES:] = halos[f]


def east(x):
    return 0.5 * (pltpu.roll(x, x.shape[0] - 1, 0) - pltpu.roll(x, 1, 0))


def north(x):
    return 0.5 * (pltpu.roll(x, x.shape[1] - 1, 1) - pltpu.roll(x, 1, 1))


def step_kernel(
    fields_ref, right_ref, own_ref, turn_ref, out_ref, work_ref, copies_ref, rrows,
):
    columns = own_ref.shape[1]
    keep = slice(SHIFT, SHIFT + columns)
    n = rrows.shape[0]
    rrows[:, :LANES] = right_ref[0:n, :].astype(f32)
    folded = right_ref[n : n + 16, :].astype(f32)
    for g in range(n // 16):
        rrows[16 * g : 16 * g + 16, LANES:] = unfold(folded, g)
    base = DISTINCT * 3 * EXTRA

    def beside(k):
        return rrows[base + EXTRA * k : base + EXTRA * (k + 1), :]

    def static(k, at):
        extra = (beside(at) + beside(at + 1)) + beside(at + 2)
        return jnp.concatenate([own_ref[k], extra], axis=0)

    depth = static(0, 0)
    friction = static(2, 3)
    obs = static(3, 6)
    wet = jnp.concatenate([own_ref[1], beside(9)], axis=0)
    damped = wet * (1.0 / (1.0 + time_step * friction))
    turning = turn_ref[...]
    for k, value in enumerate((wet, damped, obs)):
        work_ref[k] = value[keep, :]
    for i in range(DISTINCT):
        fields = []
        for f in range(3):
            at = (i * 3 + f) * EXTRA
            fields.append(
                jnp.concatenate(
                    [fields_ref[i, f * columns : (f + 1) * columns, :], rrows[at : at + EXTRA, :]],
                    axis=0,
                )
            )
        height, zonal, meridional = fields
        fresh = height - time_step * wet * (east(depth * zonal) + north(depth * meridional))
        zonal1 = damped * (zonal + time_step * (turning * meridional - east(fresh)))
        meridional1 = damped * (meridional - time_step * (turning * zonal + north(fresh)))
        change = -time_step * wet * (east(depth * zonal1) + north(depth * meridional1))
        zonal_part = damped * (zonal1 + time_step * (turning * meridional1))
        meridional_part = damped * (meridional1 - time_step * (turning * zonal1))
        innov = (obs - fresh)[keep, :LANES]
        sent = innov.astype(bf16)
        for d in range(copies_ref.shape[0]):
            copies_ref[d, i * columns : (i + 1) * columns, :] = sent
        out_ref[i, 0] = innov
        for k, value in enumerate((change, zonal_part, meridional_part)):
            out_ref[i, k + 1] = value[keep, :LANES]


def spread_dot(gathered_ref, spread_ref):
    blocks = gathered_ref.shape[0]
    lhs = jnp.concatenate([gathered_ref[b] for b in range(blocks)], axis=1)
    dims = (((1,), (1,)), ((), ()))
    return lax.dot_general(
        lhs, spread_ref[0], dims, preferred_element_type=f32
    ) + lax.dot_general(lhs, spread_ref[1], dims, preferred_element_type=f32)


def update_kernel(gathered_ref, spread_ref, all_ref, work_ref, innov_ref, copies_ref):
    columns = work_ref.shape[1]
    wet = work_ref[0, :, :LANES]
    spreaded = spread_dot(gathered_ref, spread_ref)
    for i in range(DISTINCT):
        innov = all_ref[i, 0]
        sp = spreaded[i * columns : (i + 1) * columns, :]
        new = innov - nudge_rate * wet * (innov + sp) - all_ref[i, 1]
        innov_ref[i] = new
        sent = new.astype(bf16)
        for d in range(copies_ref.shape[0]):
            copies_ref[d, i * columns : (i + 1) * columns, :] = sent


def height_kernel(
    gathered_ref, spread_ref, innov_ref, work_ref, height_ref, sums_ref, shares, *, total
):
    columns = work_ref.shape[1]
    wet = work_ref[0, :, :LANES]
    obs = work_ref[2, :, :LANES]
    column = lax.axis_index("lon") * columns + SHIFT + lax.broadcasted_iota(
        jnp.int32, (columns, LANES), 0
    )
    column = jnp.where(column >= total, column - total, column).astype(f32)
    weight = wet * (1.0 + 2.0 * column / total)
    spreaded = spread_dot(gathered_ref, spread_ref)
    for i in range(DISTINCT):
        innov = innov_ref[i]
        sp = spreaded[i * columns : (i + 1) * columns, :]
        height = (obs - innov) + nudge_rate * wet * (innov + sp)
        height_ref[i] = height
        gap = obs - height
        shares[i : i + 1, :] = jnp.sum(weight * (gap * gap), axis=0, keepdims=True)
    total_of = jnp.broadcast_to(jnp.sum(shares[...], axis=1, keepdims=True), shares.shape)
    lane = lax.broadcasted_iota(jnp.int32, shares.shape, 1)
    line = lax.broadcasted_iota(jnp.int32, shares.shape, 0)
    row = jnp.sum(jnp.where(lane == line, total_of, 0.0), axis=0, keepdims=True)
    for d in range(sums_ref.shape[0]):
        sums_ref[d] = row


def velocity_kernel(
    gathered_ref, innov_ref, all_ref, work_ref, height_ref, state_ref, tail_ref, edge_ref
):
    columns = work_ref.shape[1]
    blocks = gathered_ref.shape[0]
    me = lax.axis_index("member")
    damped = work_ref[1, :, :LANES]
    obs = work_ref[2, :, :LANES]
    obs_tile = work_ref[2, :, LANES:]
    before = jnp.maximum(me - 1, 0)
    after = jnp.minimum(me + 1, blocks - 1)
    has_before = jnp.where(me > 0, 1.0, 0.0).astype(f32)
    has_after = jnp.where(me < blocks - 1, 1.0, 0.0).astype(f32)
    lane = lax.broadcasted_iota(jnp.int32, (columns, LANES), 1)
    line = lax.broadcasted_iota(jnp.int32, (columns, LANES), 0)
    for i in range(DISTINCT):
        part = slice(i * columns, (i + 1) * columns)
        fresh = obs - innov_ref[i]
        near = gathered_ref[before, part, :].astype(f32)
        far = gathered_ref[after, part, :].astype(f32)
        fresh_before = has_before * (obs_tile - near)
        fresh_after = has_after * (obs_tile - far)
        down = jnp.where(lane == 0, pltpu.roll(fresh_before, 1, 1), pltpu.roll(fresh, 1, 1))
        up = jnp.where(
            lane == LANES - 1,
            pltpu.roll(fresh_after, LANES - 1, 1),
            pltpu.roll(fresh, LANES - 1, 1),
        )
        west = jnp.where(line == 0, 0.0, pltpu.roll(fresh, 1, 0))
        easterly = jnp.where(line == columns - 1, 0.0, pltpu.roll(fresh, columns - 1, 0))
        zonal = all_ref[i, 2] - damped * (time_step * 0.5 * (easterly - west))
        meridional = all_ref[i, 3] - damped * (time_step * 0.5 * (up - down))
        for f, value in enumerate((height_ref[i], zonal, meridional)):
            state_ref[i, f * columns : (f + 1) * columns, :] = value
            at = (i * 3 + f) * SHIFT
            tail_ref[at : at + SHIFT, :] = value[columns - SHIFT :, :]
        at = DISTINCT * 3 * SHIFT + i
        tail_ref[at : at + 1, :] = fresh[columns - 1 :, :]
        edge_ref[i : i + 1, :] = fresh[0:1, :]


LEVELS = (9, 5, 5)


def residue_level(value, rounded, levels):
    size = jnp.maximum(jnp.abs(rounded), 1e-30)
    at = (value - rounded) * 256.0 / size + 1.0
    return jnp.clip(jnp.floor(at * (0.5 * levels)), 0.0, levels - 1.0)


def restored(rounded, level, levels):
    step = 2.0 / (256.0 * levels)
    return rounded + jnp.abs(rounded) * (level * step + (0.5 * step - 1.0 / 256.0))


def coding_kernel(state_ref, tail_ref, edge_ref, own_ref, coded_ref, moved):
    columns = state_ref.shape[1] // 3
    at = slice(SHIFT - 1, SHIFT + 1)
    damped = own_ref[1, at, :LANES] * (1.0 / (1.0 + time_step * own_ref[2, at, :LANES]))
    side = damped * (time_step * 0.5)
    last = DISTINCT * 3 * SHIFT
    for i in range(DISTINCT):
        for f in range(3):
            k = i * 3 + f
            moved[i, f * columns : (f + 1) * columns, :] = jnp.concatenate(
                [
                    tail_ref[k * SHIFT : (k + 1) * SHIFT, :],
                    state_ref[i, f * columns : (f + 1) * columns - SHIFT, :],
                ],
                axis=0,
            )
        row = columns + SHIFT - 1
        moved[i, row : row + 1, :] = moved[i, row : row + 1, :] - side[0:1] * edge_ref[i : i + 1, :]
        moved[i, row + 1 : row + 2, :] = (
            moved[i, row + 1 : row + 2, :] + side[1:2] * tail_ref[last + i : last + i + 1, :]
        )
        code = jnp.zeros((columns, LANES), f32)
        for f in (2, 1, 0):
            value = moved[i, f * columns : (f + 1) * columns, :]
            sent = value.astype(bf16)
            coded_ref[i, f * columns : (f + 1) * columns, :] = sent
            code = code * LEVELS[f] + residue_level(value, sent.astype(f32), LEVELS[f])
        coded_ref[i, 3 * columns : 4 * columns, :] = code.astype(bf16)


def slots_kernel(idx_ref, coded_ref, sums_ref, out_ref):
    parts = jnp.concatenate(
        pieces(jnp.sum(sums_ref[...], axis=0)) + (jnp.zeros((13, LANES), f32),), axis=0
    ).astype(bf16)
    n = coded_ref.shape[1]
    idx = idx_ref[0:1, :]
    for d in range(out_ref.shape[0]):
        for p in range(2):
            out_ref[d, p * n : (p + 1) * n, :] = coded_ref[idx[0, DISTINCT + 2 * d + p]]
        out_ref[d, 2 * n : 2 * n + 16, :] = parts


def output_kernel(idx_ref, state_ref, out_ref, misfit_ref, *, cells):
    columns = out_ref.shape[2]
    blocks = state_ref.shape[0]
    n = 4 * columns
    p = pl.program_id(0)
    place_lane = DISTINCT + 2 * lax.axis_index("member") + p
    row = jnp.zeros((1, LANES), f32)
    for b in range(blocks):
        parts = state_ref[b, 2 * n : 2 * n + 16, :].astype(f32)
        row = row + ((parts[0:1] + parts[1:2]) + parts[2:3])
        part = slice(b * LANES, (b + 1) * LANES)
        block = state_ref[b, pl.ds(pl.multiple_of(p * n, 16), n), :].astype(f32)
        code = block[3 * columns :]
        for f in range(3):
            rounded = block[f * columns : (f + 1) * columns]
            level = code
            if f < 2:
                code = jnp.floor(code * (1.0 / LEVELS[f]) + 0.5 / LEVELS[f])
                level = level - code * LEVELS[f]
            out_ref[0, f, :, part] = restored(rounded, level, LEVELS[f])
    lane = lax.broadcasted_iota(jnp.int32, (1, LANES), 1)
    place = jnp.sum(jnp.where(lane == place_lane, idx_ref[0:1, :], 0))
    misfit_ref[p] = jnp.sum(jnp.where(lane == place, row, 0.0)) / cells


def per_device(ensemble, copy_list, depth, land_mask, friction, coriolis, spread, observed):
    columns, lat = depth.shape
    members = lax.axis_size("member")
    lons = lax.axis_size("lon")
    blocks = lat // LANES
    rows = DISTINCT * columns
    wide = 2 * LANES
    statics = 10 * EXTRA
    halo_rows = DISTINCT * 3 * EXTRA + statics
    shape = jax.ShapeDtypeStruct
    eastward = [(i, (i + 1) % lons) for i in range(lons)]
    westward = [((i + 1) % lons, i) for i in range(lons)]

    def swap(x):
        return lax.all_to_all(x, "member", 0, 0, tiled=True)

    packed = call(
        pack_kernel,
        shape((blocks, 7 * columns, LANES), bf16),
        [ANY],
        VMEM,
        [pltpu.VMEM(ensemble.shape, bf16), pltpu.SemaphoreType.DMA(())],
        limit=60,
    )(ensemble)
    packed = swap(packed)
    own, shead, turning = call(
        static_kernel,
        (shape((4, columns, wide), f32), shape((statics, wide), f32), shape((1, wide), f32)),
        [VMEM] * 5,
        (VMEM, VMEM, VMEM),
    )(depth, land_mask, friction, observed, coriolis[None, :])
    parts, idx = call(
        index_kernel,
        (shape((2,) + spread.shape, bf16), shape((8, LANES), jnp.int32)),
        [SMEM, VMEM],
        (VMEM, VMEM),
        [pltpu.SMEM((DISTINCT + 32,), jnp.int32), pltpu.SMEM((32,), jnp.int32)],
    )(copy_list, spread)
    packed, own, turning, parts = lax.optimization_barrier((packed, own, turning, parts))
    head = call(
        head_kernel,
        shape((halo_rows + 16, LANES), bf16),
        [VMEM] * 3,
        VMEM,
        [pltpu.VMEM((halo_rows, wide), f32)],
    )(idx, packed, shead)
    right = lax.ppermute(head, "lon", westward)
    packed, head = lax.optimization_barrier((packed, head))
    fields = call(
        fields_kernel, shape((DISTINCT, 3 * columns, wide), f32), [VMEM, VMEM], VMEM
    )(idx, packed)
    step1, work, copies = call(
        step_kernel,
        (
            shape((DISTINCT, 4, columns, LANES), f32),
            shape((3, columns, wide), f32),
            shape((members, rows, LANES), bf16),
        ),
        [VMEM] * 4,
        (VMEM, VMEM, VMEM),
        [pltpu.VMEM((halo_rows, wide), f32)],
    )(fields, right, own, turning)
    gathered1 = swap(copies)
    innov2, copies = call(
        update_kernel,
        (
            shape((DISTINCT, columns, LANES), f32),
            shape((members, rows, LANES), bf16),
        ),
        [VMEM] * 4,
        (VMEM, VMEM),
        flops=2 * 2 * rows * LANES * lat,
    )(gathered1, parts, step1, work)
    gathered2 = swap(copies)
    height, sums = call(
        functools.partial(height_kernel, total=columns * lons),
        (shape((DISTINCT, columns, LANES), f32), shape((lons, 1, LANES), f32)),
        [VMEM] * 4,
        (VMEM, VMEM),
        [pltpu.VMEM((DISTINCT, LANES), f32)],
        flops=2 * 2 * rows * LANES * lat,
    )(gathered2, parts, innov2, work)
    shared = lax.all_to_all(sums, "lon", 0, 0, tiled=True)
    height, sums = lax.optimization_barrier((height, sums))
    state, tail, edge = call(
        velocity_kernel,
        (
            shape((DISTINCT, 3 * columns, LANES), f32),
            shape((DISTINCT * (3 * SHIFT + 1), LANES), f32),
            shape((DISTINCT, LANES), f32),
        ),
        [VMEM] * 5,
        (VMEM,) * 3,
    )(gathered2, innov2, step1, work, height)
    tail = lax.ppermute(tail, "lon", eastward)
    coded = call(
        coding_kernel,
        shape((DISTINCT, 4 * columns, LANES), bf16),
        [VMEM] * 4,
        VMEM,
        [pltpu.VMEM((DISTINCT, 3 * columns, LANES), f32)],
    )(state, tail, edge, own)
    coded, shared = lax.optimization_barrier((coded, shared))
    state = call(
        slots_kernel,
        shape((members, 8 * columns + 16, LANES), bf16),
        [VMEM] * 3,
        VMEM,
    )(idx, coded, shared)
    state = swap(state)
    return pl.pallas_call(
        functools.partial(output_kernel, cells=float(lat * columns * lons)),
        grid=(2,),
        out_shape=(shape((2, 3, columns, lat), f32), shape((2,), f32)),
        in_specs=[VMEM, VMEM],
        out_specs=(pl.BlockSpec((1, 3, columns, lat), lambda p: (p, 0, 0, 0)), SMEM),
        compiler_params=pltpu.CompilerParams(vmem_limit_bytes=24 * 1024 * 1024),
    )(idx, state)


def solution(mesh):
    placed = (
        P("member", None, "lon", None),
        P(),
        P("lon", None),
        P("lon", None),
        P("lon", None),
        P(),
        P("member", None),
        P("lon", None),
    )
    return jax.shard_map(
        per_device,
        mesh=mesh,
        in_specs=placed,
        out_specs=(P("member", None, "lon", None), P("member")),
        check_vma=False,
    )
```

```python
import functools

import jax
import jax.numpy as jnp
from jax import lax
from jax.experimental import pallas as pl
from jax.experimental.pallas import tpu as pltpu
from jax.sharding import PartitionSpec as P

DISTINCT = 8
HALO = 3
EXTRA = 8
SHIFT = 4
LANES = 128
time_step = 0.2
nudge_rate = 0.3
f32 = jnp.float32
bf16 = jnp.bfloat16

VMEM = pl.BlockSpec(memory_space=pltpu.VMEM)
SMEM = pl.BlockSpec(memory_space=pltpu.SMEM)
ANY = pl.BlockSpec(memory_space=pl.ANY)


def call(kernel, out_shape, in_specs, out_specs, scratch=(), flops=1e6, bytes_accessed=1e6, limit=24):
    return pl.pallas_call(
        kernel,
        out_shape=out_shape,
        in_specs=in_specs,
        out_specs=out_specs,
        scratch_shapes=list(scratch),
        compiler_params=pltpu.CompilerParams(vmem_limit_bytes=limit * 1024 * 1024),
        cost_estimate=pl.CostEstimate(
            flops=int(flops), bytes_accessed=int(bytes_accessed), transcendentals=0
        ),
    )


def halo_lanes(shape):
    lane = lax.broadcasted_iota(jnp.int32, shape, 1)
    return (lane < HALO) | (lane >= LANES - HALO)


def fold(acc, tile, group):
    lane = lax.broadcasted_iota(jnp.int32, tile.shape, 1)
    at = 2 * HALO * group
    moved = pltpu.roll(tile, at + HALO, 1)
    return jnp.where((lane >= at) & (lane < at + 2 * HALO), moved, acc)


def unfold(acc, group):
    moved = pltpu.roll(acc, LANES - (2 * HALO * group + HALO), 1)
    return jnp.where(halo_lanes(acc.shape), moved, 0.0)


def pack_kernel(ens_hbm, out_ref, ens_ref, sem):
    blocks = out_ref.shape[0]
    columns = ens_ref.shape[2]
    fetch = pltpu.make_async_copy(ens_hbm, ens_ref, sem)
    fetch.start()
    fetch.wait()
    low = lax.broadcasted_iota(jnp.int32, (columns, LANES), 1) < LANES // 2
    zero = jnp.zeros((columns, LANES), f32)
    halos = [zero] * blocks
    for p in range(2):
        for f in range(3):
            k = p * 3 + f
            tiles = [ens_ref[p, f, :, b * LANES : (b + 1) * LANES] for b in range(blocks)]
            wide = [zero] + [t.astype(f32) for t in tiles] + [zero]
            for b in range(blocks):
                out_ref[b, k * columns : (k + 1) * columns, :] = tiles[b]
                halos[b] = fold(halos[b], jnp.where(low, wide[b + 2], wide[b]), k)
    for b in range(blocks):
        out_ref[b, 6 * columns : 7 * columns, :] = halos[b].astype(bf16)


def block_of(ref, b):
    return ref[:, pl.ds(pl.multiple_of(b * LANES, LANES), LANES)]


def widened(ref, b, blocks):
    main = block_of(ref, b)
    after = block_of(ref, jnp.minimum(b + 1, blocks - 1))
    before = block_of(ref, jnp.maximum(b - 1, 0))
    lane = lax.broadcasted_iota(jnp.int32, main.shape, 1)
    zero = jnp.zeros_like(main)
    after = jnp.where(b < blocks - 1, after, zero)
    before = jnp.where(b > 0, before, zero)
    return jnp.concatenate([main, jnp.where(lane < LANES // 2, after, before)], axis=1)


def pieces(x):
    first = x.astype(bf16).astype(f32)
    rest = x - first
    second = rest.astype(bf16).astype(f32)
    return first, second, rest - second


def static_kernel(depth_ref, mask_ref, fric_ref, obs_ref, cor_ref, own_ref, head_ref, turn_ref):
    blocks = depth_ref.shape[1] // LANES
    me = lax.axis_index("member")
    depth = widened(depth_ref, me, blocks)
    wet = jnp.where(widened(mask_ref, me, blocks) == 1, 1.0, 0.0).astype(f32)
    friction = widened(fric_ref, me, blocks)
    observed = widened(obs_ref, me, blocks)
    for k, value in enumerate((depth, wet, friction, observed)):
        own_ref[k] = value
    parts = [
        part for value in (depth, friction, observed) for part in pieces(value[:EXTRA, :])
    ]
    for k, part in enumerate(parts + [wet[:EXTRA, :]]):
        head_ref[EXTRA * k : EXTRA * (k + 1), :] = part
    turn_ref[...] = widened(cor_ref, me, blocks)


def index_kernel(copy_ref, spread_ref, split_ref, out_ref, idx_ref, seen):
    for p in range(32):
        seen[p] = 0
    for s in range(32):
        seen[copy_ref[s]] = 1
    for i in range(DISTINCT):
        idx_ref[i] = 0
    count = jnp.int32(0)
    for p in range(32):
        used = seen[p]
        place = jnp.minimum(count, DISTINCT - 1)
        idx_ref[place] = jnp.where(used == 1, p, idx_ref[place])
        seen[p] = place
        count = count + used
    for s in range(32):
        idx_ref[DISTINCT + s] = seen[copy_ref[s]]
    lane = lax.broadcasted_iota(jnp.int32, out_ref.shape, 1)
    values = jnp.zeros(out_ref.shape, jnp.int32)
    for k in range(DISTINCT + 32):
        values = jnp.where(lane == k, idx_ref[k], values)
    out_ref[...] = values
    spread = spread_ref[...]
    high = spread.astype(bf16)
    split_ref[0] = high
    split_ref[1] = (spread - high.astype(f32)).astype(bf16)


def particle_of(idx, all_ref, i, columns):
    part = 3 * columns
    particle = idx[0, i]
    src, p = particle // 2, particle % 2
    main = all_ref[src, pl.ds(pl.multiple_of(p * part, 16), part), :].astype(f32)
    folded = all_ref[src, 2 * part : 2 * part + columns, :].astype(f32)
    halos = [jnp.where(p == 0, unfold(folded, f), unfold(folded, 3 + f)) for f in range(3)]
    return main, halos


def head_kernel(idx_ref, all_ref, shead_ref, head_ref, rows):
    columns = all_ref.shape[1] // 7
    idx = idx_ref[0:1, :]
    for i in range(DISTINCT):
        main, halos = particle_of(idx, all_ref, i, columns)
        for f in range(3):
            at = (i * 3 + f) * EXTRA
            rows[at : at + EXTRA, :LANES] = main[f * columns : f * columns + EXTRA, :]
            rows[at : at + EXTRA, LANES:] = halos[f][:EXTRA, :]
    n = rows.shape[0]
    rows[DISTINCT * 3 * EXTRA : n, :] = shead_ref[...]
    head_ref[0:n, :] = rows[:, :LANES].astype(bf16)
    halos = jnp.zeros((16, LANES), f32)
    for g in range(n // 16):
        halos = fold(halos, rows[16 * g : 16 * g + 16, LANES:], g)
    head_ref[n : n + 16, :] = halos.astype(bf16)


def fields_kernel(idx_ref, all_ref, fields_ref):
    columns = fields_ref.shape[1] // 3
    idx = idx_ref[0:1, :]
    for i in range(DISTINCT):
        main, halos = particle_of(idx, all_ref, i, columns)
        fields_ref[i, :, :LANES] = main
        for f in range(3):
            fields_ref[i, f * columns : (f + 1) * columns, LANES:] = halos[f]


def east(x):
    return 0.5 * (pltpu.roll(x, x.shape[0] - 1, 0) - pltpu.roll(x, 1, 0))


def north(x):
    return 0.5 * (pltpu.roll(x, x.shape[1] - 1, 1) - pltpu.roll(x, 1, 1))


LEVELS = (9, 5, 5)


def residue_level(value, rounded, levels):
    size = jnp.maximum(jnp.abs(rounded), 1e-30)
    at = (value - rounded) * 256.0 / size + 1.0
    return jnp.clip(jnp.floor(at * (0.5 * levels)), 0.0, levels - 1.0)


def restored(rounded, level, levels):
    step = 2.0 / (256.0 * levels)
    return rounded + jnp.abs(rounded) * (level * step + (0.5 * step - 1.0 / 256.0))


SIXTHS = 6.0


def send_rows(copies_ref, values):
    columns = values[0].shape[0]
    tiles, levels = [], []
    for value in values:
        sent = value.astype(bf16)
        tiles.append(sent)
        levels.append(residue_level(value, sent.astype(f32), SIXTHS))
    for k in range(0, len(values), 3):
        code = jnp.zeros_like(values[0])
        for level in reversed(levels[k : k + 3]):
            code = code * SIXTHS + level
        tiles.append(code.astype(bf16))
    for d in range(copies_ref.shape[0]):
        for k, tile in enumerate(tiles):
            copies_ref[d, k * columns : (k + 1) * columns, :] = tile


def step_kernel(
    fields_ref, right_ref, own_ref, turn_ref, out_ref, work_ref, copies_ref, rrows,
):
    columns = own_ref.shape[1]
    keep = slice(SHIFT, SHIFT + columns)
    n = rrows.shape[0]
    rrows[:, :LANES] = right_ref[0:n, :].astype(f32)
    folded = right_ref[n : n + 16, :].astype(f32)
    for g in range(n // 16):
        rrows[16 * g : 16 * g + 16, LANES:] = unfold(folded, g)
    base = DISTINCT * 3 * EXTRA

    def beside(k):
        return rrows[base + EXTRA * k : base + EXTRA * (k + 1), :]

    def static(k, at):
        extra = (beside(at) + beside(at + 1)) + beside(at + 2)
        return jnp.concatenate([own_ref[k], extra], axis=0)

    depth = static(0, 0)
    friction = static(2, 3)
    obs = static(3, 6)
    wet = jnp.concatenate([own_ref[1], beside(9)], axis=0)
    damped = wet * (1.0 / (1.0 + time_step * friction))
    turning = turn_ref[...]
    for k, value in enumerate((wet, damped, obs)):
        work_ref[k] = value[keep, :]
    values = []
    for i in range(DISTINCT):
        fields = []
        for f in range(3):
            at = (i * 3 + f) * EXTRA
            fields.append(
                jnp.concatenate(
                    [fields_ref[i, f * columns : (f + 1) * columns, :], rrows[at : at + EXTRA, :]],
                    axis=0,
                )
            )
        height, zonal, meridional = fields
        fresh = height - time_step * wet * (east(depth * zonal) + north(depth * meridional))
        zonal1 = damped * (zonal + time_step * (turning * meridional - east(fresh)))
        meridional1 = damped * (meridional - time_step * (turning * zonal + north(fresh)))
        change = -time_step * wet * (east(depth * zonal1) + north(depth * meridional1))
        zonal_part = damped * (zonal1 + time_step * (turning * meridional1))
        meridional_part = damped * (meridional1 - time_step * (turning * zonal1))
        innov = (obs - fresh)[keep, :LANES]
        values.append(innov)
        out_ref[i, 0] = innov
        for k, value in enumerate((change, zonal_part, meridional_part)):
            out_ref[i, k + 1] = value[keep, :LANES]
    send_rows(copies_ref, values)


def spread_dot(gathered_ref, spread_ref, columns):
    blocks = gathered_ref.shape[0]
    n = DISTINCT * columns
    lhs = jnp.concatenate([gathered_ref[b, 0:n, :] for b in range(blocks)], axis=1)
    codes = jnp.concatenate([gathered_ref[b, n:, :] for b in range(blocks)], axis=1).astype(f32)
    step = 2.0 / (256.0 * SIXTHS)
    rest = []
    for i in range(DISTINCT):
        if i % 3 == 0:
            code = codes[i // 3 * columns : (i // 3 + 1) * columns]
        above = jnp.floor(code * (1.0 / SIXTHS) + 0.5 / SIXTHS)
        size = jnp.abs(lhs[i * columns : (i + 1) * columns].astype(f32))
        level = code - above * SIXTHS
        rest.append((size * (level * step + (0.5 * step - 1.0 / 256.0))).astype(bf16))
        code = above
    rest = jnp.concatenate(rest, axis=0)
    dims = (((1,), (1,)), ((), ()))

    def dot(x, y):
        return lax.dot_general(x, y, dims, preferred_element_type=f32)

    return dot(lhs, spread_ref[0]) + (dot(lhs, spread_ref[1]) + dot(rest, spread_ref[0]))


def update_kernel(gathered_ref, spread_ref, all_ref, work_ref, innov_ref, copies_ref):
    columns = work_ref.shape[1]
    wet = work_ref[0, :, :LANES]
    spreaded = spread_dot(gathered_ref, spread_ref, columns)
    values = []
    for i in range(DISTINCT):
        innov = all_ref[i, 0]
        sp = spreaded[i * columns : (i + 1) * columns, :]
        new = innov - nudge_rate * wet * (innov + sp) - all_ref[i, 1]
        innov_ref[i] = new
        values.append(new)
    send_rows(copies_ref, values)


def height_kernel(
    gathered_ref, spread_ref, innov_ref, work_ref, height_ref, sums_ref, shares, *, total
):
    columns = work_ref.shape[1]
    wet = work_ref[0, :, :LANES]
    obs = work_ref[2, :, :LANES]
    column = lax.axis_index("lon") * columns + SHIFT + lax.broadcasted_iota(
        jnp.int32, (columns, LANES), 0
    )
    column = jnp.where(column >= total, column - total, column).astype(f32)
    weight = wet * (1.0 + 2.0 * column / total)
    spreaded = spread_dot(gathered_ref, spread_ref, columns)
    for i in range(DISTINCT):
        innov = innov_ref[i]
        sp = spreaded[i * columns : (i + 1) * columns, :]
        height = (obs - innov) + nudge_rate * wet * (innov + sp)
        height_ref[i] = height
        gap = obs - height
        shares[i : i + 1, :] = jnp.sum(weight * (gap * gap), axis=0, keepdims=True)
    total_of = jnp.broadcast_to(jnp.sum(shares[...], axis=1, keepdims=True), shares.shape)
    lane = lax.broadcasted_iota(jnp.int32, shares.shape, 1)
    line = lax.broadcasted_iota(jnp.int32, shares.shape, 0)
    row = jnp.sum(jnp.where(lane == line, total_of, 0.0), axis=0, keepdims=True)
    for d in range(sums_ref.shape[0]):
        sums_ref[d] = row


def velocity_kernel(
    gathered_ref, innov_ref, all_ref, work_ref, height_ref, state_ref, tail_ref, edge_ref
):
    columns = work_ref.shape[1]
    blocks = gathered_ref.shape[0]
    me = lax.axis_index("member")
    damped = work_ref[1, :, :LANES]
    obs = work_ref[2, :, :LANES]
    obs_tile = work_ref[2, :, LANES:]
    before = jnp.maximum(me - 1, 0)
    after = jnp.minimum(me + 1, blocks - 1)
    has_before = jnp.where(me > 0, 1.0, 0.0).astype(f32)
    has_after = jnp.where(me < blocks - 1, 1.0, 0.0).astype(f32)
    lane = lax.broadcasted_iota(jnp.int32, (columns, LANES), 1)
    line = lax.broadcasted_iota(jnp.int32, (columns, LANES), 0)
    for i in range(DISTINCT):
        part = slice(i * columns, (i + 1) * columns)
        fresh = obs - innov_ref[i]
        near = gathered_ref[before, part, :].astype(f32)
        far = gathered_ref[after, part, :].astype(f32)
        fresh_before = has_before * (obs_tile - near)
        fresh_after = has_after * (obs_tile - far)
        down = jnp.where(lane == 0, pltpu.roll(fresh_before, 1, 1), pltpu.roll(fresh, 1, 1))
        up = jnp.where(
            lane == LANES - 1,
            pltpu.roll(fresh_after, LANES - 1, 1),
            pltpu.roll(fresh, LANES - 1, 1),
        )
        west = jnp.where(line == 0, 0.0, pltpu.roll(fresh, 1, 0))
        easterly = jnp.where(line == columns - 1, 0.0, pltpu.roll(fresh, columns - 1, 0))
        zonal = all_ref[i, 2] - damped * (time_step * 0.5 * (easterly - west))
        meridional = all_ref[i, 3] - damped * (time_step * 0.5 * (up - down))
        for f, value in enumerate((height_ref[i], zonal, meridional)):
            state_ref[i, f * columns : (f + 1) * columns, :] = value
            at = (i * 3 + f) * SHIFT
            tail_ref[at : at + SHIFT, :] = value[columns - SHIFT :, :]
        at = DISTINCT * 3 * SHIFT + i
        tail_ref[at : at + 1, :] = fresh[columns - 1 :, :]
        edge_ref[i : i + 1, :] = fresh[0:1, :]


def coding_kernel(state_ref, tail_ref, edge_ref, own_ref, coded_ref, moved):
    columns = state_ref.shape[1] // 3
    at = slice(SHIFT - 1, SHIFT + 1)
    damped = own_ref[1, at, :LANES] * (1.0 / (1.0 + time_step * own_ref[2, at, :LANES]))
    side = damped * (time_step * 0.5)
    last = DISTINCT * 3 * SHIFT
    for i in range(DISTINCT):
        for f in range(3):
            k = i * 3 + f
            moved[i, f * columns : (f + 1) * columns, :] = jnp.concatenate(
                [
                    tail_ref[k * SHIFT : (k + 1) * SHIFT, :],
                    state_ref[i, f * columns : (f + 1) * columns - SHIFT, :],
                ],
                axis=0,
            )
        row = columns + SHIFT - 1
        moved[i, row : row + 1, :] = moved[i, row : row + 1, :] - side[0:1] * edge_ref[i : i + 1, :]
        moved[i, row + 1 : row + 2, :] = (
            moved[i, row + 1 : row + 2, :] + side[1:2] * tail_ref[last + i : last + i + 1, :]
        )
        code = jnp.zeros((columns, LANES), f32)
        for f in (2, 1, 0):
            value = moved[i, f * columns : (f + 1) * columns, :]
            sent = value.astype(bf16)
            coded_ref[i, f * columns : (f + 1) * columns, :] = sent
            code = code * LEVELS[f] + residue_level(value, sent.astype(f32), LEVELS[f])
        coded_ref[i, 3 * columns : 4 * columns, :] = code.astype(bf16)


def slots_kernel(idx_ref, coded_ref, sums_ref, out_ref):
    parts = jnp.concatenate(
        pieces(jnp.sum(sums_ref[...], axis=0)) + (jnp.zeros((13, LANES), f32),), axis=0
    ).astype(bf16)
    n = coded_ref.shape[1]
    idx = idx_ref[0:1, :]
    for d in range(out_ref.shape[0]):
        for p in range(2):
            out_ref[d, p * n : (p + 1) * n, :] = coded_ref[idx[0, DISTINCT + 2 * d + p]]
        out_ref[d, 2 * n : 2 * n + 16, :] = parts


def output_kernel(idx_ref, state_ref, out_ref, misfit_ref, *, cells):
    columns = out_ref.shape[2]
    blocks = state_ref.shape[0]
    n = 4 * columns
    p = pl.program_id(0)
    place_lane = DISTINCT + 2 * lax.axis_index("member") + p
    row = jnp.zeros((1, LANES), f32)
    for b in range(blocks):
        parts = state_ref[b, 2 * n : 2 * n + 16, :].astype(f32)
        row = row + ((parts[0:1] + parts[1:2]) + parts[2:3])
        part = slice(b * LANES, (b + 1) * LANES)
        block = state_ref[b, pl.ds(pl.multiple_of(p * n, 16), n), :].astype(f32)
        code = block[3 * columns :]
        for f in range(3):
            rounded = block[f * columns : (f + 1) * columns]
            level = code
            if f < 2:
                code = jnp.floor(code * (1.0 / LEVELS[f]) + 0.5 / LEVELS[f])
                level = level - code * LEVELS[f]
            out_ref[0, f, :, part] = restored(rounded, level, LEVELS[f])
    lane = lax.broadcasted_iota(jnp.int32, (1, LANES), 1)
    place = jnp.sum(jnp.where(lane == place_lane, idx_ref[0:1, :], 0))
    misfit_ref[p] = jnp.sum(jnp.where(lane == place, row, 0.0)) / cells


def per_device(ensemble, copy_list, depth, land_mask, friction, coriolis, spread, observed):
    columns, lat = depth.shape
    members = lax.axis_size("member")
    lons = lax.axis_size("lon")
    blocks = lat // LANES
    rows = DISTINCT * columns
    wide = 2 * LANES
    statics = 10 * EXTRA
    halo_rows = DISTINCT * 3 * EXTRA + statics
    shape = jax.ShapeDtypeStruct
    eastward = [(i, (i + 1) % lons) for i in range(lons)]
    westward = [((i + 1) % lons, i) for i in range(lons)]

    def swap(x):
        return lax.all_to_all(x, "member", 0, 0, tiled=True)

    packed = call(
        pack_kernel,
        shape((blocks, 7 * columns, LANES), bf16),
        [ANY],
        VMEM,
        [pltpu.VMEM(ensemble.shape, bf16), pltpu.SemaphoreType.DMA(())],
        limit=60,
    )(ensemble)
    packed = swap(packed)
    own, shead, turning = call(
        static_kernel,
        (shape((4, columns, wide), f32), shape((statics, wide), f32), shape((1, wide), f32)),
        [VMEM] * 5,
        (VMEM, VMEM, VMEM),
    )(depth, land_mask, friction, observed, coriolis[None, :])
    parts, idx = call(
        index_kernel,
        (shape((2,) + spread.shape, bf16), shape((8, LANES), jnp.int32)),
        [SMEM, VMEM],
        (VMEM, VMEM),
        [pltpu.SMEM((DISTINCT + 32,), jnp.int32), pltpu.SMEM((32,), jnp.int32)],
    )(copy_list, spread)
    packed, own, turning, parts = lax.optimization_barrier((packed, own, turning, parts))
    head = call(
        head_kernel,
        shape((halo_rows + 16, LANES), bf16),
        [VMEM] * 3,
        VMEM,
        [pltpu.VMEM((halo_rows, wide), f32)],
    )(idx, packed, shead)
    right = lax.ppermute(head, "lon", westward)
    packed, head = lax.optimization_barrier((packed, head))
    fields = call(
        fields_kernel, shape((DISTINCT, 3 * columns, wide), f32), [VMEM, VMEM], VMEM
    )(idx, packed)
    step1, work, copies = call(
        step_kernel,
        (
            shape((DISTINCT, 4, columns, LANES), f32),
            shape((3, columns, wide), f32),
            shape((members, rows + 3 * columns, LANES), bf16),
        ),
        [VMEM] * 4,
        (VMEM, VMEM, VMEM),
        [pltpu.VMEM((halo_rows, wide), f32)],
    )(fields, right, own, turning)
    gathered1 = swap(copies)
    innov2, copies = call(
        update_kernel,
        (
            shape((DISTINCT, columns, LANES), f32),
            shape((members, rows + 3 * columns, LANES), bf16),
        ),
        [VMEM] * 4,
        (VMEM, VMEM),
        flops=2 * 2 * rows * LANES * lat,
    )(gathered1, parts, step1, work)
    gathered2 = swap(copies)
    height, sums = call(
        functools.partial(height_kernel, total=columns * lons),
        (shape((DISTINCT, columns, LANES), f32), shape((lons, 1, LANES), f32)),
        [VMEM] * 4,
        (VMEM, VMEM),
        [pltpu.VMEM((DISTINCT, LANES), f32)],
        flops=2 * 2 * rows * LANES * lat,
    )(gathered2, parts, innov2, work)
    shared = lax.all_to_all(sums, "lon", 0, 0, tiled=True)
    height, sums = lax.optimization_barrier((height, sums))
    state, tail, edge = call(
        velocity_kernel,
        (
            shape((DISTINCT, 3 * columns, LANES), f32),
            shape((DISTINCT * (3 * SHIFT + 1), LANES), f32),
            shape((DISTINCT, LANES), f32),
        ),
        [VMEM] * 5,
        (VMEM,) * 3,
    )(gathered2, innov2, step1, work, height)
    tail = lax.ppermute(tail, "lon", eastward)
    coded = call(
        coding_kernel,
        shape((DISTINCT, 4 * columns, LANES), bf16),
        [VMEM] * 4,
        VMEM,
        [pltpu.VMEM((DISTINCT, 3 * columns, LANES), f32)],
    )(state, tail, edge, own)
    coded, shared = lax.optimization_barrier((coded, shared))
    state = call(
        slots_kernel,
        shape((members, 8 * columns + 16, LANES), bf16),
        [VMEM] * 3,
        VMEM,
    )(idx, coded, shared)
    state = swap(state)
    return pl.pallas_call(
        functools.partial(output_kernel, cells=float(lat * columns * lons)),
        grid=(2,),
        out_shape=(shape((2, 3, columns, lat), f32), shape((2,), f32)),
        in_specs=[VMEM, VMEM],
        out_specs=(pl.BlockSpec((1, 3, columns, lat), lambda p: (p, 0, 0, 0)), SMEM),
        compiler_params=pltpu.CompilerParams(vmem_limit_bytes=24 * 1024 * 1024),
    )(idx, state)


def solution(mesh):
    placed = (
        P("member", None, "lon", None),
        P(),
        P("lon", None),
        P("lon", None),
        P("lon", None),
        P(),
        P("member", None),
        P("lon", None),
    )
    return jax.shard_map(
        per_device,
        mesh=mesh,
        in_specs=placed,
        out_specs=(P("member", None, "lon", None), P("member")),
        check_vma=False,
    )
```

```python
import functools

import jax
import jax.numpy as jnp
from jax import lax
from jax.experimental import pallas as pl
from jax.experimental.pallas import tpu as pltpu
from jax.sharding import PartitionSpec as P

DISTINCT = 8
HALO = 3
EXTRA = 8
SHIFT = 4
LANES = 128
time_step = 0.2
nudge_rate = 0.3
f32 = jnp.float32
bf16 = jnp.bfloat16

VMEM = pl.BlockSpec(memory_space=pltpu.VMEM)
SMEM = pl.BlockSpec(memory_space=pltpu.SMEM)
ANY = pl.BlockSpec(memory_space=pl.ANY)


def call(kernel, out_shape, in_specs, out_specs, scratch=(), flops=1e6, bytes_accessed=1e6, limit=24):
    return pl.pallas_call(
        kernel,
        out_shape=out_shape,
        in_specs=in_specs,
        out_specs=out_specs,
        scratch_shapes=list(scratch),
        compiler_params=pltpu.CompilerParams(vmem_limit_bytes=limit * 1024 * 1024),
        cost_estimate=pl.CostEstimate(
            flops=int(flops), bytes_accessed=int(bytes_accessed), transcendentals=0
        ),
    )


def halo_lanes(shape):
    lane = lax.broadcasted_iota(jnp.int32, shape, 1)
    return (lane < HALO) | (lane >= LANES - HALO)


def fold(acc, tile, group):
    lane = lax.broadcasted_iota(jnp.int32, tile.shape, 1)
    at = 2 * HALO * group
    moved = pltpu.roll(tile, at + HALO, 1)
    return jnp.where((lane >= at) & (lane < at + 2 * HALO), moved, acc)


def unfold(acc, group):
    moved = pltpu.roll(acc, LANES - (2 * HALO * group + HALO), 1)
    return jnp.where(halo_lanes(acc.shape), moved, 0.0)


def pack_kernel(ens_hbm, out_ref, ens_ref, sem):
    blocks = out_ref.shape[0]
    columns = ens_ref.shape[2]
    fetch = pltpu.make_async_copy(ens_hbm, ens_ref, sem)
    fetch.start()
    fetch.wait()
    low = lax.broadcasted_iota(jnp.int32, (columns, LANES), 1) < LANES // 2
    zero = jnp.zeros((columns, LANES), f32)
    halos = [zero] * blocks
    for p in range(2):
        for f in range(3):
            k = p * 3 + f
            tiles = [ens_ref[p, f, :, b * LANES : (b + 1) * LANES] for b in range(blocks)]
            wide = [zero] + [t.astype(f32) for t in tiles] + [zero]
            for b in range(blocks):
                out_ref[b, k * columns : (k + 1) * columns, :] = tiles[b]
                halos[b] = fold(halos[b], jnp.where(low, wide[b + 2], wide[b]), k)
    for b in range(blocks):
        out_ref[b, 6 * columns : 7 * columns, :] = halos[b].astype(bf16)


def block_of(ref, b):
    return ref[:, pl.ds(pl.multiple_of(b * LANES, LANES), LANES)]


def widened(ref, b, blocks):
    main = block_of(ref, b)
    after = block_of(ref, jnp.minimum(b + 1, blocks - 1))
    before = block_of(ref, jnp.maximum(b - 1, 0))
    lane = lax.broadcasted_iota(jnp.int32, main.shape, 1)
    zero = jnp.zeros_like(main)
    after = jnp.where(b < blocks - 1, after, zero)
    before = jnp.where(b > 0, before, zero)
    return jnp.concatenate([main, jnp.where(lane < LANES // 2, after, before)], axis=1)


def pieces(x):
    first = x.astype(bf16).astype(f32)
    rest = x - first
    second = rest.astype(bf16).astype(f32)
    return first, second, rest - second


def static_kernel(depth_ref, mask_ref, fric_ref, obs_ref, cor_ref, own_ref, head_ref, turn_ref):
    blocks = depth_ref.shape[1] // LANES
    me = lax.axis_index("member")
    depth = widened(depth_ref, me, blocks)
    wet = jnp.where(widened(mask_ref, me, blocks) == 1, 1.0, 0.0).astype(f32)
    friction = widened(fric_ref, me, blocks)
    observed = widened(obs_ref, me, blocks)
    for k, value in enumerate((depth, wet, friction, observed)):
        own_ref[k] = value
    parts = [
        part for value in (depth, friction, observed) for part in pieces(value[:EXTRA, :])
    ]
    for k, part in enumerate(parts + [wet[:EXTRA, :]]):
        head_ref[EXTRA * k : EXTRA * (k + 1), :] = part
    turn_ref[...] = widened(cor_ref, me, blocks)


def index_kernel(copy_ref, spread_ref, split_ref, out_ref, idx_ref, seen):
    for p in range(32):
        seen[p] = 0
    for s in range(32):
        seen[copy_ref[s]] = 1
    for i in range(DISTINCT):
        idx_ref[i] = 0
    count = jnp.int32(0)
    for p in range(32):
        used = seen[p]
        place = jnp.minimum(count, DISTINCT - 1)
        idx_ref[place] = jnp.where(used == 1, p, idx_ref[place])
        seen[p] = place
        count = count + used
    for s in range(32):
        idx_ref[DISTINCT + s] = seen[copy_ref[s]]
    lane = lax.broadcasted_iota(jnp.int32, out_ref.shape, 1)
    values = jnp.zeros(out_ref.shape, jnp.int32)
    for k in range(DISTINCT + 32):
        values = jnp.where(lane == k, idx_ref[k], values)
    out_ref[...] = values
    spread = spread_ref[...]
    high = spread.astype(bf16)
    split_ref[0] = high
    split_ref[1] = (spread - high.astype(f32)).astype(bf16)


def particle_of(idx, all_ref, i, columns):
    part = 3 * columns
    particle = idx[0, i]
    src, p = particle // 2, particle % 2
    main = all_ref[src, pl.ds(pl.multiple_of(p * part, 16), part), :].astype(f32)
    folded = all_ref[src, 2 * part : 2 * part + columns, :].astype(f32)
    halos = [jnp.where(p == 0, unfold(folded, f), unfold(folded, 3 + f)) for f in range(3)]
    return main, halos


def head_kernel(idx_ref, all_ref, shead_ref, head_ref, rows):
    columns = all_ref.shape[1] // 7
    idx = idx_ref[0:1, :]
    for i in range(DISTINCT):
        main, halos = particle_of(idx, all_ref, i, columns)
        for f in range(3):
            at = (i * 3 + f) * EXTRA
            rows[at : at + EXTRA, :LANES] = main[f * columns : f * columns + EXTRA, :]
            rows[at : at + EXTRA, LANES:] = halos[f][:EXTRA, :]
    n = rows.shape[0]
    rows[DISTINCT * 3 * EXTRA : n, :] = shead_ref[...]
    head_ref[0:n, :] = rows[:, :LANES].astype(bf16)
    halos = jnp.zeros((16, LANES), f32)
    for g in range(n // 16):
        halos = fold(halos, rows[16 * g : 16 * g + 16, LANES:], g)
    head_ref[n : n + 16, :] = halos.astype(bf16)


def fields_kernel(idx_ref, all_ref, fields_ref):
    columns = fields_ref.shape[1] // 3
    idx = idx_ref[0:1, :]
    for i in range(DISTINCT):
        main, halos = particle_of(idx, all_ref, i, columns)
        fields_ref[i, :, :LANES] = main
        for f in range(3):
            fields_ref[i, f * columns : (f + 1) * columns, LANES:] = halos[f]


def east(x):
    return 0.5 * (pltpu.roll(x, x.shape[0] - 1, 0) - pltpu.roll(x, 1, 0))


def north(x):
    return 0.5 * (pltpu.roll(x, x.shape[1] - 1, 1) - pltpu.roll(x, 1, 1))


LEVELS = (9, 5, 5)


def residue_level(value, rounded, levels):
    size = jnp.maximum(jnp.abs(rounded), 1e-30)
    at = (value - rounded) * 256.0 / size + 1.0
    return jnp.clip(jnp.floor(at * (0.5 * levels)), 0.0, levels - 1.0)


def restored(rounded, level, levels):
    step = 2.0 / (256.0 * levels)
    return rounded + jnp.abs(rounded) * (level * step + (0.5 * step - 1.0 / 256.0))


STEPS_EACH = 4.0
SHARED = 4


def send_rows(copies_ref, values):
    columns = values[0].shape[0]
    tiles, levels = [], []
    for value in values:
        sent = value.astype(bf16)
        tiles.append(sent)
        levels.append(residue_level(value, sent.astype(f32), STEPS_EACH))
    for k in range(0, len(values), SHARED):
        code = jnp.zeros_like(values[0])
        for level in reversed(levels[k : k + SHARED]):
            code = code * STEPS_EACH + level
        tiles.append(code.astype(bf16))
    for d in range(copies_ref.shape[0]):
        for k, tile in enumerate(tiles):
            copies_ref[d, k * columns : (k + 1) * columns, :] = tile


def step_kernel(
    fields_ref, right_ref, own_ref, turn_ref, out_ref, work_ref, copies_ref, rrows,
):
    columns = own_ref.shape[1]
    keep = slice(SHIFT, SHIFT + columns)
    n = rrows.shape[0]
    rrows[:, :LANES] = right_ref[0:n, :].astype(f32)
    folded = right_ref[n : n + 16, :].astype(f32)
    for g in range(n // 16):
        rrows[16 * g : 16 * g + 16, LANES:] = unfold(folded, g)
    base = DISTINCT * 3 * EXTRA

    def beside(k):
        return rrows[base + EXTRA * k : base + EXTRA * (k + 1), :]

    def static(k, at):
        extra = (beside(at) + beside(at + 1)) + beside(at + 2)
        return jnp.concatenate([own_ref[k], extra], axis=0)

    depth = static(0, 0)
    friction = static(2, 3)
    obs = static(3, 6)
    wet = jnp.concatenate([own_ref[1], beside(9)], axis=0)
    damped = wet * (1.0 / (1.0 + time_step * friction))
    turning = turn_ref[...]
    for k, value in enumerate((wet, damped, obs)):
        work_ref[k] = value[keep, :]
    values = []
    for i in range(DISTINCT):
        fields = []
        for f in range(3):
            at = (i * 3 + f) * EXTRA
            fields.append(
                jnp.concatenate(
                    [fields_ref[i, f * columns : (f + 1) * columns, :], rrows[at : at + EXTRA, :]],
                    axis=0,
                )
            )
        height, zonal, meridional = fields
        fresh = height - time_step * wet * (east(depth * zonal) + north(depth * meridional))
        zonal1 = damped * (zonal + time_step * (turning * meridional - east(fresh)))
        meridional1 = damped * (meridional - time_step * (turning * zonal + north(fresh)))
        change = -time_step * wet * (east(depth * zonal1) + north(depth * meridional1))
        zonal_part = damped * (zonal1 + time_step * (turning * meridional1))
        meridional_part = damped * (meridional1 - time_step * (turning * zonal1))
        innov = (obs - fresh)[keep, :LANES]
        values.append(innov)
        out_ref[i, 0] = innov
        for k, value in enumerate((change, zonal_part, meridional_part)):
            out_ref[i, k + 1] = value[keep, :LANES]
    send_rows(copies_ref, values)


def spread_dot(gathered_ref, spread_ref, columns):
    blocks = gathered_ref.shape[0]
    n = DISTINCT * columns
    lhs = jnp.concatenate([gathered_ref[b, 0:n, :] for b in range(blocks)], axis=1)
    codes = jnp.concatenate([gathered_ref[b, n:, :] for b in range(blocks)], axis=1).astype(f32)
    step = 2.0 / (256.0 * STEPS_EACH)
    rest = []
    for i in range(DISTINCT):
        if i % SHARED == 0:
            code = codes[i // SHARED * columns : (i // SHARED + 1) * columns]
        above = jnp.floor(code * (1.0 / STEPS_EACH) + 0.5 / STEPS_EACH)
        size = jnp.abs(lhs[i * columns : (i + 1) * columns].astype(f32))
        level = code - above * STEPS_EACH
        rest.append((size * (level * step + (0.5 * step - 1.0 / 256.0))).astype(bf16))
        code = above
    rest = jnp.concatenate(rest, axis=0)
    dims = (((1,), (1,)), ((), ()))

    def dot(x, y):
        return lax.dot_general(x, y, dims, preferred_element_type=f32)

    return dot(lhs, spread_ref[0]) + (dot(lhs, spread_ref[1]) + dot(rest, spread_ref[0]))


def update_kernel(gathered_ref, spread_ref, all_ref, work_ref, innov_ref, copies_ref):
    columns = work_ref.shape[1]
    wet = work_ref[0, :, :LANES]
    spreaded = spread_dot(gathered_ref, spread_ref, columns)
    values = []
    for i in range(DISTINCT):
        innov = all_ref[i, 0]
        sp = spreaded[i * columns : (i + 1) * columns, :]
        new = innov - nudge_rate * wet * (innov + sp) - all_ref[i, 1]
        innov_ref[i] = new
        values.append(new)
    send_rows(copies_ref, values)


def height_kernel(
    gathered_ref, spread_ref, innov_ref, work_ref, height_ref, sums_ref, shares, *, total
):
    columns = work_ref.shape[1]
    wet = work_ref[0, :, :LANES]
    obs = work_ref[2, :, :LANES]
    column = lax.axis_index("lon") * columns + SHIFT + lax.broadcasted_iota(
        jnp.int32, (columns, LANES), 0
    )
    column = jnp.where(column >= total, column - total, column).astype(f32)
    weight = wet * (1.0 + 2.0 * column / total)
    spreaded = spread_dot(gathered_ref, spread_ref, columns)
    for i in range(DISTINCT):
        innov = innov_ref[i]
        sp = spreaded[i * columns : (i + 1) * columns, :]
        height = (obs - innov) + nudge_rate * wet * (innov + sp)
        height_ref[i] = height
        gap = obs - height
        shares[i : i + 1, :] = jnp.sum(weight * (gap * gap), axis=0, keepdims=True)
    total_of = jnp.broadcast_to(jnp.sum(shares[...], axis=1, keepdims=True), shares.shape)
    lane = lax.broadcasted_iota(jnp.int32, shares.shape, 1)
    line = lax.broadcasted_iota(jnp.int32, shares.shape, 0)
    row = jnp.sum(jnp.where(lane == line, total_of, 0.0), axis=0, keepdims=True)
    for d in range(sums_ref.shape[0]):
        sums_ref[d] = row


def velocity_kernel(
    gathered_ref, innov_ref, all_ref, work_ref, height_ref, state_ref, tail_ref, edge_ref
):
    columns = work_ref.shape[1]
    blocks = gathered_ref.shape[0]
    me = lax.axis_index("member")
    damped = work_ref[1, :, :LANES]
    obs = work_ref[2, :, :LANES]
    obs_tile = work_ref[2, :, LANES:]
    before = jnp.maximum(me - 1, 0)
    after = jnp.minimum(me + 1, blocks - 1)
    has_before = jnp.where(me > 0, 1.0, 0.0).astype(f32)
    has_after = jnp.where(me < blocks - 1, 1.0, 0.0).astype(f32)
    lane = lax.broadcasted_iota(jnp.int32, (columns, LANES), 1)
    line = lax.broadcasted_iota(jnp.int32, (columns, LANES), 0)
    for i in range(DISTINCT):
        part = slice(i * columns, (i + 1) * columns)
        fresh = obs - innov_ref[i]
        near = gathered_ref[before, part, :].astype(f32)
        far = gathered_ref[after, part, :].astype(f32)
        fresh_before = has_before * (obs_tile - near)
        fresh_after = has_after * (obs_tile - far)
        down = jnp.where(lane == 0, pltpu.roll(fresh_before, 1, 1), pltpu.roll(fresh, 1, 1))
        up = jnp.where(
            lane == LANES - 1,
            pltpu.roll(fresh_after, LANES - 1, 1),
            pltpu.roll(fresh, LANES - 1, 1),
        )
        west = jnp.where(line == 0, 0.0, pltpu.roll(fresh, 1, 0))
        easterly = jnp.where(line == columns - 1, 0.0, pltpu.roll(fresh, columns - 1, 0))
        zonal = all_ref[i, 2] - damped * (time_step * 0.5 * (easterly - west))
        meridional = all_ref[i, 3] - damped * (time_step * 0.5 * (up - down))
        for f, value in enumerate((height_ref[i], zonal, meridional)):
            state_ref[i, f * columns : (f + 1) * columns, :] = value
            at = (i * 3 + f) * SHIFT
            tail_ref[at : at + SHIFT, :] = value[columns - SHIFT :, :]
        at = DISTINCT * 3 * SHIFT + i
        tail_ref[at : at + 1, :] = fresh[columns - 1 :, :]
        edge_ref[i : i + 1, :] = fresh[0:1, :]


def coding_kernel(state_ref, tail_ref, edge_ref, own_ref, coded_ref, moved):
    columns = state_ref.shape[1] // 3
    at = slice(SHIFT - 1, SHIFT + 1)
    damped = own_ref[1, at, :LANES] * (1.0 / (1.0 + time_step * own_ref[2, at, :LANES]))
    side = damped * (time_step * 0.5)
    last = DISTINCT * 3 * SHIFT
    for i in range(DISTINCT):
        for f in range(3):
            k = i * 3 + f
            moved[i, f * columns : (f + 1) * columns, :] = jnp.concatenate(
                [
                    tail_ref[k * SHIFT : (k + 1) * SHIFT, :],
                    state_ref[i, f * columns : (f + 1) * columns - SHIFT, :],
                ],
                axis=0,
            )
        row = columns + SHIFT - 1
        moved[i, row : row + 1, :] = moved[i, row : row + 1, :] - side[0:1] * edge_ref[i : i + 1, :]
        moved[i, row + 1 : row + 2, :] = (
            moved[i, row + 1 : row + 2, :] + side[1:2] * tail_ref[last + i : last + i + 1, :]
        )
        code = jnp.zeros((columns, LANES), f32)
        for f in (2, 1, 0):
            value = moved[i, f * columns : (f + 1) * columns, :]
            sent = value.astype(bf16)
            coded_ref[i, f * columns : (f + 1) * columns, :] = sent
            code = code * LEVELS[f] + residue_level(value, sent.astype(f32), LEVELS[f])
        coded_ref[i, 3 * columns : 4 * columns, :] = code.astype(bf16)


def slots_kernel(idx_ref, coded_ref, sums_ref, out_ref):
    parts = jnp.concatenate(
        pieces(jnp.sum(sums_ref[...], axis=0)) + (jnp.zeros((13, LANES), f32),), axis=0
    ).astype(bf16)
    n = coded_ref.shape[1]
    idx = idx_ref[0:1, :]
    for d in range(out_ref.shape[0]):
        for p in range(2):
            out_ref[d, p * n : (p + 1) * n, :] = coded_ref[idx[0, DISTINCT + 2 * d + p]]
        out_ref[d, 2 * n : 2 * n + 16, :] = parts


def output_kernel(idx_ref, state_ref, out_ref, misfit_ref, *, cells):
    columns = out_ref.shape[2]
    blocks = state_ref.shape[0]
    n = 4 * columns
    p = pl.program_id(0)
    place_lane = DISTINCT + 2 * lax.axis_index("member") + p
    row = jnp.zeros((1, LANES), f32)
    for b in range(blocks):
        parts = state_ref[b, 2 * n : 2 * n + 16, :].astype(f32)
        row = row + ((parts[0:1] + parts[1:2]) + parts[2:3])
        part = slice(b * LANES, (b + 1) * LANES)
        block = state_ref[b, pl.ds(pl.multiple_of(p * n, 16), n), :].astype(f32)
        code = block[3 * columns :]
        for f in range(3):
            rounded = block[f * columns : (f + 1) * columns]
            level = code
            if f < 2:
                code = jnp.floor(code * (1.0 / LEVELS[f]) + 0.5 / LEVELS[f])
                level = level - code * LEVELS[f]
            out_ref[0, f, :, part] = restored(rounded, level, LEVELS[f])
    lane = lax.broadcasted_iota(jnp.int32, (1, LANES), 1)
    place = jnp.sum(jnp.where(lane == place_lane, idx_ref[0:1, :], 0))
    misfit_ref[p] = jnp.sum(jnp.where(lane == place, row, 0.0)) / cells


def per_device(ensemble, copy_list, depth, land_mask, friction, coriolis, spread, observed):
    columns, lat = depth.shape
    members = lax.axis_size("member")
    lons = lax.axis_size("lon")
    blocks = lat // LANES
    rows = DISTINCT * columns
    wide = 2 * LANES
    statics = 10 * EXTRA
    halo_rows = DISTINCT * 3 * EXTRA + statics
    shape = jax.ShapeDtypeStruct
    eastward = [(i, (i + 1) % lons) for i in range(lons)]
    westward = [((i + 1) % lons, i) for i in range(lons)]

    def swap(x):
        return lax.all_to_all(x, "member", 0, 0, tiled=True)

    packed = call(
        pack_kernel,
        shape((blocks, 7 * columns, LANES), bf16),
        [ANY],
        VMEM,
        [pltpu.VMEM(ensemble.shape, bf16), pltpu.SemaphoreType.DMA(())],
        limit=60,
    )(ensemble)
    packed = swap(packed)
    own, shead, turning = call(
        static_kernel,
        (shape((4, columns, wide), f32), shape((statics, wide), f32), shape((1, wide), f32)),
        [VMEM] * 5,
        (VMEM, VMEM, VMEM),
    )(depth, land_mask, friction, observed, coriolis[None, :])
    parts, idx = call(
        index_kernel,
        (shape((2,) + spread.shape, bf16), shape((8, LANES), jnp.int32)),
        [SMEM, VMEM],
        (VMEM, VMEM),
        [pltpu.SMEM((DISTINCT + 32,), jnp.int32), pltpu.SMEM((32,), jnp.int32)],
    )(copy_list, spread)
    packed, own, turning, parts = lax.optimization_barrier((packed, own, turning, parts))
    head = call(
        head_kernel,
        shape((halo_rows + 16, LANES), bf16),
        [VMEM] * 3,
        VMEM,
        [pltpu.VMEM((halo_rows, wide), f32)],
    )(idx, packed, shead)
    right = lax.ppermute(head, "lon", westward)
    packed, head = lax.optimization_barrier((packed, head))
    fields = call(
        fields_kernel, shape((DISTINCT, 3 * columns, wide), f32), [VMEM, VMEM], VMEM
    )(idx, packed)
    step1, work, copies = call(
        step_kernel,
        (
            shape((DISTINCT, 4, columns, LANES), f32),
            shape((3, columns, wide), f32),
            shape((members, rows + DISTINCT // SHARED * columns, LANES), bf16),
        ),
        [VMEM] * 4,
        (VMEM, VMEM, VMEM),
        [pltpu.VMEM((halo_rows, wide), f32)],
    )(fields, right, own, turning)
    gathered1 = swap(copies)
    innov2, copies = call(
        update_kernel,
        (
            shape((DISTINCT, columns, LANES), f32),
            shape((members, rows + DISTINCT // SHARED * columns, LANES), bf16),
        ),
        [VMEM] * 4,
        (VMEM, VMEM),
        flops=2 * 2 * rows * LANES * lat,
    )(gathered1, parts, step1, work)
    gathered2 = swap(copies)
    height, sums = call(
        functools.partial(height_kernel, total=columns * lons),
        (shape((DISTINCT, columns, LANES), f32), shape((lons, 1, LANES), f32)),
        [VMEM] * 4,
        (VMEM, VMEM),
        [pltpu.VMEM((DISTINCT, LANES), f32)],
        flops=2 * 2 * rows * LANES * lat,
    )(gathered2, parts, innov2, work)
    shared = lax.all_to_all(sums, "lon", 0, 0, tiled=True)
    height, sums = lax.optimization_barrier((height, sums))
    state, tail, edge = call(
        velocity_kernel,
        (
            shape((DISTINCT, 3 * columns, LANES), f32),
            shape((DISTINCT * (3 * SHIFT + 1), LANES), f32),
            shape((DISTINCT, LANES), f32),
        ),
        [VMEM] * 5,
        (VMEM,) * 3,
    )(gathered2, innov2, step1, work, height)
    tail = lax.ppermute(tail, "lon", eastward)
    coded = call(
        coding_kernel,
        shape((DISTINCT, 4 * columns, LANES), bf16),
        [VMEM] * 4,
        VMEM,
        [pltpu.VMEM((DISTINCT, 3 * columns, LANES), f32)],
    )(state, tail, edge, own)
    coded, shared = lax.optimization_barrier((coded, shared))
    state = call(
        slots_kernel,
        shape((members, 8 * columns + 16, LANES), bf16),
        [VMEM] * 3,
        VMEM,
    )(idx, coded, shared)
    state = swap(state)
    return pl.pallas_call(
        functools.partial(output_kernel, cells=float(lat * columns * lons)),
        grid=(2,),
        out_shape=(shape((2, 3, columns, lat), f32), shape((2,), f32)),
        in_specs=[VMEM, VMEM],
        out_specs=(pl.BlockSpec((1, 3, columns, lat), lambda p: (p, 0, 0, 0)), SMEM),
        compiler_params=pltpu.CompilerParams(vmem_limit_bytes=24 * 1024 * 1024),
    )(idx, state)


def solution(mesh):
    placed = (
        P("member", None, "lon", None),
        P(),
        P("lon", None),
        P("lon", None),
        P("lon", None),
        P(),
        P("member", None),
        P("lon", None),
    )
    return jax.shard_map(
        per_device,
        mesh=mesh,
        in_specs=placed,
        out_specs=(P("member", None, "lon", None), P("member")),
        check_vma=False,
    )
```
